32 devices in a mesh: row: 8 (over z, x), col: 4 (over y, core).
Axes of the slice: x: 2, y: 2, z: 4, core: 2. Of those that a mesh axis runs over, the one named last changes fastest.
Arguments:
- tiles: bfloat16 [5376, 128, 128], P(('row', 'col')), may hold values from -0.0625 to 0.0625
- tile_slots: int32 [5376], P(('row', 'col')), may hold values from 0 to 383, as said below
- sketch: bfloat16 [24576, 512], P('col'), may hold values from -6 to 6
- row_sketch: bfloat16 [8192, 512], P(('row', 'col')), may hold values from -6 to 6
- subsketch: float32 [512, 128], replicated, may hold values from -0.25 to 0.25
- couplings: bfloat16 [32, 5, 128, 128], P(('row', 'col')), may hold values from -0.25 to 0.25, as said below
Outputs:
- leaf_basis: float32 [8192, 128], P(('row', 'col'))
- transfer: float32 [32, 5, 128, 128], P(('row', 'col'))
- top_samples: float32 [32, 128, 512], P(('row', 'col'))
The draws below stay inside these ranges and needn't reach their ends.
Inputs may be any that keep to these rules, and one draw needn't show every extreme that they name: `tile_slots`: the 168 slots of one device are distinct; slot v names row tile v // 48 and column tile v % 48. couplings[i, l] equals couplings[j, l] whenever i // 2 ** (l + 1) equals j // 2 ** (l + 1).
All inputs are finite; a program needn't handle non-finite values.
Results may differ from the reference program's by a relative error of at most 0.0003.
Values may be sent and summed in bfloat16 or wider, within the bound.
No kernel may reach another device: no remote copies, remote signals or barrier semaphores. Data moves between devices by JAX's collectives and lax.ppermute only.
A program may use at most 128 MiB of HBM per device.

```python
import jax
import jax.numpy as jnp
from jax import lax

TILE = 128
LEAF = 256
S = 512
RANK = 128
LEVELS = 5
CTILES = 48
RTILES = 8
TILES = 168
LEAVES = 32
ROWS = 8192
COLS = 24576
N_ROW = 8
N_COL = 4


def draw_tile_slots(key, part):
    device_keys = jax.random.split(key, LEAVES)

    def one_device(device_key):
        return jax.random.permutation(device_key, RTILES * CTILES)[:TILES]
    return jax.vmap(one_device)(device_keys).reshape(LEAVES * TILES).astype(jnp.int32)


def draw_couplings(key, part):
    shape = (LEAVES, LEVELS, RANK, RANK)
    base = jnp.clip(jax.random.normal(key, shape, jnp.float32), -4.0, 4.0) * 0.0625
    leaf_ids = jnp.arange(LEAVES, dtype=jnp.int32)
    layers = []
    for tree_level in range(LEVELS):
        source = (leaf_ids // 2 ** (tree_level + 1) * 2 ** (tree_level + 1)).astype(jnp.int32)
        layers.append(jnp.take(base[:, tree_level], source, axis=0))
    return jnp.stack(layers, axis=1).astype(jnp.bfloat16)


def level_of(rng, dims, shards, least, high):
    level, own = 1.0, jax.random.fold_in(rng, 6)
    for axis_at, parts in shards:
        heights = jnp.exp(jax.random.uniform(jax.random.fold_in(own, axis_at), (parts,), jnp.float32, least / len(shards), high / len(shards)))
        level = level * jnp.repeat(heights, dims[axis_at] // parts).reshape([-1 if axis == axis_at else 1 for axis in range(len(dims))])
    return level


def centred(key, dims, spread, limit, shards=(), kind=jnp.bfloat16):
    drawn = spread * jax.random.normal(key, dims, jnp.float32)
    if shards:
        drawn = drawn * level_of(key, dims, shards, -0.22, 0.18)
    return jnp.clip(drawn, -limit, limit).astype(kind)


def setup_inputs(seed: int = 0) -> dict:
    streams_of = jax.random.split(jax.random.key(seed), 7)
    return {
        "tiles": centred(streams_of[0], (LEAVES * TILES, TILE, TILE), (TILE * TILES * N_COL // RTILES) ** -0.5, 0.0625, ((0, 32),)),
        "tile_slots": draw_tile_slots(jax.random.fold_in(streams_of[6], 71), 0),
        "sketch": centred(streams_of[2], (COLS, S), 1.0, 6.0, ((0, 4),)),
        "row_sketch": centred(streams_of[3], (ROWS, S), 1.0, 6.0, ((0, 32),)),
        "subsketch": centred(streams_of[4], (S, RANK), S ** -0.5, 0.25, (), jnp.float32),
        "couplings": draw_couplings(jax.random.fold_in(streams_of[6], 71), 0),
    }


def orthonormal(columns):
    gram = jnp.einsum('nr,nq->rq', columns, columns, precision=lax.Precision.HIGHEST)
    shift = 0.0001 * jnp.trace(gram) / gram.shape[0] + 1e-06
    lower = jnp.linalg.cholesky(gram + shift * jnp.eye(gram.shape[0], dtype=jnp.float32))
    basis_t = jax.scipy.linalg.solve_triangular(lower, columns.T, lower=True)
    return basis_t

def leaf_step(leaf_sample, leaf_sketch, subsketch):
    reduced = jnp.dot(leaf_sample, subsketch, precision=lax.Precision.HIGHEST)
    basis_t = orthonormal(reduced)
    proj_sample = jnp.dot(basis_t, leaf_sample, precision=lax.Precision.HIGHEST)
    proj_sketch = jnp.dot(basis_t, leaf_sketch.astype(jnp.float32), precision=lax.Precision.HIGHEST)
    return (basis_t.T, proj_sample, proj_sketch)

def merge_pair(low_sample, low_sketch, high_sample, high_sketch, coupling, subsketch):
    coup_f = coupling.astype(jnp.float32)
    low_part = low_sample - jnp.dot(coup_f, high_sketch, precision=lax.Precision.HIGHEST)
    high_part = high_sample - jnp.einsum('ji,js->is', coup_f, low_sketch, precision=lax.Precision.HIGHEST)
    stacked = jnp.concatenate([low_part, high_part], axis=0)
    stacked_sketch = jnp.concatenate([low_sketch, high_sketch], axis=0)
    reduced = jnp.dot(stacked, subsketch, precision=lax.Precision.HIGHEST)
    basis_t = orthonormal(reduced)
    new_sample = jnp.dot(basis_t, stacked, precision=lax.Precision.HIGHEST)
    new_sketch = jnp.dot(basis_t, stacked_sketch, precision=lax.Precision.HIGHEST)
    return (basis_t.T, new_sample, new_sketch)

def reference(tiles, tile_slots, sketch, row_sketch, subsketch, couplings):
    group_rows = RTILES * TILE
    tile_view = tiles.reshape(N_ROW, N_COL, TILES, TILE, TILE)
    slot_view = tile_slots.reshape(N_ROW, N_COL, TILES)
    sketch_view = sketch.reshape(N_COL, CTILES, TILE, S)

    def device_partial(dev_tiles, dev_slots, dev_sketch):
        picked = jnp.take(dev_sketch, dev_slots % CTILES, axis=0).astype(jnp.float32)
        product = jnp.einsum('tij,tjs->tis', dev_tiles.astype(jnp.float32), picked)
        summed = jax.ops.segment_sum(product, dev_slots // CTILES, num_segments=RTILES)
        return summed.reshape(group_rows, S)

    def group_sum(inputs):
        group_tiles, group_slots = inputs
        partials = jax.vmap(device_partial)(group_tiles, group_slots, sketch_view)
        return jnp.sum(partials, axis=0)
    samples = lax.map(group_sum, (tile_view, slot_view)).reshape(LEAVES, LEAF, S)
    leaf_rows = row_sketch.reshape(LEAVES, LEAF, S)
    bases, proj_sample, proj_sketch = jax.vmap(leaf_step, in_axes=(0, 0, None))(samples, leaf_rows, subsketch)
    leaf_basis = bases.reshape(LEAVES * LEAF, RANK)
    leaf_ids = jnp.arange(LEAVES, dtype=jnp.int32)
    blocks = []
    for tree_level in range(LEVELS):
        coupling = couplings[::2 ** (tree_level + 1), tree_level]
        parent_basis, proj_sample, proj_sketch = jax.vmap(merge_pair, in_axes=(0, 0, 0, 0, 0, None))(proj_sample[0::2], proj_sketch[0::2], proj_sample[1::2], proj_sketch[1::2], coupling, subsketch)
        node_count = parent_basis.shape[0]
        halves = parent_basis.reshape(node_count, 2, RANK, RANK)
        parent_ids = (leaf_ids // 2 ** (tree_level + 1)).astype(jnp.int32)
        half_ids = (leaf_ids // 2 ** tree_level % 2).astype(jnp.int32)
        blocks.append(halves[parent_ids, half_ids])
    transfer = jnp.stack(blocks, axis=1)
    top_samples = proj_sample[(leaf_ids // 2 ** LEVELS).astype(jnp.int32)]
    return (leaf_basis, transfer, top_samples)
```

```python
import math

import jax
import jax.numpy as jnp
from jax import lax
from jax.experimental import pallas as pl
from jax.experimental.pallas import tpu as pltpu
from jax.sharding import PartitionSpec as P

LEVELS = 5


def from_partner(block, axis, bit):
    count = lax.axis_size(axis)
    route = []
    for low in range(count):
        high = low | 1 << bit
        if high != low and high < count:
            route += [(low, high), (high, low)]
    return lax.ppermute(block, axis, route)


def orthonormal(columns):
    gram = jnp.einsum("nr,nq->rq", columns, columns, precision=lax.Precision.HIGHEST)
    shift = 0.0001 * jnp.trace(gram) / gram.shape[0] + 1e-06
    lower = jnp.linalg.cholesky(gram + shift * jnp.eye(gram.shape[0], dtype=jnp.float32))
    return jax.scipy.linalg.solve_triangular(lower, columns.T, lower=True)


def leaf_step(leaf_sample, leaf_sketch, subsketch):
    reduced = jnp.dot(leaf_sample, subsketch, precision=lax.Precision.HIGHEST)
    basis_t = orthonormal(reduced)
    proj_sample = jnp.dot(basis_t, leaf_sample, precision=lax.Precision.HIGHEST)
    proj_sketch = jnp.dot(basis_t, leaf_sketch.astype(jnp.float32), precision=lax.Precision.HIGHEST)
    return (basis_t.T, proj_sample, proj_sketch)


def merge_pair(low_sample, low_sketch, high_sample, high_sketch, coupling, subsketch):
    coup_f = coupling.astype(jnp.float32)
    low_part = low_sample - jnp.dot(coup_f, high_sketch, precision=lax.Precision.HIGHEST)
    high_part = high_sample - jnp.einsum(
        "ji,js->is", coup_f, low_sketch, precision=lax.Precision.HIGHEST
    )
    stacked = jnp.concatenate([low_part, high_part], axis=0)
    stacked_sketch = jnp.concatenate([low_sketch, high_sketch], axis=0)
    reduced = jnp.dot(stacked, subsketch, precision=lax.Precision.HIGHEST)
    basis_t = orthonormal(reduced)
    new_sample = jnp.dot(basis_t, stacked, precision=lax.Precision.HIGHEST)
    new_sketch = jnp.dot(basis_t, stacked_sketch, precision=lax.Precision.HIGHEST)
    return (basis_t.T, new_sample, new_sketch)


def spmm_body(slots_ref, tiles_ref, sketch_ref, out_ref, dense, held, tile_sem, sketch_sems):
    tile_count, tile_size, _ = tiles_ref.shape
    depth = sketch_ref.shape[0]
    rows = dense.shape[0]
    col_tiles = depth // tile_size
    chunks = sketch_sems.shape[0]
    chunk = depth // chunks
    loads = [
        pltpu.make_async_copy(
            sketch_ref.at[pl.ds(k * chunk, chunk)], held.at[pl.ds(k * chunk, chunk)], sketch_sems.at[k]
        )
        for k in range(chunks)
    ]

    @pl.loop(0, rows // 64)
    def _(i):
        dense[pl.ds(pl.multiple_of(i * 64, 64), 64), :] = jnp.zeros((64, depth), dense.dtype)

    @pl.loop(0, tile_count)
    def _(t):
        slot = slots_ref[t]
        row = pl.multiple_of(slot // col_tiles * tile_size, tile_size)
        col = pl.multiple_of(slot % col_tiles * tile_size, tile_size)
        pltpu.make_async_copy(
            tiles_ref.at[t], dense.at[pl.ds(row, tile_size), pl.ds(col, tile_size)], tile_sem
        ).start()

    for load in loads:
        load.start()
    pltpu.make_async_copy(tiles_ref, tiles_ref, tile_sem).wait()
    for k in range(chunks):
        loads[k].wait()
        part = jnp.dot(
            dense[:, k * chunk : (k + 1) * chunk],
            held[k * chunk : (k + 1) * chunk, :],
            preferred_element_type=jnp.float32,
        )
        if k == 0:
            out_ref[...] = part
        else:
            out_ref[...] += part


def sample_rows(tiles, tile_slots, sketch, row_tiles):
    tile_count, tile_size, _ = tiles.shape
    depth, width = sketch.shape
    rows = row_tiles * tile_size
    chunks = math.gcd(depth // tile_size, 4)
    return pl.pallas_call(
        spmm_body,
        out_shape=jax.ShapeDtypeStruct((rows, width), jnp.float32),
        in_specs=[
            pl.BlockSpec(memory_space=pltpu.SMEM),
            pl.BlockSpec(memory_space=pl.ANY),
            pl.BlockSpec(memory_space=pl.ANY),
        ],
        out_specs=pl.BlockSpec(memory_space=pltpu.VMEM),
        scratch_shapes=[
            pltpu.VMEM((rows, depth), jnp.bfloat16),
            pltpu.VMEM((depth, width), jnp.bfloat16),
            pltpu.SemaphoreType.DMA,
            pltpu.SemaphoreType.DMA((chunks,)),
        ],
        compiler_params=pltpu.CompilerParams(vmem_limit_bytes=48 * 2**20),
        cost_estimate=pl.CostEstimate(
            flops=2 * rows * depth * width,
            bytes_accessed=2 * (tiles.size + sketch.size) + 4 * rows * width,
            transcendentals=0,
        ),
        name="spmm",
    )(tile_slots, tiles, sketch)


def upper_levels(proj_sample, proj_sketch, couplings, subsketch, first_level, blocks):
    rank_size = proj_sample.shape[0]
    position = lax.axis_index(("row", "col"))
    for tree_level in range(first_level, LEVELS):
        other_sample, other_sketch = from_partner(
            (proj_sample, proj_sketch), ("row", "col"), tree_level
        )
        upper = position // 2**tree_level % 2 == 1
        low_sample = jnp.where(upper, other_sample, proj_sample)
        low_sketch = jnp.where(upper, other_sketch, proj_sketch)
        high_sample = jnp.where(upper, proj_sample, other_sample)
        high_sketch = jnp.where(upper, proj_sketch, other_sketch)
        parent_basis, proj_sample, proj_sketch = merge_pair(
            low_sample, low_sketch, high_sample, high_sketch, couplings[0, tree_level], subsketch
        )
        blocks.append(jnp.where(upper, parent_basis[rank_size:], parent_basis[:rank_size]))
    return proj_sample


def per_device(tiles, tile_slots, sketch, row_sketch, subsketch, couplings):
    col_count = lax.axis_size("col")
    leaf_rows = row_sketch.shape[0]
    row_tiles = leaf_rows * col_count // tiles.shape[1]
    partial_value = sample_rows(tiles, tile_slots, sketch, row_tiles)
    blocks = []
    leaf_sample = lax.psum_scatter(partial_value, "col", scatter_dimension=0, tiled=True)
    leaf_basis, proj_sample, proj_sketch = leaf_step(leaf_sample, row_sketch, subsketch)
    top_sample = upper_levels(proj_sample, proj_sketch, couplings, subsketch, 0, blocks)
    transfer = jnp.stack(blocks, axis=0)[None]
    return (leaf_basis, transfer, top_sample[None])


def solution(mesh):
    return jax.shard_map(
        per_device,
        mesh=mesh,
        in_specs=(
            P(("row", "col"), None, None),
            P(("row", "col")),
            P("col", None),
            P(("row", "col"), None),
            P(),
            P(("row", "col"), None, None, None),
        ),
        out_specs=(
            P(("row", "col"), None),
            P(("row", "col"), None, None, None),
            P(("row", "col"), None, None),
        ),
        check_vma=False,
    )
```

```python
import functools
import math

import jax
import jax.numpy as jnp
from jax import lax
from jax.experimental import pallas as pl
from jax.experimental.pallas import tpu as pltpu
from jax.sharding import PartitionSpec as P

LEVELS = 5
ROW_COL = ("row", "col")
VMEM = pl.BlockSpec(memory_space=pltpu.VMEM)


def from_partner(block, axis, distance):
    count = lax.axis_size(axis)
    route = []
    for low in range(count):
        high = low ^ distance
        if high < count:
            route.append((low, high))
    return lax.ppermute(block, axis, route)


def dot(left, right):
    return jnp.dot(left, right, precision=lax.Precision.HIGHEST, preferred_element_type=jnp.float32)


def dot_nt(left, right):
    return lax.dot_general(
        left,
        right,
        (((1,), (1,)), ((), ())),
        precision=lax.Precision.HIGHEST,
        preferred_element_type=jnp.float32,
    )


def inverse_factor(gram):
    size = gram.shape[0]
    high = 8
    count = size // high
    lane_all = lax.broadcasted_iota(jnp.int32, (size, size), 1)
    diag = lane_all == lax.broadcasted_iota(jnp.int32, (size, size), 0)
    trace = jnp.sum(
        jnp.sum(jnp.where(diag, gram, 0.0), axis=0, keepdims=True), axis=1, keepdims=True
    )
    shift = 0.0001 * trace / size + 1e-06
    gram = jnp.where(diag, gram + shift, gram)
    rows = [gram[high * g : high * g + high, :] for g in range(count)]
    shape = (high, size)
    lane = lax.broadcasted_iota(jnp.int32, shape, 1)
    sub = lax.broadcasted_iota(jnp.int32, shape, 0)

    def along_lanes(block, at):
        return jnp.broadcast_to(block[:, at : at + 1], shape)

    def along_rows(block, at):
        return jnp.broadcast_to(block[at : at + 1, :], shape)

    found = []
    for b in range(count):
        first = b * high
        panel = rows[b]
        columns = [along_lanes(panel, first + k) for k in range(high)]
        inside = (lane >= first) & (lane < first + high)
        panel = jnp.where(inside, jnp.where(lane - first == sub, 1.0, 0.0), panel)
        forward, full = panel, panel
        forward_scale = jnp.zeros(shape, jnp.float32)
        full_scale = jnp.zeros(shape, jnp.float32)
        for i in range(high):
            pivot = along_rows(columns[i], i)
            inverse = 1.0 / pivot
            others = jnp.where(sub == i, 0.0, columns[i])
            below = jnp.where(sub > i, columns[i], 0.0)
            for k in range(i + 1, high):
                columns[k] = columns[k] - others * along_rows(columns[k], i) * inverse
            row = along_rows(forward, i) * inverse
            forward = forward - below * row
            full = full - others * row
            forward_scale = jnp.where(sub == i, lax.rsqrt(pivot), forward_scale)
            full_scale = jnp.where(sub == i, inverse, full_scale)
        found.append(jnp.where(lane < first + high, forward * forward_scale, 0.0))
        if b + 1 == count:
            break
        full = full * full_scale
        full_rows = [along_rows(full, k) for k in range(high)]
        for g in range(b + 1, count):
            terms = [along_lanes(rows[g], first + k) * full_rows[k] for k in range(high)]
            while len(terms) > 1:
                terms = [terms[t] + terms[t + 1] for t in range(0, len(terms), 2)]
            rows[g] = jnp.where(inside, 0.0, rows[g]) - terms[0]
    return jnp.concatenate(found, axis=0)


def spmm_body(
    slots_ref,
    tiles_ref,
    sketch_ref,
    sub_ref,
    leaf_sketch_ref,
    keep_ref,
    send_ref,
    keep_red_ref,
    send_red_ref,
    sketch_red_ref,
    dense,
    held,
    tile_sem,
    sketch_sems,
):
    tile_count, tile_size, _ = tiles_ref.shape
    depth = sketch_ref.shape[0]
    rows = dense.shape[0]
    half = rows // 2
    col_tiles = depth // tile_size
    chunks = sketch_sems.shape[0]
    chunk = depth // chunks
    leaf_tiles = leaf_sketch_ref.shape[0] // tile_size
    leaves = rows // leaf_sketch_ref.shape[0]
    me = lax.axis_index("col")
    loads = [
        pltpu.make_async_copy(
            sketch_ref.at[pl.ds(k * chunk, chunk)], held.at[pl.ds(k * chunk, chunk)], sketch_sems.at[k]
        )
        for k in range(chunks)
    ]

    @pl.loop(0, rows // 64)
    def _(i):
        dense[pl.ds(pl.multiple_of(i * 64, 64), 64), :] = jnp.zeros((64, depth), dense.dtype)

    @pl.loop(0, tile_count)
    def _(t):
        slot = slots_ref[t]
        row_tile = slot // col_tiles
        away = (row_tile // leaf_tiles) ^ me
        block = away % 2 * (leaves // 2) + away // 2
        row = pl.multiple_of((block * leaf_tiles + row_tile % leaf_tiles) * tile_size, tile_size)
        col = pl.multiple_of(slot % col_tiles * tile_size, tile_size)
        pltpu.make_async_copy(
            tiles_ref.at[t], dense.at[pl.ds(row, tile_size), pl.ds(col, tile_size)], tile_sem
        ).start()

    for load in loads:
        load.start()
    subsketch = sub_ref[...]
    sketch_red_ref[...] = dot(leaf_sketch_ref[...].astype(jnp.float32), subsketch)
    pltpu.make_async_copy(tiles_ref, tiles_ref, tile_sem).wait()
    for k in range(chunks):
        loads[k].wait()
        for start, ref in ((half, send_ref), (0, keep_ref)):
            part = jnp.dot(
                dense[start : start + half, k * chunk : (k + 1) * chunk],
                held[k * chunk : (k + 1) * chunk, :],
                preferred_element_type=jnp.float32,
            )
            if k == 0:
                ref[...] = part
            else:
                ref[...] += part
    send_red_ref[...] = dot(send_ref[...], subsketch)
    keep_red_ref[...] = dot(keep_ref[...], subsketch)


def sample_rows(tiles, tile_slots, sketch, subsketch, row_sketch):
    tile_size = tiles.shape[1]
    depth, width = sketch.shape
    rank = subsketch.shape[1]
    leaf = row_sketch.shape[0]
    rows = leaf * lax.axis_size("col")
    half = rows // 2
    chunks = math.gcd(depth // tile_size, 4)
    f32 = jnp.float32
    return pl.pallas_call(
        spmm_body,
        out_shape=[
            jax.ShapeDtypeStruct((half, width), f32),
            jax.ShapeDtypeStruct((half, width), f32),
            jax.ShapeDtypeStruct((half, rank), f32),
            jax.ShapeDtypeStruct((half, rank), f32),
            jax.ShapeDtypeStruct((leaf, rank), f32),
        ],
        in_specs=[
            pl.BlockSpec(memory_space=pltpu.SMEM),
            pl.BlockSpec(memory_space=pl.ANY),
            pl.BlockSpec(memory_space=pl.ANY),
            VMEM,
            VMEM,
        ],
        out_specs=[VMEM] * 5,
        scratch_shapes=[
            pltpu.VMEM((rows, depth), jnp.bfloat16),
            pltpu.VMEM((depth, width), jnp.bfloat16),
            pltpu.SemaphoreType.DMA,
            pltpu.SemaphoreType.DMA((chunks,)),
        ],
        compiler_params=pltpu.CompilerParams(vmem_limit_bytes=48 * 2**20),
        cost_estimate=pl.CostEstimate(
            flops=2 * rows * depth * width,
            bytes_accessed=2 * (tiles.size + sketch.size) + 4 * rows * width,
            transcendentals=0,
        ),
        name="spmm",
    )(tile_slots, tiles, sketch, subsketch, row_sketch)


def leaf_body(keep_ref, first_ref, second_ref, sketch_red_ref, basis_ref, basis_t_ref, pair_ref):
    rank = keep_ref.shape[-1]
    reduced = keep_ref[...] + first_ref[...] + second_ref[...]
    reduced_t = reduced.T
    both = dot(reduced_t, jnp.concatenate([reduced, sketch_red_ref[...]], axis=1))
    inverse = inverse_factor(both[:, :rank])
    moved = dot(inverse, both)
    pair_ref[:rank, :] = moved[:, :rank]
    pair_ref[rank:, :] = moved[:, rank:]
    basis_ref[...] = dot_nt(reduced, inverse)
    basis_t_ref[...] = dot(inverse, reduced_t)


def small_params():
    return pltpu.CompilerParams(vmem_limit_bytes=32 * 2**20)


def small_cost(micros):
    return pl.CostEstimate(flops=micros * 10**9, bytes_accessed=micros * 3 * 10**6, transcendentals=0)


def leaf_step(keep, first, second, sketch_red):
    leaf, rank = sketch_red.shape
    f32 = jnp.float32
    part = pl.BlockSpec((leaf, rank), lambda step: (0, 0))
    return pl.pallas_call(
        leaf_body,
        grid=(1,),
        out_shape=[
            jax.ShapeDtypeStruct((leaf, rank), f32),
            jax.ShapeDtypeStruct((rank, leaf), f32),
            jax.ShapeDtypeStruct((2 * rank, rank), f32),
        ],
        in_specs=[part, part, VMEM, VMEM],
        out_specs=[VMEM] * 3,
        compiler_params=small_params(),
        cost_estimate=small_cost(8),
        name="leaf_orth",
    )(keep, first, second, sketch_red)


def turned(coupling_ref, tree_level):
    position = lax.axis_index("row") * lax.axis_size("col") + lax.axis_index("col")
    upper = position // 2**tree_level % 2 == 1
    coupling = coupling_ref[0, 0].astype(jnp.float32)
    coupling_t = coupling.T
    return jnp.where(upper, coupling_t, coupling), jnp.where(upper, coupling, coupling_t)


def merge_body(tree_level, own_ref, other_ref, coupling_ref, block_ref, maps_ref, pair_ref):
    rank = own_ref.shape[-1]
    ahead, back = turned(coupling_ref, tree_level)
    own_sample, own_sketch = own_ref[:rank], own_ref[rank:]
    other_sample, other_sketch = other_ref[:rank], other_ref[rank:]
    own = own_sample - dot(ahead, other_sketch)
    other = other_sample - dot(back, own_sketch)
    own_t, other_t = own.T, other.T
    stacked_t = jnp.concatenate([own_t, other_t], axis=1)
    right = jnp.concatenate(
        [
            jnp.concatenate([own, own_sketch], axis=1),
            jnp.concatenate([other, other_sketch], axis=1),
        ],
        axis=0,
    )
    both = dot(stacked_t, right)
    inverse = inverse_factor(both[:, :rank])
    moved = dot(inverse, both)
    pair_ref[:rank, :] = moved[:, :rank]
    pair_ref[rank:, :] = moved[:, rank:]
    block_ref[...] = dot_nt(own, inverse)
    maps_ref[0] = dot(inverse, own_t)
    maps_ref[1] = dot(inverse, dot(other_t, back))


def coupling_spec(couplings, tree_level):
    return pl.BlockSpec((1, 1) + couplings.shape[2:], lambda step: (0, tree_level, 0, 0))


def merge_step(tree_level, own, other, couplings):
    rank = own.shape[1]
    f32 = jnp.float32
    return pl.pallas_call(
        functools.partial(merge_body, tree_level),
        grid=(1,),
        out_shape=[
            jax.ShapeDtypeStruct((rank, rank), f32),
            jax.ShapeDtypeStruct((2, rank, rank), f32),
            jax.ShapeDtypeStruct((2 * rank, rank), f32),
        ],
        in_specs=[VMEM, VMEM, coupling_spec(couplings, tree_level)],
        out_specs=[VMEM] * 3,
        compiler_params=small_params(),
        cost_estimate=small_cost(8),
        name=f"merge_orth_{tree_level}",
    )(own, other, couplings)


def lower_body(*refs):
    keep_ref, first_ref, second_ref, leaf_sketch_ref, basis_t_ref = refs[:5]
    ways = (refs[-1].shape[1]) // refs[-2].shape[1]
    maps_refs = refs[5 : -1 - ways]
    out_refs = refs[-1 - ways : -1]
    wide = refs[-1]
    rank = basis_t_ref.shape[0]
    sample = keep_ref[...] + first_ref[...] + second_ref[...]
    sketch = leaf_sketch_ref[...].astype(jnp.float32)
    on_sample = basis_t_ref[...]
    on_sketch = jnp.zeros_like(on_sample)
    for maps_ref in maps_refs:
        lifted, crossed = maps_ref[0], maps_ref[1]
        on_sketch = dot(lifted, on_sketch) - dot(crossed, on_sample)
        on_sample = dot(lifted, on_sample)
    wide[:rank, :] = dot(on_sample, sample) + dot(on_sketch, sketch)
    wide[rank:, :] = dot(on_sample, sketch)
    me = lax.axis_index("col")
    part = wide.shape[1] // ways
    for away in range(ways):
        out_refs[away][...] = wide[:, pl.ds(pl.multiple_of((me ^ away) * part, part), part)]


def lower_step(keep, first, second, row_sketch, basis_t, maps):
    ways = lax.axis_size("col")
    leaf, width = row_sketch.shape
    rank = basis_t.shape[0]
    part = pl.BlockSpec((leaf, width), lambda step: (0, 0))
    return pl.pallas_call(
        lower_body,
        grid=(1,),
        out_shape=[jax.ShapeDtypeStruct((2 * rank, width // ways), jnp.float32)] * ways,
        in_specs=[part, part] + [VMEM] * (3 + len(maps)),
        out_specs=[VMEM] * ways,
        scratch_shapes=[pltpu.VMEM((2 * rank, width), jnp.float32)],
        compiler_params=small_params(),
        cost_estimate=small_cost(2),
        name="lower_maps",
    )(keep, first, second, row_sketch, basis_t, *maps)


def upper_body(last, *refs):
    maps_ref, out_ref = refs[-2:]
    total = refs[0][...]
    for ref in refs[1:-2]:
        total = total + ref[...]
    rank = maps_ref.shape[1]
    sample, sketch = total[:rank], total[rank:]
    lifted = maps_ref[0]
    out_ref[:rank, :] = dot(lifted, sample) - dot(maps_ref[1], sketch)
    if not last:
        out_ref[rank:, :] = dot(lifted, sketch)


def upper_step(tree_level, parts, maps):
    last = tree_level == LEVELS - 1
    rows, width = parts[0].shape
    return pl.pallas_call(
        functools.partial(upper_body, last),
        out_shape=jax.ShapeDtypeStruct((rows // 2 if last else rows, width), jnp.float32),
        in_specs=[VMEM] * (len(parts) + 1),
        out_specs=VMEM,
        compiler_params=small_params(),
        cost_estimate=small_cost(1),
        name=f"upper_maps_{tree_level}",
    )(*parts, maps)


def top_body(ways, *refs):
    out_ref = refs[-1]
    me = lax.axis_index("col")
    part = out_ref.shape[2] // ways
    for away in range(ways):
        out_ref[0, :, pl.ds(pl.multiple_of((me ^ away) * part, part), part)] = refs[away][...]


def per_device(tiles, tile_slots, sketch, row_sketch, subsketch, couplings):
    ways = lax.axis_size("col")
    col_bits = ways.bit_length() - 1
    leaf = row_sketch.shape[0]
    keep, send, keep_red, send_red, sketch_red = sample_rows(
        tiles, tile_slots, sketch, subsketch, row_sketch
    )

    def gathered(kept, sent):
        first = from_partner(sent, "col", 1)
        second = from_partner(kept[leaf:] + first[leaf:], "col", 2)
        return kept, first, second

    reduced = gathered(keep_red, send_red)
    samples = gathered(keep, send)
    leaf_basis, basis_t, pair = leaf_step(*reduced, sketch_red)
    blocks, low_maps, parts = [], [], []
    for tree_level in range(LEVELS):
        other = from_partner(pair, ROW_COL, 2**tree_level)
        block, maps, pair = merge_step(tree_level, pair, other, couplings)
        blocks.append(block)
        if tree_level < col_bits:
            low_maps.append(maps)
        else:
            mine = upper_step(tree_level, parts, maps)
            parts = [mine, from_partner(mine, ROW_COL, 2**tree_level)]
        if tree_level == col_bits - 1:
            cut = lower_step(*samples, row_sketch, basis_t, low_maps)
            parts = [cut[0]] + [from_partner(cut[away], "col", away) for away in range(1, ways)]
    top = [parts[0] + parts[1]]
    for bit in reversed(range(col_bits)):
        top += [from_partner(piece, "col", 2**bit) for piece in top]
    order = [0]
    for bit in reversed(range(col_bits)):
        order += [away ^ 2**bit for away in order]
    pieces = [top[order.index(away)] for away in range(ways)]
    rank, part = pieces[0].shape
    top_sample = pl.pallas_call(
        functools.partial(top_body, ways),
        out_shape=jax.ShapeDtypeStruct((1, rank, part * ways), jnp.float32),
        in_specs=[VMEM] * ways,
        out_specs=VMEM,
        name="top_columns",
    )(*pieces)
    transfer = jnp.stack(blocks, axis=0)[None]
    return (leaf_basis, transfer, top_sample)


def solution(mesh):
    return jax.shard_map(
        per_device,
        mesh=mesh,
        in_specs=(
            P(("row", "col"), None, None),
            P(("row", "col")),
            P("col", None),
            P(("row", "col"), None),
            P(),
            P(("row", "col"), None, None, None),
        ),
        out_specs=(
            P(("row", "col"), None),
            P(("row", "col"), None, None, None),
            P(("row", "col"), None, None),
        ),
        check_vma=False,
    )
```

```python
import functools
import math

import jax
import jax.numpy as jnp
from jax import lax
from jax.experimental import pallas as pl
from jax.experimental.pallas import tpu as pltpu
from jax.sharding import PartitionSpec as P

LEVELS = 5
ROW_COL = ("row", "col")
VMEM = pl.BlockSpec(memory_space=pltpu.VMEM)
ANY = pl.BlockSpec(memory_space=pl.ANY)
HBM = pl.BlockSpec(memory_space=pltpu.HBM)


def from_partner(block, axis, distance):
    count = lax.axis_size(axis)
    route = []
    for low in range(count):
        high = low ^ distance
        if high < count:
            route.append((low, high))
    return lax.ppermute(block, axis, route)


def dot(left, right):
    return jnp.dot(left, right, precision=lax.Precision.HIGHEST, preferred_element_type=jnp.float32)


def dot_nt(left, right):
    return lax.dot_general(
        left,
        right,
        (((1,), (1,)), ((), ())),
        precision=lax.Precision.HIGHEST,
        preferred_element_type=jnp.float32,
    )


def inverse_factor(gram):
    size = gram.shape[0]
    high = 8
    count = size // high
    lane_all = lax.broadcasted_iota(jnp.int32, (size, size), 1)
    diag = lane_all == lax.broadcasted_iota(jnp.int32, (size, size), 0)
    trace = jnp.sum(
        jnp.sum(jnp.where(diag, gram, 0.0), axis=0, keepdims=True), axis=1, keepdims=True
    )
    shift = 0.0001 * trace / size + 1e-06
    gram = jnp.where(diag, gram + shift, gram)
    rows = [gram[high * g : high * g + high, :] for g in range(count)]
    shape = (high, size)
    lane = lax.broadcasted_iota(jnp.int32, shape, 1)
    sub = lax.broadcasted_iota(jnp.int32, shape, 0)

    def along_lanes(block, at):
        return jnp.broadcast_to(block[:, at : at + 1], shape)

    def along_rows(block, at):
        return jnp.broadcast_to(block[at : at + 1, :], shape)

    found = []
    for b in range(count):
        first = b * high
        panel = rows[b]
        columns = [along_lanes(panel, first + k) for k in range(high)]
        inside = (lane >= first) & (lane < first + high)
        panel = jnp.where(inside, jnp.where(lane - first == sub, 1.0, 0.0), panel)
        forward, full = panel, panel
        forward_scale = jnp.zeros(shape, jnp.float32)
        full_scale = jnp.zeros(shape, jnp.float32)
        for i in range(high):
            pivot = along_rows(columns[i], i)
            inverse = 1.0 / pivot
            others = jnp.where(sub == i, 0.0, columns[i])
            below = jnp.where(sub > i, columns[i], 0.0)
            for k in range(i + 1, high):
                columns[k] = columns[k] - others * along_rows(columns[k], i) * inverse
            row = along_rows(forward, i) * inverse
            forward = forward - below * row
            full = full - others * row
            forward_scale = jnp.where(sub == i, lax.rsqrt(pivot), forward_scale)
            full_scale = jnp.where(sub == i, inverse, full_scale)
        found.append(jnp.where(lane < first + high, forward * forward_scale, 0.0))
        if b + 1 == count:
            break
        full = full * full_scale
        full_rows = [along_rows(full, k) for k in range(high)]
        for g in range(b + 1, count):
            terms = [along_lanes(rows[g], first + k) * full_rows[k] for k in range(high)]
            while len(terms) > 1:
                terms = [terms[t] + terms[t + 1] for t in range(0, len(terms), 2)]
            rows[g] = jnp.where(inside, 0.0, rows[g]) - terms[0]
    return jnp.concatenate(found, axis=0)


def in_parts(block):
    high = block.astype(jnp.bfloat16)
    rest = block - high.astype(jnp.float32)
    middle = rest.astype(jnp.bfloat16)
    return high, middle, (rest - middle.astype(jnp.float32)).astype(jnp.bfloat16)


def short_dot(left, right):
    return jnp.dot(left, right, preferred_element_type=jnp.float32)


def quotient(value, divisor, below):
    shift = 20
    factor = -(-(2**shift) // divisor)
    assert all(v * factor >> shift == v // divisor for v in range(below))
    assert below * factor < 2**31
    return value * factor >> shift


def spmm_body(
    slots_ref,
    tiles_ref,
    sketch_ref,
    sub_ref,
    leaf_sketch_ref,
    keep_ref,
    send_ref,
    keep_red_ref,
    send_red_ref,
    sketch_red_ref,
    dense,
    held,
    slots,
    sub,
    leaf_sketch,
    tile_sem,
    sketch_sems,
    small_sems,
):
    tile_count, tile_size, _ = tiles_ref.shape
    depth = sketch_ref.shape[0]
    rows = dense.shape[0]
    half = rows // 2
    rank = sub.shape[1]
    col_tiles = depth // tile_size
    chunks = sketch_sems.shape[0]
    chunk = depth // chunks
    leaf_tiles = leaf_sketch_ref.shape[0] // tile_size
    leaves = rows // leaf_sketch_ref.shape[0]
    me = lax.axis_index("col")
    small = [
        pltpu.make_async_copy(source, target, small_sems.at[k])
        for k, (source, target) in enumerate(
            ((slots_ref, slots), (sub_ref, sub), (leaf_sketch_ref, leaf_sketch))
        )
    ]
    loads = [
        pltpu.make_async_copy(
            sketch_ref.at[pl.ds(k * chunk, chunk)], held.at[pl.ds(k * chunk, chunk)], sketch_sems.at[k]
        )
        for k in range(chunks)
    ]
    for load in small + loads:
        load.start()

    @pl.loop(0, rows // 64)
    def _(i):
        dense[pl.ds(pl.multiple_of(i * 64, 64), 64), :] = jnp.zeros((64, depth), dense.dtype)

    small[0].wait()
    together = math.gcd(tile_count, 8)

    @pl.loop(0, tile_count // together)
    def _(group):
        for member in range(together):
            t = group * together + member
            slot = slots[t]
            row_tile = quotient(slot, col_tiles, rows // tile_size * col_tiles)
            column = slot - row_tile * col_tiles
            leaf = quotient(row_tile, leaf_tiles, rows // tile_size)
            away = leaf ^ me
            block = (away & 1) * (leaves // 2) + (away >> 1)
            row = pl.multiple_of((block * leaf_tiles + row_tile - leaf * leaf_tiles) * tile_size, tile_size)
            col = pl.multiple_of(column * tile_size, tile_size)
            pltpu.make_async_copy(
                tiles_ref.at[t], dense.at[pl.ds(row, tile_size), pl.ds(col, tile_size)], tile_sem
            ).start()

    small[1].wait()
    small[2].wait()
    high, middle, low = in_parts(sub[...])
    two = jnp.concatenate([high, middle], axis=1)
    sketch_two = short_dot(leaf_sketch[...], two)
    sketch_red_ref[...] = sketch_two[:, :rank] + (
        sketch_two[:, rank:] + short_dot(leaf_sketch[...], low)
    )
    pltpu.make_async_copy(tiles_ref, tiles_ref, tile_sem).wait()
    for k in range(chunks):
        loads[k].wait()
        for start, ref in ((half, send_ref), (0, keep_ref)):
            part = jnp.dot(
                dense[start : start + half, k * chunk : (k + 1) * chunk],
                held[k * chunk : (k + 1) * chunk, :],
                preferred_element_type=jnp.float32,
            )
            if k == 0:
                ref[...] = part
            else:
                ref[...] += part
    for ref, red_ref in ((send_ref, send_red_ref), (keep_ref, keep_red_ref)):
        first, second, third = in_parts(ref[...])
        wide = short_dot(second, two) + short_dot(first, two)
        rest = short_dot(third, high) + short_dot(first, low)
        red_ref[...] = wide[:, :rank] + (wide[:, rank:] + rest)


def sample_rows(tiles, tile_slots, sketch, subsketch, row_sketch):
    tile_size = tiles.shape[1]
    depth, width = sketch.shape
    rank = subsketch.shape[1]
    leaf = row_sketch.shape[0]
    rows = leaf * lax.axis_size("col")
    half = rows // 2
    chunks = math.gcd(depth // tile_size, 4)
    f32 = jnp.float32
    return pl.pallas_call(
        spmm_body,
        out_shape=[
            jax.ShapeDtypeStruct((half, width), f32),
            jax.ShapeDtypeStruct((half, width), f32),
            jax.ShapeDtypeStruct((half, rank), f32),
            jax.ShapeDtypeStruct((half, rank), f32),
            jax.ShapeDtypeStruct((leaf, rank), f32),
        ],
        in_specs=[HBM] * 5,
        out_specs=[VMEM] * 5,
        scratch_shapes=[
            pltpu.VMEM((rows, depth), jnp.bfloat16),
            pltpu.VMEM((depth, width), jnp.bfloat16),
            pltpu.SMEM(tile_slots.shape, jnp.int32),
            pltpu.VMEM(subsketch.shape, f32),
            pltpu.VMEM(row_sketch.shape, jnp.bfloat16),
            pltpu.SemaphoreType.DMA,
            pltpu.SemaphoreType.DMA((chunks,)),
            pltpu.SemaphoreType.DMA((3,)),
        ],
        compiler_params=pltpu.CompilerParams(vmem_limit_bytes=48 * 2**20),
        cost_estimate=pl.CostEstimate(
            flops=2 * rows * depth * width,
            bytes_accessed=2 * (tiles.size + sketch.size) + 4 * rows * width,
            transcendentals=0,
        ),
        name="spmm",
    )(tile_slots, tiles, sketch, subsketch, row_sketch)


def leaf_body(keep_ref, first_ref, second_ref, sketch_red_ref, _, basis_ref, basis_t_ref, pair_ref):
    rank = keep_ref.shape[-1]
    reduced = keep_ref[...] + first_ref[...] + second_ref[...]
    reduced_t = reduced.T
    both = dot(reduced_t, jnp.concatenate([reduced, sketch_red_ref[...]], axis=1))
    inverse = inverse_factor(both[:, :rank])
    moved = dot(inverse, both)
    pair_ref[:rank, :] = moved[:, :rank]
    pair_ref[rank:, :] = moved[:, rank:]
    basis_ref[...] = dot_nt(reduced, inverse)
    basis_t_ref[...] = dot(inverse, reduced_t)


def small_params():
    return pltpu.CompilerParams(vmem_limit_bytes=32 * 2**20)


def small_cost(micros):
    return pl.CostEstimate(flops=micros * 10**9, bytes_accessed=micros * 3 * 10**6, transcendentals=0)


def leaf_step(keep, first, second, sketch_red, after):
    leaf, rank = sketch_red.shape
    f32 = jnp.float32
    part = pl.BlockSpec((leaf, rank), lambda step: (0, 0))
    return pl.pallas_call(
        leaf_body,
        grid=(1,),
        out_shape=[
            jax.ShapeDtypeStruct((leaf, rank), f32),
            jax.ShapeDtypeStruct((rank, leaf), f32),
            jax.ShapeDtypeStruct((2 * rank, rank), f32),
        ],
        in_specs=[part, part, VMEM, VMEM, ANY],
        out_specs=[VMEM] * 3,
        compiler_params=small_params(),
        cost_estimate=small_cost(8),
        name="leaf_orth",
    )(keep, first, second, sketch_red, after)


def turned(coupling_ref, tree_level):
    position = lax.axis_index("row") * lax.axis_size("col") + lax.axis_index("col")
    upper = position // 2**tree_level % 2 == 1
    coupling = coupling_ref[0, 0].astype(jnp.float32)
    coupling_t = coupling.T
    return jnp.where(upper, coupling_t, coupling), jnp.where(upper, coupling, coupling_t)


def merge_body(tree_level, *refs):
    own_ref, other_ref, coupling_ref = refs[:3]
    block_ref, maps_ref, pair_ref = refs[-3:]
    last = tree_level == LEVELS - 1
    rank = own_ref.shape[-1]
    ahead, back = turned(coupling_ref, tree_level)
    own_sample, own_sketch = own_ref[:rank], own_ref[rank:]
    other_sample, other_sketch = other_ref[:rank], other_ref[rank:]
    own = own_sample - dot(ahead, other_sketch)
    other = other_sample - dot(back, own_sketch)
    own_t, other_t = own.T, other.T
    stacked_t = jnp.concatenate([own_t, other_t], axis=1)
    right = jnp.concatenate(
        [
            jnp.concatenate([own, own_sketch], axis=1),
            jnp.concatenate([other, other_sketch], axis=1),
        ],
        axis=0,
    )
    both = dot(stacked_t, right)
    inverse = inverse_factor(both[:, :rank])
    block_ref[...] = dot_nt(own, inverse)
    if last:
        pair_ref[...] = dot(inverse, stacked_t)
        return
    moved = dot(inverse, both)
    pair_ref[:rank, :] = moved[:, :rank]
    pair_ref[rank:, :] = moved[:, rank:]
    maps_ref[0] = dot(inverse, own_t)
    maps_ref[1] = dot(inverse, dot(other_t, back))


def coupling_spec(couplings, tree_level):
    return pl.BlockSpec((1, 1) + couplings.shape[2:], lambda step: (0, tree_level, 0, 0))


def merge_step(tree_level, own, other, couplings, after):
    rank = own.shape[1]
    f32 = jnp.float32
    last = tree_level == LEVELS - 1
    return pl.pallas_call(
        functools.partial(merge_body, tree_level),
        grid=(1,),
        out_shape=[
            jax.ShapeDtypeStruct((rank, rank), f32),
            jax.ShapeDtypeStruct((8, rank) if last else (2, rank, rank), f32),
            jax.ShapeDtypeStruct((rank, 2 * rank) if last else (2 * rank, rank), f32),
        ],
        in_specs=[VMEM, VMEM, coupling_spec(couplings, tree_level)] + [ANY] * len(after),
        out_specs=[VMEM, ANY if last else VMEM, VMEM],
        compiler_params=small_params(),
        cost_estimate=small_cost(8),
        name=f"merge_orth_{tree_level}",
    )(own, other, couplings, *after)


def lower_body(*refs):
    keep_ref, first_ref, second_ref, leaf_sketch_ref, basis_t_ref = refs[:5]
    ways = (refs[-1].shape[1]) // refs[-2].shape[1]
    maps_refs = refs[5 : -1 - ways]
    out_refs = refs[-1 - ways : -1]
    wide = refs[-1]
    rank = basis_t_ref.shape[0]
    sample = keep_ref[...] + first_ref[...] + second_ref[...]
    sketch = leaf_sketch_ref[...].astype(jnp.float32)
    on_sample = basis_t_ref[...]
    on_sketch = jnp.zeros_like(on_sample)
    for maps_ref in maps_refs:
        lifted, crossed = maps_ref[0], maps_ref[1]
        on_sketch = dot(lifted, on_sketch) - dot(crossed, on_sample)
        on_sample = dot(lifted, on_sample)
    wide[:rank, :] = dot(on_sample, sample) + dot(on_sketch, sketch)
    wide[rank:, :] = dot(on_sample, sketch)
    me = lax.axis_index("col")
    part = wide.shape[1] // ways
    for away in range(ways):
        out_refs[away][...] = wide[:, pl.ds(pl.multiple_of((me ^ away) * part, part), part)]


def lower_step(keep, first, second, row_sketch, basis_t, maps):
    ways = lax.axis_size("col")
    leaf, width = row_sketch.shape
    rank = basis_t.shape[0]
    part = pl.BlockSpec((leaf, width), lambda step: (0, 0))
    return pl.pallas_call(
        lower_body,
        grid=(1,),
        out_shape=[jax.ShapeDtypeStruct((2 * rank, width // ways), jnp.float32)] * ways,
        in_specs=[part, part] + [VMEM] * (3 + len(maps)),
        out_specs=[VMEM] * ways,
        scratch_shapes=[pltpu.VMEM((2 * rank, width), jnp.float32)],
        compiler_params=small_params(),
        cost_estimate=small_cost(2),
        name="lower_maps",
    )(keep, first, second, row_sketch, basis_t, *maps)


def upper_body(*refs):
    maps_ref, out_ref = refs[-2:]
    total = refs[0][...]
    for ref in refs[1:-2]:
        total = total + ref[...]
    rank = maps_ref.shape[1]
    sample, sketch = total[:rank], total[rank:]
    lifted = maps_ref[0]
    out_ref[:rank, :] = dot(lifted, sample) - dot(maps_ref[1], sketch)
    out_ref[rank:, :] = dot(lifted, sketch)


def upper_step(tree_level, parts, maps):
    return pl.pallas_call(
        upper_body,
        out_shape=jax.ShapeDtypeStruct(parts[0].shape, jnp.float32),
        in_specs=[VMEM] * (len(parts) + 1),
        out_specs=VMEM,
        compiler_params=small_params(),
        cost_estimate=small_cost(1),
        name=f"upper_maps_{tree_level}",
    )(*parts, maps)


def top_body(own_ref, other_ref, coupling_ref, basis_t_ref, out_ref):
    rank = own_ref.shape[0] // 2
    ahead, back = turned(coupling_ref, LEVELS - 1)
    own = own_ref[:rank] - dot(ahead, other_ref[rank:])
    other = other_ref[:rank] - dot(back, own_ref[rank:])
    out_ref[...] = dot(basis_t_ref[...], jnp.concatenate([own, other], axis=0))


def top_step(own, other, couplings, basis_t):
    return pl.pallas_call(
        top_body,
        grid=(1,),
        out_shape=jax.ShapeDtypeStruct((own.shape[0] // 2, own.shape[1]), jnp.float32),
        in_specs=[VMEM, VMEM, coupling_spec(couplings, LEVELS - 1), VMEM],
        out_specs=VMEM,
        compiler_params=small_params(),
        cost_estimate=small_cost(1),
        name="top_sample",
    )(own, other, couplings, basis_t)


def columns_body(*refs):
    sems = refs[-1]
    out_ref = refs[-2]
    pieces = refs[:-2]
    ways = len(pieces)
    me = lax.axis_index("col")
    part = out_ref.shape[2] // ways
    copies = [
        pltpu.make_async_copy(
            pieces[away],
            out_ref.at[0, :, pl.ds(pl.multiple_of((me ^ away) * part, part), part)],
            sems.at[away],
        )
        for away in range(ways)
    ]
    for copy in copies:
        copy.start()
    for copy in copies:
        copy.wait()


def columns_step(pieces):
    rank, part = pieces[0].shape
    ways = len(pieces)
    return pl.pallas_call(
        columns_body,
        out_shape=jax.ShapeDtypeStruct((1, rank, part * ways), jnp.float32),
        in_specs=[VMEM] * ways,
        out_specs=ANY,
        scratch_shapes=[pltpu.SemaphoreType.DMA((ways,))],
        name="top_columns",
    )(*pieces)


def per_device(tiles, tile_slots, sketch, row_sketch, subsketch, couplings):
    ways = lax.axis_size("col")
    col_bits = ways.bit_length() - 1
    leaf = row_sketch.shape[0]
    keep, send, keep_red, send_red, sketch_red = sample_rows(
        tiles, tile_slots, sketch, subsketch, row_sketch
    )
    first_red = from_partner(send_red, "col", 1)
    first = from_partner(send, "col", 1)
    second_red = from_partner(keep_red[leaf:] + first_red[leaf:], "col", 2)
    passed = keep[leaf:] + first[leaf:]
    second = from_partner(passed, "col", 2)
    leaf_basis, basis_t, pair = leaf_step(keep_red, first_red, second_red, sketch_red, passed)
    blocks, low_maps, after, parts = [], [], [], []
    for tree_level in range(LEVELS):
        other = from_partner(pair, ROW_COL, 2**tree_level)
        if tree_level == col_bits - 1:
            after = [second]
        block, maps, pair = merge_step(tree_level, pair, other, couplings, after)
        blocks.append(block)
        if tree_level == LEVELS - 1:
            break
        if tree_level < col_bits:
            low_maps.append(maps)
        else:
            mine = upper_step(tree_level, parts, maps)
            parts = [mine, from_partner(mine, ROW_COL, 2**tree_level)]
            after = [mine]
        if tree_level == col_bits - 1:
            cut = lower_step(keep, first, second, row_sketch, basis_t, low_maps)
            parts = [cut[0]] + [from_partner(cut[away], "col", away) for away in range(1, ways)]
            after = [cut[0]]
        if tree_level == LEVELS - 2:
            whole = parts[0] + parts[1]
            far = from_partner(whole, ROW_COL, 2 ** (LEVELS - 1))
            after = [whole]
    top = top_step(whole, far, couplings, pair)
    pieces = [top] + [from_partner(top, "col", away) for away in range(1, ways)]
    transfer = jnp.stack(blocks, axis=0)[None]
    return (leaf_basis, transfer, columns_step(pieces))


def solution(mesh):
    return jax.shard_map(
        per_device,
        mesh=mesh,
        in_specs=(
            P(("row", "col"), None, None),
            P(("row", "col")),
            P("col", None),
            P(("row", "col"), None),
            P(),
            P(("row", "col"), None, None, None),
        ),
        out_specs=(
            P(("row", "col"), None),
            P(("row", "col"), None, None, None),
            P(("row", "col"), None, None),
        ),
        check_vma=False,
    )
```

```python
import functools
import math

import jax
import jax.numpy as jnp
from jax import lax
from jax.experimental import pallas as pl
from jax.experimental.pallas import tpu as pltpu
from jax.sharding import PartitionSpec as P

LEVELS = 5
ROW_COL = ("row", "col")
VMEM = pl.BlockSpec(memory_space=pltpu.VMEM)
ANY = pl.BlockSpec(memory_space=pl.ANY)
HBM = pl.BlockSpec(memory_space=pltpu.HBM)


def from_partner(block, axis, distance):
    count = lax.axis_size(axis)
    route = []
    for low in range(count):
        high = low ^ distance
        if high < count:
            route.append((low, high))
    return lax.ppermute(block, axis, route)


def dot(left, right):
    return jnp.dot(left, right, precision=lax.Precision.HIGHEST, preferred_element_type=jnp.float32)


def dot_nt(left, right):
    return lax.dot_general(
        left,
        right,
        (((1,), (1,)), ((), ())),
        precision=lax.Precision.HIGHEST,
        preferred_element_type=jnp.float32,
    )


def inverse_factor(gram):
    size = gram.shape[0]
    high = 8
    count = size // high
    lane_all = lax.broadcasted_iota(jnp.int32, (size, size), 1)
    diag = lane_all == lax.broadcasted_iota(jnp.int32, (size, size), 0)
    trace = jnp.sum(
        jnp.sum(jnp.where(diag, gram, 0.0), axis=0, keepdims=True), axis=1, keepdims=True
    )
    shift = 0.0001 * trace / size + 1e-06
    gram = jnp.where(diag, gram + shift, gram)
    rows = [gram[high * g : high * g + high, :] for g in range(count)]
    shape = (high, size)
    lane = lax.broadcasted_iota(jnp.int32, shape, 1)
    sub = lax.broadcasted_iota(jnp.int32, shape, 0)

    def along_lanes(block, at):
        return jnp.broadcast_to(block[:, at : at + 1], shape)

    def along_rows(block, at):
        return jnp.broadcast_to(block[at : at + 1, :], shape)

    found = []
    for b in range(count):
        first = b * high
        panel = rows[b]
        columns = [along_lanes(panel, first + k) for k in range(high)]
        inside = (lane >= first) & (lane < first + high)
        panel = jnp.where(inside, jnp.where(lane - first == sub, 1.0, 0.0), panel)
        forward, full = panel, panel
        forward_scale = jnp.zeros(shape, jnp.float32)
        full_scale = jnp.zeros(shape, jnp.float32)
        for i in range(high):
            pivot = along_rows(columns[i], i)
            inverse = 1.0 / pivot
            others = jnp.where(sub == i, 0.0, columns[i])
            below = jnp.where(sub > i, columns[i], 0.0)
            for k in range(i + 1, high):
                columns[k] = columns[k] - others * along_rows(columns[k], i) * inverse
            row = along_rows(forward, i) * inverse
            forward = forward - below * row
            full = full - others * row
            forward_scale = jnp.where(sub == i, lax.rsqrt(pivot), forward_scale)
            full_scale = jnp.where(sub == i, inverse, full_scale)
        found.append(jnp.where(lane < first + high, forward * forward_scale, 0.0))
        if b + 1 == count:
            break
        full = full * full_scale
        full_rows = [along_rows(full, k) for k in range(high)]
        for g in range(b + 1, count):
            terms = [along_lanes(rows[g], first + k) * full_rows[k] for k in range(high)]
            while len(terms) > 1:
                terms = [terms[t] + terms[t + 1] for t in range(0, len(terms), 2)]
            rows[g] = jnp.where(inside, 0.0, rows[g]) - terms[0]
    return jnp.concatenate(found, axis=0)


def in_parts(block):
    high = block.astype(jnp.bfloat16)
    rest = block - high.astype(jnp.float32)
    middle = rest.astype(jnp.bfloat16)
    return high, middle, (rest - middle.astype(jnp.float32)).astype(jnp.bfloat16)


def short_dot(left, right):
    return jnp.dot(left, right, preferred_element_type=jnp.float32)


def quotient(value, divisor, below):
    shift = 20
    factor = -(-(2**shift) // divisor)
    assert all(v * factor >> shift == v // divisor for v in range(below))
    assert below * factor < 2**31
    return value * factor >> shift


def spmm_body(
    slots_ref,
    tiles_ref,
    sketch_ref,
    keep_ref,
    send_ref,
    dense,
    held,
    slots,
    tile_sem,
    sketch_sems,
    slots_sem,
    *,
    leaves,
):
    tile_count, tile_size, _ = tiles_ref.shape
    depth = sketch_ref.shape[0]
    rows = dense.shape[0]
    half = rows // 2
    col_tiles = depth // tile_size
    chunks = sketch_sems.shape[0]
    chunk = depth // chunks
    leaf_tiles = rows // leaves // tile_size
    me = lax.axis_index("col")
    slots_load = pltpu.make_async_copy(slots_ref, slots, slots_sem)
    loads = [
        pltpu.make_async_copy(
            sketch_ref.at[pl.ds(k * chunk, chunk)], held.at[pl.ds(k * chunk, chunk)], sketch_sems.at[k]
        )
        for k in range(chunks)
    ]
    for load in [slots_load] + loads:
        load.start()

    @pl.loop(0, rows // 64)
    def _(i):
        dense[pl.ds(pl.multiple_of(i * 64, 64), 64), :] = jnp.zeros((64, depth), dense.dtype)

    slots_load.wait()
    together = math.gcd(tile_count, 8)

    @pl.loop(0, tile_count // together)
    def _(group):
        for member in range(together):
            t = group * together + member
            slot = slots[t]
            row_tile = quotient(slot, col_tiles, rows // tile_size * col_tiles)
            column = slot - row_tile * col_tiles
            leaf = quotient(row_tile, leaf_tiles, rows // tile_size)
            away = leaf ^ me
            block = (away & 1) * (leaves // 2) + (away >> 1)
            row = pl.multiple_of((block * leaf_tiles + row_tile - leaf * leaf_tiles) * tile_size, tile_size)
            col = pl.multiple_of(column * tile_size, tile_size)
            pltpu.make_async_copy(
                tiles_ref.at[t], dense.at[pl.ds(row, tile_size), pl.ds(col, tile_size)], tile_sem
            ).start()

    pltpu.make_async_copy(tiles_ref, tiles_ref, tile_sem).wait()
    for k in range(chunks):
        loads[k].wait()
        for start, ref in ((half, send_ref), (0, keep_ref)):
            part = jnp.dot(
                dense[start : start + half, k * chunk : (k + 1) * chunk],
                held[k * chunk : (k + 1) * chunk, :],
                preferred_element_type=jnp.float32,
            )
            if k == 0:
                ref[...] = part
            else:
                ref[...] += part


def sample_rows(tiles, tile_slots, sketch, leaf):
    tile_size = tiles.shape[1]
    depth, width = sketch.shape
    leaves = lax.axis_size("col")
    rows = leaf * leaves
    half = rows // 2
    chunks = math.gcd(depth // tile_size, 4)
    return pl.pallas_call(
        functools.partial(spmm_body, leaves=leaves),
        out_shape=[jax.ShapeDtypeStruct((half, width), jnp.float32)] * 2,
        in_specs=[HBM] * 3,
        out_specs=[VMEM] * 2,
        scratch_shapes=[
            pltpu.VMEM((rows, depth), jnp.bfloat16),
            pltpu.VMEM((depth, width), jnp.bfloat16),
            pltpu.SMEM(tile_slots.shape, jnp.int32),
            pltpu.SemaphoreType.DMA,
            pltpu.SemaphoreType.DMA((chunks,)),
            pltpu.SemaphoreType.DMA,
        ],
        compiler_params=pltpu.CompilerParams(vmem_limit_bytes=48 * 2**20),
        cost_estimate=pl.CostEstimate(
            flops=2 * rows * depth * width,
            bytes_accessed=2 * (tiles.size + sketch.size) + 4 * rows * width,
            transcendentals=0,
        ),
        name="spmm",
    )(tile_slots, tiles, sketch)


def reduce_body(*refs):
    sub_ref, ref = refs[:2]
    outs = refs[len(refs) // 2 + 1 :]
    rank = sub_ref.shape[1]
    high, middle, low = in_parts(sub_ref[...])
    two = jnp.concatenate([high, middle], axis=1)
    first, second, third = in_parts(ref[...])
    wide = short_dot(second, two) + short_dot(first, two)
    rest = short_dot(third, high) + short_dot(first, low)
    outs[0][...] = wide[:, :rank] + (wide[:, rank:] + rest)
    if len(outs) > 1:
        exact = refs[2][...]
        wide = short_dot(exact, two)
        outs[1][...] = wide[:, :rank] + (wide[:, rank:] + short_dot(exact, low))


def reduce_step(subsketch, *blocks):
    rank = subsketch.shape[1]
    return pl.pallas_call(
        reduce_body,
        out_shape=[jax.ShapeDtypeStruct((block.shape[0], rank), jnp.float32) for block in blocks],
        in_specs=[VMEM] * (1 + len(blocks)),
        out_specs=[VMEM] * len(blocks),
        compiler_params=small_params(),
        cost_estimate=small_cost(1),
        name="reduced_" + str(len(blocks)),
    )(subsketch, *blocks)


def leaf_body(keep_ref, first_ref, second_ref, sketch_red_ref, _, basis_ref, basis_t_ref, pair_ref):
    rank = keep_ref.shape[-1]
    reduced = keep_ref[...] + first_ref[...] + second_ref[...]
    reduced_t = reduced.T
    both = dot(reduced_t, jnp.concatenate([reduced, sketch_red_ref[...]], axis=1))
    inverse = inverse_factor(both[:, :rank])
    moved = dot(inverse, both)
    pair_ref[:rank, :] = moved[:, :rank]
    pair_ref[rank:, :] = moved[:, rank:]
    basis_ref[...] = dot_nt(reduced, inverse)
    basis_t_ref[...] = dot(inverse, reduced_t)


def small_params():
    return pltpu.CompilerParams(vmem_limit_bytes=32 * 2**20)


def small_cost(micros):
    return pl.CostEstimate(flops=micros * 10**7, bytes_accessed=micros * 3 * 10**4, transcendentals=0)


def leaf_step(keep, first, second, sketch_red, after):
    leaf, rank = sketch_red.shape
    f32 = jnp.float32
    part = pl.BlockSpec((leaf, rank), lambda step: (0, 0))
    return pl.pallas_call(
        leaf_body,
        grid=(1,),
        out_shape=[
            jax.ShapeDtypeStruct((leaf, rank), f32),
            jax.ShapeDtypeStruct((rank, leaf), f32),
            jax.ShapeDtypeStruct((2 * rank, rank), f32),
        ],
        in_specs=[part, part, VMEM, VMEM, ANY],
        out_specs=[VMEM] * 3,
        compiler_params=small_params(),
        cost_estimate=small_cost(8),
        name="leaf_orth",
    )(keep, first, second, sketch_red, after)


def turned(coupling_ref, tree_level):
    position = lax.axis_index("row") * lax.axis_size("col") + lax.axis_index("col")
    upper = position // 2**tree_level % 2 == 1
    coupling = coupling_ref[0, 0].astype(jnp.float32)
    coupling_t = coupling.T
    return jnp.where(upper, coupling_t, coupling), jnp.where(upper, coupling, coupling_t)


def merge_body(tree_level, *refs):
    own_ref, other_ref, coupling_ref = refs[:3]
    block_ref, maps_ref, pair_ref = refs[-3:]
    last = tree_level == LEVELS - 1
    rank = own_ref.shape[-1]
    ahead, back = turned(coupling_ref, tree_level)
    own_sample, own_sketch = own_ref[:rank], own_ref[rank:]
    other_sample, other_sketch = other_ref[:rank], other_ref[rank:]
    own = own_sample - dot(ahead, other_sketch)
    other = other_sample - dot(back, own_sketch)
    own_t, other_t = own.T, other.T
    stacked_t = jnp.concatenate([own_t, other_t], axis=1)
    right = jnp.concatenate(
        [
            jnp.concatenate([own, own_sketch], axis=1),
            jnp.concatenate([other, other_sketch], axis=1),
        ],
        axis=0,
    )
    both = dot(stacked_t, right)
    inverse = inverse_factor(both[:, :rank])
    block_ref[...] = dot_nt(own, inverse)
    if last:
        pair_ref[...] = dot(inverse, stacked_t)
        return
    moved = dot(inverse, both)
    pair_ref[:rank, :] = moved[:, :rank]
    pair_ref[rank:, :] = moved[:, rank:]
    maps_ref[0] = dot(inverse, own_t)
    maps_ref[1] = dot(inverse, dot(other_t, back))


def coupling_spec(couplings, tree_level):
    return pl.BlockSpec((1, 1) + couplings.shape[2:], lambda step: (0, tree_level, 0, 0))


def merge_step(tree_level, own, other, couplings, after):
    rank = own.shape[1]
    f32 = jnp.float32
    last = tree_level == LEVELS - 1
    return pl.pallas_call(
        functools.partial(merge_body, tree_level),
        grid=(1,),
        out_shape=[
            jax.ShapeDtypeStruct((rank, rank), f32),
            jax.ShapeDtypeStruct((8, rank) if last else (2, rank, rank), f32),
            jax.ShapeDtypeStruct((rank, 2 * rank) if last else (2 * rank, rank), f32),
        ],
        in_specs=[VMEM, VMEM, coupling_spec(couplings, tree_level)] + [ANY] * len(after),
        out_specs=[VMEM, ANY if last else VMEM, VMEM],
        compiler_params=small_params(),
        cost_estimate=small_cost(8),
        name=f"merge_orth_{tree_level}",
    )(own, other, couplings, *after)


def lower_body(*refs):
    keep_ref, first_ref, second_ref, leaf_sketch_ref, basis_t_ref = refs[:5]
    ways = (refs[-1].shape[1]) // refs[-2].shape[1]
    maps_refs = refs[5 : -1 - ways]
    out_refs = refs[-1 - ways : -1]
    wide = refs[-1]
    rank = basis_t_ref.shape[0]
    sample = keep_ref[...] + first_ref[...] + second_ref[...]
    sketch = leaf_sketch_ref[...].astype(jnp.float32)
    on_sample = basis_t_ref[...]
    on_sketch = jnp.zeros_like(on_sample)
    for maps_ref in maps_refs:
        lifted, crossed = maps_ref[0], maps_ref[1]
        on_sketch = dot(lifted, on_sketch) - dot(crossed, on_sample)
        on_sample = dot(lifted, on_sample)
    wide[:rank, :] = dot(on_sample, sample) + dot(on_sketch, sketch)
    wide[rank:, :] = dot(on_sample, sketch)
    me = lax.axis_index("col")
    part = wide.shape[1] // ways
    for away in range(ways):
        out_refs[away][...] = wide[:, pl.ds(pl.multiple_of((me ^ away) * part, part), part)]


def lower_step(keep, first, second, row_sketch, basis_t, maps):
    ways = lax.axis_size("col")
    leaf, width = row_sketch.shape
    rank = basis_t.shape[0]
    part = pl.BlockSpec((leaf, width), lambda step: (0, 0))
    return pl.pallas_call(
        lower_body,
        grid=(1,),
        out_shape=[jax.ShapeDtypeStruct((2 * rank, width // ways), jnp.float32)] * ways,
        in_specs=[part, part] + [VMEM] * (3 + len(maps)),
        out_specs=[VMEM] * ways,
        scratch_shapes=[pltpu.VMEM((2 * rank, width), jnp.float32)],
        compiler_params=small_params(),
        cost_estimate=small_cost(2),
        name="lower_maps",
    )(keep, first, second, row_sketch, basis_t, *maps)


def upper_body(*refs):
    maps_ref, out_ref = refs[-2:]
    total = refs[0][...]
    for ref in refs[1:-2]:
        total = total + ref[...]
    rank = maps_ref.shape[1]
    sample, sketch = total[:rank], total[rank:]
    lifted = maps_ref[0]
    out_ref[:rank, :] = dot(lifted, sample) - dot(maps_ref[1], sketch)
    out_ref[rank:, :] = dot(lifted, sketch)


def upper_step(tree_level, parts, maps):
    return pl.pallas_call(
        upper_body,
        out_shape=jax.ShapeDtypeStruct(parts[0].shape, jnp.float32),
        in_specs=[VMEM] * (len(parts) + 1),
        out_specs=VMEM,
        compiler_params=small_params(),
        cost_estimate=small_cost(1),
        name=f"upper_maps_{tree_level}",
    )(*parts, maps)


def top_body(own_ref, other_ref, coupling_ref, basis_t_ref, out_ref):
    rank = own_ref.shape[0] // 2
    ahead, back = turned(coupling_ref, LEVELS - 1)
    own = own_ref[:rank] - dot(ahead, other_ref[rank:])
    other = other_ref[:rank] - dot(back, own_ref[rank:])
    out_ref[...] = dot(basis_t_ref[...], jnp.concatenate([own, other], axis=0))


def top_step(own, other, couplings, basis_t):
    return pl.pallas_call(
        top_body,
        grid=(1,),
        out_shape=jax.ShapeDtypeStruct((own.shape[0] // 2, own.shape[1]), jnp.float32),
        in_specs=[VMEM, VMEM, coupling_spec(couplings, LEVELS - 1), VMEM],
        out_specs=VMEM,
        compiler_params=small_params(),
        cost_estimate=small_cost(1),
        name="top_sample",
    )(own, other, couplings, basis_t)


def columns_body(*refs):
    sems = refs[-1]
    out_ref = refs[-2]
    pieces = refs[:-2]
    ways = len(pieces)
    me = lax.axis_index("col")
    part = out_ref.shape[2] // ways
    copies = [
        pltpu.make_async_copy(
            pieces[away],
            out_ref.at[0, :, pl.ds(pl.multiple_of((me ^ away) * part, part), part)],
            sems.at[away],
        )
        for away in range(ways)
    ]
    for copy in copies:
        copy.start()
    for copy in copies:
        copy.wait()


def columns_step(pieces):
    rank, part = pieces[0].shape
    ways = len(pieces)
    return pl.pallas_call(
        columns_body,
        out_shape=jax.ShapeDtypeStruct((1, rank, part * ways), jnp.float32),
        in_specs=[VMEM] * ways,
        out_specs=ANY,
        scratch_shapes=[pltpu.SemaphoreType.DMA((ways,))],
        name="top_columns",
    )(*pieces)


def per_device(tiles, tile_slots, sketch, row_sketch, subsketch, couplings):
    ways = lax.axis_size("col")
    col_bits = ways.bit_length() - 1
    leaf = row_sketch.shape[0]
    keep, send = sample_rows(tiles, tile_slots, sketch, leaf)
    (send_red,) = reduce_step(subsketch, send)
    first_red = from_partner(send_red, "col", 1)
    keep_red, sketch_red = reduce_step(subsketch, keep, row_sketch)
    passed_red, send = lax.optimization_barrier((keep_red[leaf:] + first_red[leaf:], send))
    second_red = from_partner(passed_red, "col", 2)
    first = from_partner(send, "col", 1)
    passed, second_red = lax.optimization_barrier((keep[leaf:] + first[leaf:], second_red))
    second = from_partner(passed, "col", 2)
    leaf_basis, basis_t, pair = leaf_step(keep_red, first_red, second_red, sketch_red, passed)
    blocks, low_maps, after, parts = [], [], [], []
    for tree_level in range(LEVELS):
        if tree_level < LEVELS - 1:
            other = from_partner(pair, ROW_COL, 2**tree_level)
        else:
            other = waiting
        if tree_level == col_bits - 1:
            after = [second]
        block, maps, pair = merge_step(tree_level, pair, other, couplings, after)
        blocks.append(block)
        if tree_level == LEVELS - 1:
            break
        if tree_level < col_bits:
            low_maps.append(maps)
        else:
            mine = upper_step(tree_level, parts, maps)
            parts = [mine, from_partner(mine, ROW_COL, 2**tree_level)]
            after = [mine]
        if tree_level == col_bits - 1:
            cut = lower_step(keep, first, second, row_sketch, basis_t, low_maps)
            parts = [cut[0]] + [from_partner(cut[away], "col", away) for away in range(1, ways)]
            after = [cut[0]]
        if tree_level == LEVELS - 2:
            waiting = from_partner(pair, ROW_COL, 2 ** (LEVELS - 1))
            whole, waiting = lax.optimization_barrier((parts[0] + parts[1], waiting))
            far = from_partner(whole, ROW_COL, 2 ** (LEVELS - 1))
            after = [whole]
    top = top_step(whole, far, couplings, pair)
    pieces = [top] + [from_partner(top, "col", away) for away in range(1, ways)]
    transfer = jnp.stack(blocks, axis=0)[None]
    return (leaf_basis, transfer, columns_step(pieces))


def solution(mesh):
    return jax.shard_map(
        per_device,
        mesh=mesh,
        in_specs=(
            P(("row", "col"), None, None),
            P(("row", "col")),
            P("col", None),
            P(("row", "col"), None),
            P(),
            P(("row", "col"), None, None, None),
        ),
        out_specs=(
            P(("row", "col"), None),
            P(("row", "col"), None, None, None),
            P(("row", "col"), None, None),
        ),
        check_vma=False,
    )
```

```python
import functools
import math

import jax
import jax.numpy as jnp
from jax import lax
from jax.experimental import pallas as pl
from jax.experimental.pallas import tpu as pltpu
from jax.sharding import PartitionSpec as P

LEVELS = 5
ROW_COL = ("row", "col")
VMEM = pl.BlockSpec(memory_space=pltpu.VMEM)
ANY = pl.BlockSpec(memory_space=pl.ANY)
HBM = pl.BlockSpec(memory_space=pltpu.HBM)


def from_partner(block, axis, distance):
    count = lax.axis_size(axis)
    route = []
    for low in range(count):
        high = low ^ distance
        if high < count:
            route.append((low, high))
    return lax.ppermute(block, axis, route)


def dot(left, right):
    return jnp.dot(left, right, precision=lax.Precision.HIGHEST, preferred_element_type=jnp.float32)


def dot_nt(left, right):
    return lax.dot_general(
        left,
        right,
        (((1,), (1,)), ((), ())),
        precision=lax.Precision.HIGHEST,
        preferred_element_type=jnp.float32,
    )


def square_sum(block):
    squares = block * block
    return jnp.sum(jnp.sum(squares, axis=0, keepdims=True), axis=1, keepdims=True)


def inverse_factor(gram, trace):
    size = gram.shape[0]
    high = 8
    count = size // high
    square = (size, size)
    diag = lax.broadcasted_iota(jnp.int32, square, 1) == lax.broadcasted_iota(jnp.int32, square, 0)
    gram = jnp.where(diag, gram + (0.0001 * trace / size + 1e-06), gram)
    rows = [gram[high * g : high * g + high, :] for g in range(count)]
    shape = (high, size)
    lane = lax.broadcasted_iota(jnp.int32, shape, 1)
    sub = lax.broadcasted_iota(jnp.int32, shape, 0)

    def along_lanes(block, first):
        return [jnp.broadcast_to(block[:, first + k : first + k + 1], shape) for k in range(high)]

    def along_rows(block, at):
        return jnp.broadcast_to(block[at : at + 1, :], shape)

    found = []
    here = along_lanes(rows[0], 0)
    for b in range(count):
        first, after = b * high, (b + 1) * high
        more = b + 1 < count
        inside = (lane >= first) & (lane < after)
        full = jnp.where(inside, jnp.where(lane - first == sub, 1.0, 0.0), rows[b])
        done = jnp.zeros(shape, jnp.float32)
        if more:
            under = along_lanes(rows[b + 1], first)
            right = along_lanes(rows[b], after)
            corner = along_lanes(rows[b + 1], after)
        for i in range(high):
            root = lax.rsqrt(along_rows(here[i], i))
            inverse = root * root
            below = jnp.where(sub > i, here[i], 0.0)
            scaled = below * inverse
            if more:
                low = under[i] * inverse
            for k in range(i + 1, high):
                x = along_rows(here[k], i)
                here[k] = here[k] - ((below * x) * inverse if k < i + 3 else scaled * x)
                if more:
                    under[k] = under[k] - low * x
            if more:
                for k in range(high):
                    x = along_rows(right[k], i)
                    right[k] = right[k] - scaled * x
                    corner[k] = corner[k] - low * x
            x = along_rows(full, i)
            done = jnp.where(sub == i, x * root, done)
            full = full - scaled * x
        found.append(jnp.where(lane < after, done, 0.0))
        if not more:
            break
        change = dot(done.T, done)
        for g in range(b + 1, count):
            rows[g] = jnp.where(inside, 0.0, rows[g]) - change[high * g : high * g + high]
        here = corner
    return jnp.concatenate(found, axis=0)


def in_parts(block):
    high = block.astype(jnp.bfloat16)
    rest = block - high.astype(jnp.float32)
    middle = rest.astype(jnp.bfloat16)
    return high, middle, (rest - middle.astype(jnp.float32)).astype(jnp.bfloat16)


def short_dot(left, right):
    return jnp.dot(left, right, preferred_element_type=jnp.float32)


def quotient(value, divisor, below):
    shift = 20
    factor = -(-(2**shift) // divisor)
    assert all(v * factor >> shift == v // divisor for v in range(below))
    assert below * factor < 2**31
    return value * factor >> shift


def spmm_body(
    slots_ref,
    tiles_ref,
    sketch_ref,
    keep_ref,
    send_ref,
    dense,
    held,
    slots,
    tile_sem,
    sketch_sems,
    slots_sem,
    *,
    leaves,
):
    tile_count, tile_size, _ = tiles_ref.shape
    depth = sketch_ref.shape[0]
    rows = dense.shape[0]
    half = rows // 2
    col_tiles = depth // tile_size
    chunks = sketch_sems.shape[0]
    chunk = depth // chunks
    leaf_tiles = rows // leaves // tile_size
    me = lax.axis_index("col")
    slots_load = pltpu.make_async_copy(slots_ref, slots, slots_sem)
    loads = [
        pltpu.make_async_copy(
            sketch_ref.at[pl.ds(k * chunk, chunk)], held.at[pl.ds(k * chunk, chunk)], sketch_sems.at[k]
        )
        for k in range(chunks)
    ]
    for load in [slots_load] + loads:
        load.start()

    @pl.loop(0, rows // 64)
    def _(i):
        dense[pl.ds(pl.multiple_of(i * 64, 64), 64), :] = jnp.zeros((64, depth), dense.dtype)

    slots_load.wait()
    together = math.gcd(tile_count, 8)

    @pl.loop(0, tile_count // together)
    def _(group):
        for member in range(together):
            t = group * together + member
            slot = slots[t]
            row_tile = quotient(slot, col_tiles, rows // tile_size * col_tiles)
            column = slot - row_tile * col_tiles
            leaf = quotient(row_tile, leaf_tiles, rows // tile_size)
            away = leaf ^ me
            block = (away & 1) * (leaves // 2) + (away >> 1)
            row = pl.multiple_of((block * leaf_tiles + row_tile - leaf * leaf_tiles) * tile_size, tile_size)
            col = pl.multiple_of(column * tile_size, tile_size)
            pltpu.make_async_copy(
                tiles_ref.at[t], dense.at[pl.ds(row, tile_size), pl.ds(col, tile_size)], tile_sem
            ).start()

    pltpu.make_async_copy(tiles_ref, tiles_ref, tile_sem).wait()
    for k in range(chunks):
        loads[k].wait()
        for start, ref in ((half, send_ref), (0, keep_ref)):
            part = jnp.dot(
                dense[start : start + half, k * chunk : (k + 1) * chunk],
                held[k * chunk : (k + 1) * chunk, :],
                preferred_element_type=jnp.float32,
            )
            if k == 0:
                ref[...] = part
            else:
                ref[...] += part


def sample_rows(tiles, tile_slots, sketch, leaf):
    tile_size = tiles.shape[1]
    depth, width = sketch.shape
    leaves = lax.axis_size("col")
    rows = leaf * leaves
    half = rows // 2
    chunks = math.gcd(depth // tile_size, 4)
    return pl.pallas_call(
        functools.partial(spmm_body, leaves=leaves),
        out_shape=[jax.ShapeDtypeStruct((half, width), jnp.float32)] * 2,
        in_specs=[HBM] * 3,
        out_specs=[VMEM] * 2,
        scratch_shapes=[
            pltpu.VMEM((rows, depth), jnp.bfloat16),
            pltpu.VMEM((depth, width), jnp.bfloat16),
            pltpu.SMEM(tile_slots.shape, jnp.int32),
            pltpu.SemaphoreType.DMA,
            pltpu.SemaphoreType.DMA((chunks,)),
            pltpu.SemaphoreType.DMA,
        ],
        compiler_params=pltpu.CompilerParams(vmem_limit_bytes=48 * 2**20),
        cost_estimate=pl.CostEstimate(
            flops=2 * rows * depth * width,
            bytes_accessed=2 * (tiles.size + sketch.size) + 4 * rows * width,
            transcendentals=0,
        ),
        name="spmm",
    )(tile_slots, tiles, sketch)


def reduce_body(*refs):
    sub_ref, ref = refs[:2]
    outs = refs[len(refs) // 2 + 1 :]
    rank = sub_ref.shape[1]
    high, middle, low = in_parts(sub_ref[...])
    two = jnp.concatenate([high, middle], axis=1)
    first, second, third = in_parts(ref[...])
    wide = short_dot(second, two) + short_dot(first, two)
    rest = short_dot(third, high) + short_dot(first, low)
    outs[0][...] = wide[:, :rank] + (wide[:, rank:] + rest)
    if len(outs) > 1:
        exact = refs[2][...]
        wide = short_dot(exact, two)
        outs[1][...] = wide[:, :rank] + (wide[:, rank:] + short_dot(exact, low))


def reduce_step(subsketch, *blocks):
    rank = subsketch.shape[1]
    return pl.pallas_call(
        reduce_body,
        out_shape=[jax.ShapeDtypeStruct((block.shape[0], rank), jnp.float32) for block in blocks],
        in_specs=[VMEM] * (1 + len(blocks)),
        out_specs=[VMEM] * len(blocks),
        compiler_params=small_params(),
        cost_estimate=small_cost(1),
        name="reduced_" + str(len(blocks)),
    )(subsketch, *blocks)


def leaf_body(keep_ref, first_ref, second_ref, sketch_red_ref, _, basis_ref, basis_t_ref, pair_ref):
    rank = keep_ref.shape[-1]
    reduced = keep_ref[...] + first_ref[...] + second_ref[...]
    reduced_t = reduced.T
    both = dot(reduced_t, jnp.concatenate([reduced, sketch_red_ref[...]], axis=1))
    inverse = inverse_factor(both[:, :rank], square_sum(reduced))
    moved = dot(inverse, jnp.concatenate([both, reduced_t], axis=1))
    pair_ref[:rank, :] = moved[:, :rank]
    pair_ref[rank:, :] = moved[:, rank : 2 * rank]
    basis_t_ref[...] = moved[:, 2 * rank :]
    basis_ref[...] = dot_nt(reduced, inverse)


def small_params():
    return pltpu.CompilerParams(vmem_limit_bytes=32 * 2**20)


def small_cost(micros):
    return pl.CostEstimate(flops=micros * 10**7, bytes_accessed=micros * 3 * 10**4, transcendentals=0)


def leaf_step(keep, first, second, sketch_red, after):
    leaf, rank = sketch_red.shape
    f32 = jnp.float32
    part = pl.BlockSpec((leaf, rank), lambda step: (0, 0))
    return pl.pallas_call(
        leaf_body,
        grid=(1,),
        out_shape=[
            jax.ShapeDtypeStruct((leaf, rank), f32),
            jax.ShapeDtypeStruct((rank, leaf), f32),
            jax.ShapeDtypeStruct((2 * rank, rank), f32),
        ],
        in_specs=[part, part, VMEM, VMEM, ANY],
        out_specs=[VMEM] * 3,
        compiler_params=small_params(),
        cost_estimate=small_cost(8),
        name="leaf_orth",
    )(keep, first, second, sketch_red, after)


def turned(coupling_ref, tree_level):
    position = lax.axis_index("row") * lax.axis_size("col") + lax.axis_index("col")
    upper = position // 2**tree_level % 2 == 1
    coupling = coupling_ref[0, 0].astype(jnp.float32)
    coupling_t = coupling.T
    return jnp.where(upper, coupling_t, coupling), jnp.where(upper, coupling, coupling_t)


def merge_body(tree_level, *refs):
    own_ref, other_ref, coupling_ref = refs[:3]
    block_ref, maps_ref, pair_ref = refs[-3:]
    last = tree_level == LEVELS - 1
    rank = own_ref.shape[-1]
    ahead, back = turned(coupling_ref, tree_level)
    own_sample, own_sketch = own_ref[:rank], own_ref[rank:]
    other_sample, other_sketch = other_ref[:rank], other_ref[rank:]
    own = own_sample - dot(ahead, other_sketch)
    other = other_sample - dot(back, own_sketch)
    own_t, other_t = own.T, other.T
    stacked_t = jnp.concatenate([own_t, other_t], axis=1)
    stacked = jnp.concatenate([own, other], axis=0)
    right = jnp.concatenate(
        [stacked, jnp.concatenate([own_sketch, other_sketch], axis=0)], axis=1
    )
    both = dot(stacked_t, stacked if last else right)
    if not last:
        crossed = dot(other_t, back)
    inverse = inverse_factor(both[:, :rank], square_sum(own) + square_sum(other))
    block_ref[...] = dot_nt(own, inverse)
    if last:
        pair_ref[...] = dot(inverse, stacked_t)
        return
    moved = dot(inverse, jnp.concatenate([both, own_t, crossed], axis=1))
    pair_ref[:rank, :] = moved[:, :rank]
    pair_ref[rank:, :] = moved[:, rank : 2 * rank]
    maps_ref[0] = moved[:, 2 * rank : 3 * rank]
    maps_ref[1] = moved[:, 3 * rank :]


def coupling_spec(couplings, tree_level):
    return pl.BlockSpec((1, 1) + couplings.shape[2:], lambda step: (0, tree_level, 0, 0))


def merge_step(tree_level, own, other, couplings, after):
    rank = own.shape[1]
    f32 = jnp.float32
    last = tree_level == LEVELS - 1
    return pl.pallas_call(
        functools.partial(merge_body, tree_level),
        grid=(1,),
        out_shape=[
            jax.ShapeDtypeStruct((rank, rank), f32),
            jax.ShapeDtypeStruct((8, rank) if last else (2, rank, rank), f32),
            jax.ShapeDtypeStruct((rank, 2 * rank) if last else (2 * rank, rank), f32),
        ],
        in_specs=[VMEM, VMEM, coupling_spec(couplings, tree_level)] + [ANY] * len(after),
        out_specs=[VMEM, ANY if last else VMEM, VMEM],
        compiler_params=small_params(),
        cost_estimate=small_cost(8),
        name=f"merge_orth_{tree_level}",
    )(own, other, couplings, *after)


def lower_body(*refs):
    keep_ref, first_ref, second_ref, leaf_sketch_ref, basis_t_ref = refs[:5]
    ways = (refs[-1].shape[1]) // refs[-2].shape[1]
    maps_refs = refs[5 : -1 - ways]
    out_refs = refs[-1 - ways : -1]
    wide = refs[-1]
    rank = basis_t_ref.shape[0]
    sample = keep_ref[...] + first_ref[...] + second_ref[...]
    sketch = leaf_sketch_ref[...].astype(jnp.float32)
    on_sample = basis_t_ref[...]
    on_sketch = jnp.zeros_like(on_sample)
    for maps_ref in maps_refs:
        lifted, crossed = maps_ref[0], maps_ref[1]
        on_sketch = dot(lifted, on_sketch) - dot(crossed, on_sample)
        on_sample = dot(lifted, on_sample)
    wide[:rank, :] = dot(on_sample, sample) + dot(on_sketch, sketch)
    wide[rank:, :] = dot(on_sample, sketch)
    me = lax.axis_index("col")
    part = wide.shape[1] // ways
    for away in range(ways):
        out_refs[away][...] = wide[:, pl.ds(pl.multiple_of((me ^ away) * part, part), part)]


def lower_step(keep, first, second, row_sketch, basis_t, maps):
    ways = lax.axis_size("col")
    leaf, width = row_sketch.shape
    rank = basis_t.shape[0]
    part = pl.BlockSpec((leaf, width), lambda step: (0, 0))
    return pl.pallas_call(
        lower_body,
        grid=(1,),
        out_shape=[jax.ShapeDtypeStruct((2 * rank, width // ways), jnp.float32)] * ways,
        in_specs=[part, part] + [VMEM] * (3 + len(maps)),
        out_specs=[VMEM] * ways,
        scratch_shapes=[pltpu.VMEM((2 * rank, width), jnp.float32)],
        compiler_params=small_params(),
        cost_estimate=small_cost(2),
        name="lower_maps",
    )(keep, first, second, row_sketch, basis_t, *maps)


def upper_body(*refs):
    maps_ref, out_ref = refs[-2:]
    total = refs[0][...]
    for ref in refs[1:-2]:
        total = total + ref[...]
    rank = maps_ref.shape[1]
    sample, sketch = total[:rank], total[rank:]
    lifted = maps_ref[0]
    out_ref[:rank, :] = dot(lifted, sample) - dot(maps_ref[1], sketch)
    out_ref[rank:, :] = dot(lifted, sketch)


def upper_step(tree_level, parts, maps):
    return pl.pallas_call(
        upper_body,
        out_shape=jax.ShapeDtypeStruct(parts[0].shape, jnp.float32),
        in_specs=[VMEM] * (len(parts) + 1),
        out_specs=VMEM,
        compiler_params=small_params(),
        cost_estimate=small_cost(1),
        name=f"upper_maps_{tree_level}",
    )(*parts, maps)


def top_body(own_ref, other_ref, coupling_ref, basis_t_ref, out_ref):
    rank = own_ref.shape[0] // 2
    ahead, back = turned(coupling_ref, LEVELS - 1)
    own = own_ref[:rank] - dot(ahead, other_ref[rank:])
    other = other_ref[:rank] - dot(back, own_ref[rank:])
    out_ref[...] = dot(basis_t_ref[...], jnp.concatenate([own, other], axis=0))


def top_step(own, other, couplings, basis_t):
    return pl.pallas_call(
        top_body,
        grid=(1,),
        out_shape=jax.ShapeDtypeStruct((own.shape[0] // 2, own.shape[1]), jnp.float32),
        in_specs=[VMEM, VMEM, coupling_spec(couplings, LEVELS - 1), VMEM],
        out_specs=VMEM,
        compiler_params=small_params(),
        cost_estimate=small_cost(1),
        name="top_sample",
    )(own, other, couplings, basis_t)


def columns_body(*refs):
    sems = refs[-1]
    out_ref = refs[-2]
    pieces = refs[:-2]
    ways = len(pieces)
    me = lax.axis_index("col")
    part = out_ref.shape[2] // ways
    copies = [
        pltpu.make_async_copy(
            pieces[away],
            out_ref.at[0, :, pl.ds(pl.multiple_of((me ^ away) * part, part), part)],
            sems.at[away],
        )
        for away in range(ways)
    ]
    for copy in copies:
        copy.start()
    for copy in copies:
        copy.wait()


def columns_step(pieces):
    rank, part = pieces[0].shape
    ways = len(pieces)
    return pl.pallas_call(
        columns_body,
        out_shape=jax.ShapeDtypeStruct((1, rank, part * ways), jnp.float32),
        in_specs=[VMEM] * ways,
        out_specs=ANY,
        scratch_shapes=[pltpu.SemaphoreType.DMA((ways,))],
        name="top_columns",
    )(*pieces)


def per_device(tiles, tile_slots, sketch, row_sketch, subsketch, couplings):
    ways = lax.axis_size("col")
    col_bits = ways.bit_length() - 1
    leaf = row_sketch.shape[0]
    keep, send = sample_rows(tiles, tile_slots, sketch, leaf)
    (send_red,) = reduce_step(subsketch, send)
    first_red = from_partner(send_red, "col", 1)
    keep_red, sketch_red = reduce_step(subsketch, keep, row_sketch)
    passed_red, send = lax.optimization_barrier((keep_red[leaf:] + first_red[leaf:], send))
    second_red = from_partner(passed_red, "col", 2)
    first = from_partner(send, "col", 1)
    passed, second_red = lax.optimization_barrier((keep[leaf:] + first[leaf:], second_red))
    second = from_partner(passed, "col", 2)
    leaf_basis, basis_t, pair = leaf_step(keep_red, first_red, second_red, sketch_red, passed)
    blocks, low_maps, after, parts = [], [], [], []
    for tree_level in range(LEVELS):
        if tree_level < LEVELS - 1:
            other = from_partner(pair, ROW_COL, 2**tree_level)
        else:
            other = waiting
        if tree_level == col_bits - 1:
            after = [second]
        block, maps, pair = merge_step(tree_level, pair, other, couplings, after)
        blocks.append(block)
        if tree_level == LEVELS - 1:
            break
        if tree_level < col_bits:
            low_maps.append(maps)
        else:
            mine = upper_step(tree_level, parts, maps)
            parts = [mine, from_partner(mine, ROW_COL, 2**tree_level)]
            after = [mine]
        if tree_level == col_bits - 1:
            cut = lower_step(keep, first, second, row_sketch, basis_t, low_maps)
            parts = [cut[0]] + [from_partner(cut[away], "col", away) for away in range(1, ways)]
            after = [cut[0]]
        if tree_level == LEVELS - 2:
            waiting = from_partner(pair, ROW_COL, 2 ** (LEVELS - 1))
            whole, waiting = lax.optimization_barrier((parts[0] + parts[1], waiting))
            far = from_partner(whole, ROW_COL, 2 ** (LEVELS - 1))
            after = [whole]
    top = top_step(whole, far, couplings, pair)
    pieces = [top] + [from_partner(top, "col", away) for away in range(1, ways)]
    transfer = jnp.stack(blocks, axis=0)[None]
    return (leaf_basis, transfer, columns_step(pieces))


def solution(mesh):
    return jax.shard_map(
        per_device,
        mesh=mesh,
        in_specs=(
            P(("row", "col"), None, None),
            P(("row", "col")),
            P("col", None),
            P(("row", "col"), None),
            P(),
            P(("row", "col"), None, None, None),
        ),
        out_specs=(
            P(("row", "col"), None),
            P(("row", "col"), None, None, None),
            P(("row", "col"), None, None),
        ),
        check_vma=False,
    )
```

```python
import functools
import math

import jax
import jax.numpy as jnp
from jax import lax
from jax.experimental import pallas as pl
from jax.experimental.pallas import tpu as pltpu
from jax.sharding import PartitionSpec as P

LEVELS = 5
ROW_COL = ("row", "col")
VMEM = pl.BlockSpec(memory_space=pltpu.VMEM)
ANY = pl.BlockSpec(memory_space=pl.ANY)
HBM = pl.BlockSpec(memory_space=pltpu.HBM)


def from_partner(block, axis, distance):
    count = lax.axis_size(axis)
    route = []
    for low in range(count):
        high = low ^ distance
        if high < count:
            route.append((low, high))
    return lax.ppermute(block, axis, route)


def dot(left, right):
    return jnp.dot(left, right, precision=lax.Precision.HIGHEST, preferred_element_type=jnp.float32)


def dot_nt(left, right):
    return lax.dot_general(
        left,
        right,
        (((1,), (1,)), ((), ())),
        precision=lax.Precision.HIGHEST,
        preferred_element_type=jnp.float32,
    )


def square_sum(block):
    squares = block * block
    return jnp.sum(jnp.sum(squares, axis=0, keepdims=True), axis=1, keepdims=True)


def inverse_factor(gram, trace):
    size = gram.shape[0]
    high = 8
    count = size // high
    square = (size, size)
    diag = lax.broadcasted_iota(jnp.int32, square, 1) == lax.broadcasted_iota(jnp.int32, square, 0)
    gram = jnp.where(diag, gram + (0.0001 * trace / size + 1e-06), gram)
    rows = [gram[high * g : high * g + high, :] for g in range(count)]
    shape = (high, size)
    lane = lax.broadcasted_iota(jnp.int32, shape, 1)
    sub = lax.broadcasted_iota(jnp.int32, shape, 0)

    def along_lanes(block, first):
        return [jnp.broadcast_to(block[:, first + k : first + k + 1], shape) for k in range(high)]

    def along_rows(block, at):
        return jnp.broadcast_to(block[at : at + 1, :], shape)

    found = []
    here = along_lanes(rows[0], 0)
    for b in range(count):
        first, after = b * high, (b + 1) * high
        more = b + 1 < count
        inside = (lane >= first) & (lane < after)
        full = jnp.where(inside, jnp.where(lane - first == sub, 1.0, 0.0), rows[b])
        done = jnp.zeros(shape, jnp.float32)
        steps = []
        if more:
            under = along_lanes(rows[b + 1], first)
            right = along_lanes(rows[b], after)
            corner = along_lanes(rows[b + 1], after)
            below_row = jnp.where(inside, 0.0, rows[b + 1])
        for i in range(high):
            root = lax.rsqrt(along_rows(here[i], i))
            inverse = root * root
            below = jnp.where(sub > i, here[i], 0.0)
            scaled = below * inverse
            entries = {k: along_rows(here[k], i) for k in range(i + 1, high)}
            for k, x in entries.items():
                here[k] = here[k] - ((below * x) * inverse if k < i + 3 else scaled * x)
            x = along_rows(full, i)
            done = jnp.where(sub == i, x * root, done)
            full = full - scaled * x
            if not more:
                continue
            steps.append(({k: entry * inverse for k, entry in entries.items()}, x * inverse))
            low = under[i] * inverse
            for k, entry in entries.items():
                under[k] = under[k] - low * entry
            for k in range(high):
                entry = along_rows(right[k], i)
                right[k] = right[k] - scaled * entry
                corner[k] = corner[k] - low * entry
            below_row = below_row - low * x
        found.append(jnp.where(lane < after, done, 0.0))
        if not more:
            break
        rows[b + 1] = below_row
        for g in range(b + 2, count):
            columns = along_lanes(rows[g], first)
            row = jnp.where(inside, 0.0, rows[g])
            for i, (entries, x) in enumerate(steps):
                for k, entry in entries.items():
                    columns[k] = columns[k] - columns[i] * entry
                row = row - columns[i] * x
            rows[g] = row
        here = corner
    return jnp.concatenate(found, axis=0)


def in_parts(block):
    high = block.astype(jnp.bfloat16)
    rest = block - high.astype(jnp.float32)
    middle = rest.astype(jnp.bfloat16)
    return high, middle, (rest - middle.astype(jnp.float32)).astype(jnp.bfloat16)


def short_dot(left, right):
    return jnp.dot(left, right, preferred_element_type=jnp.float32)


def quotient(value, divisor, below):
    shift = 20
    factor = -(-(2**shift) // divisor)
    assert all(v * factor >> shift == v // divisor for v in range(below))
    assert below * factor < 2**31
    return value * factor >> shift


def spmm_body(
    slots_ref,
    tiles_ref,
    sketch_ref,
    keep_ref,
    send_ref,
    dense,
    held,
    slots,
    tile_sem,
    sketch_sems,
    slots_sem,
    *,
    leaves,
):
    tile_count, tile_size, _ = tiles_ref.shape
    depth = sketch_ref.shape[0]
    rows = dense.shape[0]
    half = rows // 2
    col_tiles = depth // tile_size
    chunks = sketch_sems.shape[0]
    chunk = depth // chunks
    leaf_tiles = rows // leaves // tile_size
    me = lax.axis_index("col")
    slots_load = pltpu.make_async_copy(slots_ref, slots, slots_sem)
    loads = [
        pltpu.make_async_copy(
            sketch_ref.at[pl.ds(k * chunk, chunk)], held.at[pl.ds(k * chunk, chunk)], sketch_sems.at[k]
        )
        for k in range(chunks)
    ]
    for load in [slots_load] + loads:
        load.start()

    @pl.loop(0, rows // 64)
    def _(i):
        dense[pl.ds(pl.multiple_of(i * 64, 64), 64), :] = jnp.zeros((64, depth), dense.dtype)

    slots_load.wait()
    together = math.gcd(tile_count, 8)

    @pl.loop(0, tile_count // together)
    def _(group):
        for member in range(together):
            t = group * together + member
            slot = slots[t]
            row_tile = quotient(slot, col_tiles, rows // tile_size * col_tiles)
            column = slot - row_tile * col_tiles
            leaf = quotient(row_tile, leaf_tiles, rows // tile_size)
            away = leaf ^ me
            block = (away & 1) * (leaves // 2) + (away >> 1)
            row = pl.multiple_of((block * leaf_tiles + row_tile - leaf * leaf_tiles) * tile_size, tile_size)
            col = pl.multiple_of(column * tile_size, tile_size)
            pltpu.make_async_copy(
                tiles_ref.at[t], dense.at[pl.ds(row, tile_size), pl.ds(col, tile_size)], tile_sem
            ).start()

    pltpu.make_async_copy(tiles_ref, tiles_ref, tile_sem).wait()
    for k in range(chunks):
        loads[k].wait()
        for start, ref in ((half, send_ref), (0, keep_ref)):
            part = jnp.dot(
                dense[start : start + half, k * chunk : (k + 1) * chunk],
                held[k * chunk : (k + 1) * chunk, :],
                preferred_element_type=jnp.float32,
            )
            if k == 0:
                ref[...] = part
            else:
                ref[...] += part


def sample_rows(tiles, tile_slots, sketch, leaf):
    tile_size = tiles.shape[1]
    depth, width = sketch.shape
    leaves = lax.axis_size("col")
    rows = leaf * leaves
    half = rows // 2
    chunks = math.gcd(depth // tile_size, 4)
    return pl.pallas_call(
        functools.partial(spmm_body, leaves=leaves),
        out_shape=[jax.ShapeDtypeStruct((half, width), jnp.float32)] * 2,
        in_specs=[HBM] * 3,
        out_specs=[VMEM] * 2,
        scratch_shapes=[
            pltpu.VMEM((rows, depth), jnp.bfloat16),
            pltpu.VMEM((depth, width), jnp.bfloat16),
            pltpu.SMEM(tile_slots.shape, jnp.int32),
            pltpu.SemaphoreType.DMA,
            pltpu.SemaphoreType.DMA((chunks,)),
            pltpu.SemaphoreType.DMA,
        ],
        compiler_params=pltpu.CompilerParams(vmem_limit_bytes=48 * 2**20),
        cost_estimate=pl.CostEstimate(
            flops=2 * rows * depth * width,
            bytes_accessed=2 * (tiles.size + sketch.size) + 4 * rows * width,
            transcendentals=0,
        ),
        name="spmm",
    )(tile_slots, tiles, sketch)


def reduce_body(*refs):
    sub_ref, ref = refs[:2]
    outs = refs[len(refs) // 2 + 1 :]
    rank = sub_ref.shape[1]
    high, middle, low = in_parts(sub_ref[...])
    two = jnp.concatenate([high, middle], axis=1)
    first, second, third = in_parts(ref[...])
    wide = short_dot(second, two) + short_dot(first, two)
    rest = short_dot(third, high) + short_dot(first, low)
    outs[0][...] = wide[:, :rank] + (wide[:, rank:] + rest)
    if len(outs) > 1:
        exact = refs[2][...]
        wide = short_dot(exact, two)
        outs[1][...] = wide[:, :rank] + (wide[:, rank:] + short_dot(exact, low))


def reduce_step(subsketch, *blocks):
    rank = subsketch.shape[1]
    return pl.pallas_call(
        reduce_body,
        out_shape=[jax.ShapeDtypeStruct((block.shape[0], rank), jnp.float32) for block in blocks],
        in_specs=[VMEM] * (1 + len(blocks)),
        out_specs=[VMEM] * len(blocks),
        compiler_params=small_params(),
        cost_estimate=small_cost(1),
        name="reduced_" + str(len(blocks)),
    )(subsketch, *blocks)


def leaf_body(keep_ref, first_ref, second_ref, sketch_red_ref, _, basis_ref, basis_t_ref, pair_ref):
    rank = keep_ref.shape[-1]
    reduced = keep_ref[...] + first_ref[...] + second_ref[...]
    reduced_t = reduced.T
    both = dot(reduced_t, jnp.concatenate([reduced, sketch_red_ref[...]], axis=1))
    inverse = inverse_factor(both[:, :rank], square_sum(reduced))
    moved = dot(inverse, jnp.concatenate([both, reduced_t], axis=1))
    pair_ref[:rank, :] = moved[:, :rank]
    pair_ref[rank:, :] = moved[:, rank : 2 * rank]
    basis_t_ref[...] = moved[:, 2 * rank :]
    basis_ref[...] = dot_nt(reduced, inverse)


def small_params():
    return pltpu.CompilerParams(vmem_limit_bytes=32 * 2**20)


def small_cost(micros):
    return pl.CostEstimate(flops=micros * 10**7, bytes_accessed=micros * 3 * 10**4, transcendentals=0)


def leaf_step(keep, first, second, sketch_red, after):
    leaf, rank = sketch_red.shape
    f32 = jnp.float32
    part = pl.BlockSpec((leaf, rank), lambda step: (0, 0))
    return pl.pallas_call(
        leaf_body,
        grid=(1,),
        out_shape=[
            jax.ShapeDtypeStruct((leaf, rank), f32),
            jax.ShapeDtypeStruct((rank, leaf), f32),
            jax.ShapeDtypeStruct((2 * rank, rank), f32),
        ],
        in_specs=[part, part, VMEM, VMEM, ANY],
        out_specs=[VMEM] * 3,
        compiler_params=small_params(),
        cost_estimate=small_cost(8),
        name="leaf_orth",
    )(keep, first, second, sketch_red, after)


def turned(coupling_ref, tree_level):
    position = lax.axis_index("row") * lax.axis_size("col") + lax.axis_index("col")
    upper = position // 2**tree_level % 2 == 1
    coupling = coupling_ref[0, 0].astype(jnp.float32)
    coupling_t = coupling.T
    return jnp.where(upper, coupling_t, coupling), jnp.where(upper, coupling, coupling_t)


def merge_body(tree_level, *refs):
    own_ref, other_ref, coupling_ref = refs[:3]
    block_ref, maps_ref, pair_ref = refs[-3:]
    last = tree_level == LEVELS - 1
    rank = own_ref.shape[-1]
    ahead, back = turned(coupling_ref, tree_level)
    own_sample, own_sketch = own_ref[:rank], own_ref[rank:]
    other_sample, other_sketch = other_ref[:rank], other_ref[rank:]
    own = own_sample - dot(ahead, other_sketch)
    other = other_sample - dot(back, own_sketch)
    own_t, other_t = own.T, other.T
    stacked_t = jnp.concatenate([own_t, other_t], axis=1)
    stacked = jnp.concatenate([own, other], axis=0)
    right = jnp.concatenate(
        [stacked, jnp.concatenate([own_sketch, other_sketch], axis=0)], axis=1
    )
    both = dot(stacked_t, stacked if last else right)
    if not last:
        crossed = dot(other_t, back)
    inverse = inverse_factor(both[:, :rank], square_sum(own) + square_sum(other))
    block_ref[...] = dot_nt(own, inverse)
    if last:
        pair_ref[...] = dot(inverse, stacked_t)
        return
    moved = dot(inverse, jnp.concatenate([both, own_t, crossed], axis=1))
    pair_ref[:rank, :] = moved[:, :rank]
    pair_ref[rank:, :] = moved[:, rank : 2 * rank]
    maps_ref[0] = moved[:, 2 * rank : 3 * rank]
    maps_ref[1] = moved[:, 3 * rank :]


def coupling_spec(couplings, tree_level):
    return pl.BlockSpec((1, 1) + couplings.shape[2:], lambda step: (0, tree_level, 0, 0))


def merge_step(tree_level, own, other, couplings, after):
    rank = own.shape[1]
    f32 = jnp.float32
    last = tree_level == LEVELS - 1
    return pl.pallas_call(
        functools.partial(merge_body, tree_level),
        grid=(1,),
        out_shape=[
            jax.ShapeDtypeStruct((rank, rank), f32),
            jax.ShapeDtypeStruct((8, rank) if last else (2, rank, rank), f32),
            jax.ShapeDtypeStruct((rank, 2 * rank) if last else (2 * rank, rank), f32),
        ],
        in_specs=[VMEM, VMEM, coupling_spec(couplings, tree_level)] + [ANY] * len(after),
        out_specs=[VMEM, ANY if last else VMEM, VMEM],
        compiler_params=small_params(),
        cost_estimate=small_cost(8),
        name=f"merge_orth_{tree_level}",
    )(own, other, couplings, *after)


def lower_body(*refs):
    keep_ref, first_ref, second_ref, leaf_sketch_ref, basis_t_ref = refs[:5]
    ways = (refs[-1].shape[1]) // refs[-2].shape[1]
    maps_refs = refs[5 : -1 - ways]
    out_refs = refs[-1 - ways : -1]
    wide = refs[-1]
    rank = basis_t_ref.shape[0]
    sample = keep_ref[...] + first_ref[...] + second_ref[...]
    sketch = leaf_sketch_ref[...].astype(jnp.float32)
    on_sample = basis_t_ref[...]
    on_sketch = jnp.zeros_like(on_sample)
    for maps_ref in maps_refs:
        lifted, crossed = maps_ref[0], maps_ref[1]
        on_sketch = dot(lifted, on_sketch) - dot(crossed, on_sample)
        on_sample = dot(lifted, on_sample)
    wide[:rank, :] = dot(on_sample, sample) + dot(on_sketch, sketch)
    wide[rank:, :] = dot(on_sample, sketch)
    me = lax.axis_index("col")
    part = wide.shape[1] // ways
    for away in range(ways):
        out_refs[away][...] = wide[:, pl.ds(pl.multiple_of((me ^ away) * part, part), part)]


def lower_step(keep, first, second, row_sketch, basis_t, maps):
    ways = lax.axis_size("col")
    leaf, width = row_sketch.shape
    rank = basis_t.shape[0]
    part = pl.BlockSpec((leaf, width), lambda step: (0, 0))
    return pl.pallas_call(
        lower_body,
        grid=(1,),
        out_shape=[jax.ShapeDtypeStruct((2 * rank, width // ways), jnp.float32)] * ways,
        in_specs=[part, part] + [VMEM] * (3 + len(maps)),
        out_specs=[VMEM] * ways,
        scratch_shapes=[pltpu.VMEM((2 * rank, width), jnp.float32)],
        compiler_params=small_params(),
        cost_estimate=small_cost(2),
        name="lower_maps",
    )(keep, first, second, row_sketch, basis_t, *maps)


def upper_body(*refs):
    maps_ref, out_ref = refs[-2:]
    total = refs[0][...]
    for ref in refs[1:-2]:
        total = total + ref[...]
    rank = maps_ref.shape[1]
    sample, sketch = total[:rank], total[rank:]
    lifted = maps_ref[0]
    out_ref[:rank, :] = dot(lifted, sample) - dot(maps_ref[1], sketch)
    out_ref[rank:, :] = dot(lifted, sketch)


def upper_step(tree_level, parts, maps):
    return pl.pallas_call(
        upper_body,
        out_shape=jax.ShapeDtypeStruct(parts[0].shape, jnp.float32),
        in_specs=[VMEM] * (len(parts) + 1),
        out_specs=VMEM,
        compiler_params=small_params(),
        cost_estimate=small_cost(1),
        name=f"upper_maps_{tree_level}",
    )(*parts, maps)


def top_body(own_ref, other_ref, coupling_ref, basis_t_ref, out_ref):
    rank = own_ref.shape[0] // 2
    ahead, back = turned(coupling_ref, LEVELS - 1)
    own = own_ref[:rank] - dot(ahead, other_ref[rank:])
    other = other_ref[:rank] - dot(back, own_ref[rank:])
    out_ref[...] = dot(basis_t_ref[...], jnp.concatenate([own, other], axis=0))


def top_step(own, other, couplings, basis_t):
    return pl.pallas_call(
        top_body,
        grid=(1,),
        out_shape=jax.ShapeDtypeStruct((own.shape[0] // 2, own.shape[1]), jnp.float32),
        in_specs=[VMEM, VMEM, coupling_spec(couplings, LEVELS - 1), VMEM],
        out_specs=VMEM,
        compiler_params=small_params(),
        cost_estimate=small_cost(1),
        name="top_sample",
    )(own, other, couplings, basis_t)


def columns_body(*refs):
    sems = refs[-1]
    out_ref = refs[-2]
    pieces = refs[:-2]
    ways = len(pieces)
    me = lax.axis_index("col")
    part = out_ref.shape[2] // ways
    copies = [
        pltpu.make_async_copy(
            pieces[away],
            out_ref.at[0, :, pl.ds(pl.multiple_of((me ^ away) * part, part), part)],
            sems.at[away],
        )
        for away in range(ways)
    ]
    for copy in copies:
        copy.start()
    for copy in copies:
        copy.wait()


def columns_step(pieces):
    rank, part = pieces[0].shape
    ways = len(pieces)
    return pl.pallas_call(
        columns_body,
        out_shape=jax.ShapeDtypeStruct((1, rank, part * ways), jnp.float32),
        in_specs=[VMEM] * ways,
        out_specs=ANY,
        scratch_shapes=[pltpu.SemaphoreType.DMA((ways,))],
        name="top_columns",
    )(*pieces)


def per_device(tiles, tile_slots, sketch, row_sketch, subsketch, couplings):
    ways = lax.axis_size("col")
    col_bits = ways.bit_length() - 1
    leaf = row_sketch.shape[0]
    keep, send = sample_rows(tiles, tile_slots, sketch, leaf)
    (send_red,) = reduce_step(subsketch, send)
    first_red = from_partner(send_red, "col", 1)
    keep_red, sketch_red = reduce_step(subsketch, keep, row_sketch)
    passed_red, send = lax.optimization_barrier((keep_red[leaf:] + first_red[leaf:], send))
    second_red = from_partner(passed_red, "col", 2)
    first = from_partner(send, "col", 1)
    passed, second_red = lax.optimization_barrier((keep[leaf:] + first[leaf:], second_red))
    second = from_partner(passed, "col", 2)
    leaf_basis, basis_t, pair = leaf_step(keep_red, first_red, second_red, sketch_red, passed)
    blocks, low_maps, after, parts = [], [], [], []
    for tree_level in range(LEVELS):
        if tree_level < LEVELS - 1:
            other = from_partner(pair, ROW_COL, 2**tree_level)
        else:
            other = waiting
        if tree_level == col_bits - 1:
            after = [second]
        block, maps, pair = merge_step(tree_level, pair, other, couplings, after)
        blocks.append(block)
        if tree_level == LEVELS - 1:
            break
        if tree_level < col_bits:
            low_maps.append(maps)
        else:
            mine = upper_step(tree_level, parts, maps)
            parts = [mine, from_partner(mine, ROW_COL, 2**tree_level)]
            after = [mine]
        if tree_level == col_bits - 1:
            cut = lower_step(keep, first, second, row_sketch, basis_t, low_maps)
            parts = [cut[0]] + [from_partner(cut[away], "col", away) for away in range(1, ways)]
            after = [cut[0]]
        if tree_level == LEVELS - 2:
            waiting = from_partner(pair, ROW_COL, 2 ** (LEVELS - 1))
            whole, waiting = lax.optimization_barrier((parts[0] + parts[1], waiting))
            far = from_partner(whole, ROW_COL, 2 ** (LEVELS - 1))
            after = [whole]
    top = top_step(whole, far, couplings, pair)
    pieces = [top] + [from_partner(top, "col", away) for away in range(1, ways)]
    transfer = jnp.stack(blocks, axis=0)[None]
    return (leaf_basis, transfer, columns_step(pieces))


def solution(mesh):
    return jax.shard_map(
        per_device,
        mesh=mesh,
        in_specs=(
            P(("row", "col"), None, None),
            P(("row", "col")),
            P("col", None),
            P(("row", "col"), None),
            P(),
            P(("row", "col"), None, None, None),
        ),
        out_specs=(
            P(("row", "col"), None),
            P(("row", "col"), None, None, None),
            P(("row", "col"), None, None),
        ),
        check_vma=False,
    )
```

```python
import functools
import math

import jax
import jax.numpy as jnp
from jax import lax
from jax.experimental import pallas as pl
from jax.experimental.pallas import tpu as pltpu
from jax.sharding import PartitionSpec as P

LEVELS = 5
ROW_COL = ("row", "col")
VMEM = pl.BlockSpec(memory_space=pltpu.VMEM)
ANY = pl.BlockSpec(memory_space=pl.ANY)
HBM = pl.BlockSpec(memory_space=pltpu.HBM)


def from_partner(block, axis, distance):
    count = lax.axis_size(axis)
    route = []
    for low in range(count):
        high = low ^ distance
        if high < count:
            route.append((low, high))
    return lax.ppermute(block, axis, route)


def dot(left, right):
    return jnp.dot(left, right, precision=lax.Precision.HIGHEST, preferred_element_type=jnp.float32)


def dot_nt(left, right):
    return lax.dot_general(
        left,
        right,
        (((1,), (1,)), ((), ())),
        precision=lax.Precision.HIGHEST,
        preferred_element_type=jnp.float32,
    )


def square_sum(block):
    squares = block * block
    return jnp.sum(jnp.sum(squares, axis=0, keepdims=True), axis=1, keepdims=True)


def inverse_factor(gram, trace):
    size = gram.shape[0]
    high = 8
    count = size // high
    square = (size, size)
    diag = lax.broadcasted_iota(jnp.int32, square, 1) == lax.broadcasted_iota(jnp.int32, square, 0)
    gram = jnp.where(diag, gram + (0.0001 * trace / size + 1e-06), gram)
    rows = [gram[high * g : high * g + high, :] for g in range(count)]
    shape = (high, size)
    lane = lax.broadcasted_iota(jnp.int32, shape, 1)
    sub = lax.broadcasted_iota(jnp.int32, shape, 0)

    def along_lanes(block, first):
        return [jnp.broadcast_to(block[:, first + k : first + k + 1], shape) for k in range(high)]

    def along_rows(block, at):
        return jnp.broadcast_to(block[at : at + 1, :], shape)

    found = []
    here = along_lanes(rows[0], 0)
    for b in range(count):
        first, after = b * high, (b + 1) * high
        more = b + 1 < count
        inside = (lane >= first) & (lane < after)
        full = jnp.where(inside, jnp.where(lane - first == sub, 1.0, 0.0), rows[b])
        done = jnp.zeros(shape, jnp.float32)
        steps = []
        if more:
            under = along_lanes(rows[b + 1], first)
            right = along_lanes(rows[b], after)
            corner = along_lanes(rows[b + 1], after)
            below_row = jnp.where(inside, 0.0, rows[b + 1])
        for i in range(high):
            root = lax.rsqrt(along_rows(here[i], i))
            inverse = root * root
            below = jnp.where(sub > i, here[i], 0.0)
            scaled = below * inverse
            entries = {k: along_rows(here[k], i) for k in range(i + 1, high)}
            for k, x in entries.items():
                here[k] = here[k] - ((below * x) * inverse if k < i + 3 else scaled * x)
            x = along_rows(full, i)
            done = jnp.where(sub == i, x * root, done)
            full = full - scaled * x
            if not more:
                continue
            steps.append(({k: entry * inverse for k, entry in entries.items()}, x * inverse))
            low = under[i] * inverse
            for k, entry in entries.items():
                under[k] = under[k] - low * entry
            for k in range(high):
                entry = along_rows(right[k], i)
                right[k] = right[k] - scaled * entry
                corner[k] = corner[k] - low * entry
            below_row = below_row - low * x
        found.append(jnp.where(lane < after, done, 0.0))
        if not more:
            break
        rows[b + 1] = below_row
        for g in range(b + 2, count):
            columns = along_lanes(rows[g], first)
            row = jnp.where(inside, 0.0, rows[g])
            for i, (entries, x) in enumerate(steps):
                for k, entry in entries.items():
                    columns[k] = columns[k] - columns[i] * entry
                row = row - columns[i] * x
            rows[g] = row
        here = corner
    return jnp.concatenate(found, axis=0)


def in_parts(block):
    high = block.astype(jnp.bfloat16)
    rest = block - high.astype(jnp.float32)
    middle = rest.astype(jnp.bfloat16)
    return high, middle, (rest - middle.astype(jnp.float32)).astype(jnp.bfloat16)


def short_dot(left, right):
    return jnp.dot(left, right, preferred_element_type=jnp.float32)


def quotient(value, divisor, below):
    shift = 20
    factor = -(-(2**shift) // divisor)
    assert all(v * factor >> shift == v // divisor for v in range(below))
    assert below * factor < 2**31
    return value * factor >> shift


def spmm_body(
    slots_ref,
    tiles_ref,
    sketch_ref,
    keep_ref,
    send_ref,
    dense,
    held,
    slots,
    tile_sem,
    sketch_sems,
    slots_sem,
    *,
    leaves,
):
    tile_count, tile_size, _ = tiles_ref.shape
    depth = sketch_ref.shape[0]
    rows = dense.shape[0]
    half = rows // 2
    col_tiles = depth // tile_size
    chunks = sketch_sems.shape[0]
    chunk = depth // chunks
    leaf_tiles = rows // leaves // tile_size
    me = lax.axis_index("col")
    slots_load = pltpu.make_async_copy(slots_ref, slots, slots_sem)
    loads = [
        pltpu.make_async_copy(
            sketch_ref.at[pl.ds(k * chunk, chunk)], held.at[pl.ds(k * chunk, chunk)], sketch_sems.at[k]
        )
        for k in range(chunks)
    ]
    for load in [slots_load] + loads:
        load.start()

    @pl.loop(0, rows // 64)
    def _(i):
        dense[pl.ds(pl.multiple_of(i * 64, 64), 64), :] = jnp.zeros((64, depth), dense.dtype)

    slots_load.wait()
    together = math.gcd(tile_count, 8)

    @pl.loop(0, tile_count // together)
    def _(group):
        for member in range(together):
            t = group * together + member
            slot = slots[t]
            row_tile = quotient(slot, col_tiles, rows // tile_size * col_tiles)
            column = slot - row_tile * col_tiles
            leaf = quotient(row_tile, leaf_tiles, rows // tile_size)
            away = leaf ^ me
            block = (away & 1) * (leaves // 2) + (away >> 1)
            row = pl.multiple_of((block * leaf_tiles + row_tile - leaf * leaf_tiles) * tile_size, tile_size)
            col = pl.multiple_of(column * tile_size, tile_size)
            pltpu.make_async_copy(
                tiles_ref.at[t], dense.at[pl.ds(row, tile_size), pl.ds(col, tile_size)], tile_sem
            ).start()

    pltpu.make_async_copy(tiles_ref, tiles_ref, tile_sem).wait()
    for k in range(chunks):
        loads[k].wait()
        for start, ref in ((half, send_ref), (0, keep_ref)):
            part = jnp.dot(
                dense[start : start + half, k * chunk : (k + 1) * chunk],
                held[k * chunk : (k + 1) * chunk, :],
                preferred_element_type=jnp.float32,
            )
            if k == 0:
                ref[...] = part
            else:
                ref[...] += part


def sample_rows(tiles, tile_slots, sketch, leaf):
    tile_size = tiles.shape[1]
    depth, width = sketch.shape
    leaves = lax.axis_size("col")
    rows = leaf * leaves
    half = rows // 2
    chunks = math.gcd(depth // tile_size, 4)
    return pl.pallas_call(
        functools.partial(spmm_body, leaves=leaves),
        out_shape=[jax.ShapeDtypeStruct((half, width), jnp.float32)] * 2,
        in_specs=[HBM] * 3,
        out_specs=[VMEM] * 2,
        scratch_shapes=[
            pltpu.VMEM((rows, depth), jnp.bfloat16),
            pltpu.VMEM((depth, width), jnp.bfloat16),
            pltpu.SMEM(tile_slots.shape, jnp.int32),
            pltpu.SemaphoreType.DMA,
            pltpu.SemaphoreType.DMA((chunks,)),
            pltpu.SemaphoreType.DMA,
        ],
        compiler_params=pltpu.CompilerParams(vmem_limit_bytes=48 * 2**20),
        cost_estimate=pl.CostEstimate(
            flops=2 * rows * depth * width,
            bytes_accessed=2 * (tiles.size + sketch.size) + 4 * rows * width,
            transcendentals=0,
        ),
        name="spmm",
    )(tile_slots, tiles, sketch)


def reduce_body(*refs):
    sub_ref, ref = refs[:2]
    outs = refs[len(refs) // 2 + 1 :]
    rank = sub_ref.shape[1]
    high, middle, low = in_parts(sub_ref[...])
    two = jnp.concatenate([high, middle], axis=1)
    first, second, third = in_parts(ref[...])
    wide = short_dot(second, two) + short_dot(first, two)
    rest = short_dot(third, high) + short_dot(first, low)
    outs[0][...] = wide[:, :rank] + (wide[:, rank:] + rest)
    if len(outs) > 1:
        exact = refs[2][...]
        wide = short_dot(exact, two)
        outs[1][...] = wide[:, :rank] + (wide[:, rank:] + short_dot(exact, low))


def reduce_step(subsketch, *blocks):
    rank = subsketch.shape[1]
    return pl.pallas_call(
        reduce_body,
        out_shape=[jax.ShapeDtypeStruct((block.shape[0], rank), jnp.float32) for block in blocks],
        in_specs=[VMEM] * (1 + len(blocks)),
        out_specs=[VMEM] * len(blocks),
        compiler_params=small_params(),
        cost_estimate=small_cost(1),
        name="reduced_" + str(len(blocks)),
    )(subsketch, *blocks)


def leaf_body(keep_ref, first_ref, second_ref, sketch_red_ref, _, basis_t_ref, pair_ref):
    rank = keep_ref.shape[-1]
    reduced = keep_ref[...] + first_ref[...] + second_ref[...]
    reduced_t = reduced.T
    both = dot(reduced_t, jnp.concatenate([reduced, sketch_red_ref[...]], axis=1))
    inverse = inverse_factor(both[:, :rank], square_sum(reduced))
    moved = dot(inverse, jnp.concatenate([both, reduced_t], axis=1))
    pair_ref[:rank, :] = moved[:, :rank]
    pair_ref[rank:, :] = moved[:, rank : 2 * rank]
    basis_t_ref[...] = moved[:, 2 * rank :]


def small_params():
    return pltpu.CompilerParams(vmem_limit_bytes=32 * 2**20)


def small_cost(micros):
    return pl.CostEstimate(flops=micros * 10**7, bytes_accessed=micros * 3 * 10**4, transcendentals=0)


def leaf_step(keep, first, second, sketch_red, after):
    leaf, rank = sketch_red.shape
    f32 = jnp.float32
    part = pl.BlockSpec((leaf, rank), lambda step: (0, 0))
    return pl.pallas_call(
        leaf_body,
        grid=(1,),
        out_shape=[
            jax.ShapeDtypeStruct((rank, leaf), f32),
            jax.ShapeDtypeStruct((2 * rank, rank), f32),
        ],
        in_specs=[part, part, VMEM, VMEM, ANY],
        out_specs=[VMEM] * 2,
        compiler_params=small_params(),
        cost_estimate=small_cost(8),
        name="leaf_orth",
    )(keep, first, second, sketch_red, after)


def basis_body(basis_t_ref, basis_ref, mark_ref):
    basis_ref[...] = basis_t_ref[...].T
    mark_ref[...] = jnp.zeros_like(mark_ref)


def basis_step(basis_t):
    return pl.pallas_call(
        basis_body,
        out_shape=[
            jax.ShapeDtypeStruct(basis_t.shape[::-1], jnp.float32),
            jax.ShapeDtypeStruct((8, 128), jnp.float32),
        ],
        in_specs=[VMEM],
        out_specs=[VMEM] * 2,
        compiler_params=small_params(),
        cost_estimate=small_cost(1),
        name="leaf_basis",
    )(basis_t)


def position():
    return lax.axis_index("row") * lax.axis_size("col") + lax.axis_index("col")


def turned(coupling_ref, tree_level):
    upper = position() // 2**tree_level % 2 == 1
    coupling = coupling_ref[0, 0].astype(jnp.float32)
    coupling_t = coupling.T
    return jnp.where(upper, coupling_t, coupling), jnp.where(upper, coupling, coupling_t)


def merge_body(tree_level, *refs):
    last = tree_level == LEVELS - 1
    coupling_ref, own_ref, other_ref = refs[:3]
    if tree_level == LEVELS - 2:
        block_ref, maps_ref, pair_ref, half_ref = refs[-4:]
    else:
        block_ref, maps_ref, pair_ref = refs[-3:]
    odd = position() % 2 == 1
    rank = own_ref.shape[-1]
    ahead, back = turned(coupling_ref, tree_level)
    own_sample, own_sketch = own_ref[:rank], own_ref[rank:]
    if last:
        other_sample = jnp.where(odd, refs[3][...], other_ref[...])
        other_sketch = jnp.where(odd, other_ref[...], refs[3][...])
    else:
        other_sample, other_sketch = other_ref[:rank], other_ref[rank:]
    own = own_sample - dot(ahead, other_sketch)
    other = other_sample - dot(back, own_sketch)
    own_t, other_t = own.T, other.T
    stacked_t = jnp.concatenate([own_t, other_t], axis=1)
    stacked = jnp.concatenate([own, other], axis=0)
    right = jnp.concatenate(
        [stacked, jnp.concatenate([own_sketch, other_sketch], axis=0)], axis=1
    )
    both = dot(stacked_t, stacked if last else right)
    if not last:
        crossed = dot(other_t, back)
    inverse = inverse_factor(both[:, :rank], square_sum(own) + square_sum(other))
    block_ref[...] = dot_nt(own, inverse)
    if last:
        pair_ref[...] = dot(inverse, stacked_t)
        return
    moved = dot(inverse, jnp.concatenate([both, own_t, crossed], axis=1))
    pair_ref[:rank, :] = moved[:, :rank]
    pair_ref[rank:, :] = moved[:, rank : 2 * rank]
    if tree_level == LEVELS - 2:
        half_ref[...] = jnp.where(odd, moved[:, rank : 2 * rank], moved[:, :rank])
    maps_ref[0] = moved[:, 2 * rank : 3 * rank]
    maps_ref[1] = moved[:, 3 * rank :]


def coupling_spec(couplings, tree_level):
    return pl.BlockSpec((1, 1) + couplings.shape[2:], lambda step: (0, tree_level, 0, 0))


def merge_step(tree_level, own, others, couplings, after):
    rank = own.shape[1]
    f32 = jnp.float32
    last = tree_level == LEVELS - 1
    split = tree_level == LEVELS - 2
    return pl.pallas_call(
        functools.partial(merge_body, tree_level),
        grid=(1,),
        out_shape=[
            jax.ShapeDtypeStruct((rank, rank), f32),
            jax.ShapeDtypeStruct((8, rank) if last else (2, rank, rank), f32),
            jax.ShapeDtypeStruct((rank, 2 * rank) if last else (2 * rank, rank), f32),
        ]
        + [jax.ShapeDtypeStruct((rank, rank), f32)] * split,
        in_specs=[coupling_spec(couplings, tree_level)] + [VMEM] * (1 + len(others)) + [ANY] * len(after),
        out_specs=[VMEM, ANY if last else VMEM, VMEM] + [VMEM] * split,
        compiler_params=small_params(),
        cost_estimate=small_cost(8),
        name=f"merge_orth_{tree_level}",
    )(couplings, own, *others, *after)


def lower_body(*refs):
    keep_ref, first_ref, second_ref, leaf_sketch_ref, basis_t_ref = refs[:5]
    ways = (refs[-1].shape[1]) // refs[-2].shape[1]
    maps_refs = refs[5 : -1 - ways]
    out_refs = refs[-1 - ways : -1]
    wide = refs[-1]
    rank = basis_t_ref.shape[0]
    sample = keep_ref[...] + first_ref[...] + second_ref[...]
    sketch = leaf_sketch_ref[...].astype(jnp.float32)
    on_sample = basis_t_ref[...]
    on_sketch = jnp.zeros_like(on_sample)
    for maps_ref in maps_refs:
        lifted, crossed = maps_ref[0], maps_ref[1]
        on_sketch = dot(lifted, on_sketch) - dot(crossed, on_sample)
        on_sample = dot(lifted, on_sample)
    wide[:rank, :] = dot(on_sample, sample) + dot(on_sketch, sketch)
    wide[rank:, :] = dot(on_sample, sketch)
    me = lax.axis_index("col")
    part = wide.shape[1] // ways
    for away in range(ways):
        out_refs[away][...] = wide[:, pl.ds(pl.multiple_of((me ^ away) * part, part), part)]


def lower_step(keep, first, second, row_sketch, basis_t, maps):
    ways = lax.axis_size("col")
    leaf, width = row_sketch.shape
    rank = basis_t.shape[0]
    part = pl.BlockSpec((leaf, width), lambda step: (0, 0))
    return pl.pallas_call(
        lower_body,
        grid=(1,),
        out_shape=[jax.ShapeDtypeStruct((2 * rank, width // ways), jnp.float32)] * ways,
        in_specs=[part, part] + [VMEM] * (3 + len(maps)),
        out_specs=[VMEM] * ways,
        scratch_shapes=[pltpu.VMEM((2 * rank, width), jnp.float32)],
        compiler_params=small_params(),
        cost_estimate=small_cost(2),
        name="lower_maps",
    )(keep, first, second, row_sketch, basis_t, *maps)


def upper_body(*refs):
    maps_ref, out_ref = refs[-2:]
    total = refs[0][...]
    for ref in refs[1:-2]:
        total = total + ref[...]
    rank = maps_ref.shape[1]
    sample, sketch = total[:rank], total[rank:]
    lifted = maps_ref[0]
    out_ref[:rank, :] = dot(lifted, sample) - dot(maps_ref[1], sketch)
    out_ref[rank:, :] = dot(lifted, sketch)


def upper_step(tree_level, parts, maps):
    return pl.pallas_call(
        upper_body,
        out_shape=jax.ShapeDtypeStruct(parts[0].shape, jnp.float32),
        in_specs=[VMEM] * (len(parts) + 1),
        out_specs=VMEM,
        compiler_params=small_params(),
        cost_estimate=small_cost(200),
        name=f"upper_maps_{tree_level}",
    )(*parts, maps)


def top_body(own_ref, other_ref, coupling_ref, basis_t_ref, out_ref):
    rank = own_ref.shape[0] // 2
    ahead, back = turned(coupling_ref, LEVELS - 1)
    own = own_ref[:rank] - dot(ahead, other_ref[rank:])
    other = other_ref[:rank] - dot(back, own_ref[rank:])
    out_ref[...] = dot(basis_t_ref[...], jnp.concatenate([own, other], axis=0))


def top_step(own, other, couplings, basis_t):
    return pl.pallas_call(
        top_body,
        grid=(1,),
        out_shape=jax.ShapeDtypeStruct((own.shape[0] // 2, own.shape[1]), jnp.float32),
        in_specs=[VMEM, VMEM, coupling_spec(couplings, LEVELS - 1), VMEM],
        out_specs=VMEM,
        compiler_params=small_params(),
        cost_estimate=small_cost(1),
        name="top_sample",
    )(own, other, couplings, basis_t)


def columns_body(*refs):
    sems = refs[-1]
    out_ref = refs[-2]
    pieces = refs[:-2]
    ways = len(pieces)
    me = lax.axis_index("col")
    part = out_ref.shape[2] // ways
    copies = [
        pltpu.make_async_copy(
            pieces[away],
            out_ref.at[0, :, pl.ds(pl.multiple_of((me ^ away) * part, part), part)],
            sems.at[away],
        )
        for away in range(ways)
    ]
    for copy in copies:
        copy.start()
    for copy in copies:
        copy.wait()


def columns_step(pieces):
    rank, part = pieces[0].shape
    ways = len(pieces)
    return pl.pallas_call(
        columns_body,
        out_shape=jax.ShapeDtypeStruct((1, rank, part * ways), jnp.float32),
        in_specs=[VMEM] * ways,
        out_specs=ANY,
        scratch_shapes=[pltpu.SemaphoreType.DMA((ways,))],
        compiler_params=small_params(),
        name="top_columns",
    )(*pieces)


def per_device(tiles, tile_slots, sketch, row_sketch, subsketch, couplings):
    ways = lax.axis_size("col")
    col_bits = ways.bit_length() - 1
    leaf = row_sketch.shape[0]
    keep, send = sample_rows(tiles, tile_slots, sketch, leaf)
    (send_red,) = reduce_step(subsketch, send)
    first_red = from_partner(send_red, "col", 1)
    keep_red, sketch_red = reduce_step(subsketch, keep, row_sketch)
    passed_red, send = lax.optimization_barrier((keep_red[leaf:] + first_red[leaf:], send))
    second_red = from_partner(passed_red, "col", 2)
    first = from_partner(send, "col", 1)
    passed, second_red = lax.optimization_barrier((keep[leaf:] + first[leaf:], second_red))
    second = from_partner(passed, "col", 2)
    basis_t, pair = leaf_step(keep_red, first_red, second_red, sketch_red, passed)
    blocks, low_maps, after, parts = [], [], [], []
    for tree_level in range(LEVELS):
        if tree_level < LEVELS - 1:
            others = [from_partner(pair, ROW_COL, 2**tree_level)]
        else:
            others = [waiting, from_partner(waiting, ROW_COL, 1)]
        if tree_level == col_bits - 1:
            leaf_basis, mark = basis_step(basis_t)
            after = [second, mark]
        block, maps, pair, *half = merge_step(tree_level, pair, others, couplings, after)
        blocks.append(block)
        if tree_level == LEVELS - 1:
            break
        if tree_level < col_bits:
            low_maps.append(maps)
        else:
            mine = upper_step(tree_level, parts, maps)
            parts = [mine, from_partner(mine, ROW_COL, 2**tree_level)]
            after = [mine]
        if tree_level == col_bits - 1:
            cut = lower_step(keep, first, second, row_sketch, basis_t, low_maps)
            parts = [cut[0]] + [from_partner(cut[away], "col", away) for away in range(1, ways)]
            after = [cut[0]]
        if tree_level == LEVELS - 2:
            waiting = from_partner(half[0], ROW_COL, 2 ** (LEVELS - 1))
            whole, waiting = lax.optimization_barrier((parts[0] + parts[1], waiting))
            far = from_partner(whole, ROW_COL, 2 ** (LEVELS - 1))
            after = [whole]
    top = top_step(whole, far, couplings, pair)
    pieces = [top] + [from_partner(top, "col", away) for away in range(1, ways)]
    transfer = jnp.stack(blocks, axis=0)[None]
    return (leaf_basis, transfer, columns_step(pieces))


def solution(mesh):
    return jax.shard_map(
        per_device,
        mesh=mesh,
        in_specs=(
            P(("row", "col"), None, None),
            P(("row", "col")),
            P("col", None),
            P(("row", "col"), None),
            P(),
            P(("row", "col"), None, None, None),
        ),
        out_specs=(
            P(("row", "col"), None),
            P(("row", "col"), None, None, None),
            P(("row", "col"), None, None),
        ),
        check_vma=False,
    )
```

```python
import functools
import math

import jax
import jax.numpy as jnp
from jax import lax
from jax.experimental import pallas as pl
from jax.experimental.pallas import tpu as pltpu
from jax.sharding import PartitionSpec as P

LEVELS = 5
ROW_COL = ("row", "col")
VMEM = pl.BlockSpec(memory_space=pltpu.VMEM)
ANY = pl.BlockSpec(memory_space=pl.ANY)
HBM = pl.BlockSpec(memory_space=pltpu.HBM)


def from_partner(block, axis, distance):
    count = lax.axis_size(axis)
    route = []
    for low in range(count):
        high = low ^ distance
        if high < count:
            route.append((low, high))
    return lax.ppermute(block, axis, route)


def dot(left, right):
    return jnp.dot(left, right, precision=lax.Precision.HIGHEST, preferred_element_type=jnp.float32)


def dot_nt(left, right):
    return lax.dot_general(
        left,
        right,
        (((1,), (1,)), ((), ())),
        precision=lax.Precision.HIGHEST,
        preferred_element_type=jnp.float32,
    )


def square_sum(block):
    squares = block * block
    return jnp.sum(jnp.sum(squares, axis=0, keepdims=True), axis=1, keepdims=True)


def inverse_factor(gram, trace):
    size = gram.shape[0]
    high = 8
    count = size // high
    square = (size, size)
    diag = lax.broadcasted_iota(jnp.int32, square, 1) == lax.broadcasted_iota(jnp.int32, square, 0)
    gram = jnp.where(diag, gram + (0.0001 * trace / size + 1e-06), gram)
    rows = [gram[high * g : high * g + high, :] for g in range(count)]
    shape = (high, size)
    lane = lax.broadcasted_iota(jnp.int32, shape, 1)
    sub = lax.broadcasted_iota(jnp.int32, shape, 0)

    def along_lanes(block, first):
        return [jnp.broadcast_to(block[:, first + k : first + k + 1], shape) for k in range(high)]

    def along_rows(block, at):
        return jnp.broadcast_to(block[at : at + 1, :], shape)

    found = []
    here = along_lanes(rows[0], 0)
    for b in range(count):
        first, after = b * high, (b + 1) * high
        more = b + 1 < count
        inside = (lane >= first) & (lane < after)
        full = jnp.where(inside, jnp.where(lane - first == sub, 1.0, 0.0), rows[b])
        done = jnp.zeros(shape, jnp.float32)
        steps = []
        if more:
            under = along_lanes(rows[b + 1], first)
            right = along_lanes(rows[b], after)
            corner = along_lanes(rows[b + 1], after)
            below_row = jnp.where(inside, 0.0, rows[b + 1])
        for i in range(high):
            root = lax.rsqrt(along_rows(here[i], i))
            inverse = root * root
            below = jnp.where(sub > i, here[i], 0.0)
            scaled = below * inverse
            entries = {k: along_rows(here[k], i) for k in range(i + 1, high)}
            for k, x in entries.items():
                here[k] = here[k] - ((below * x) * inverse if k < i + 3 else scaled * x)
            x = along_rows(full, i)
            done = jnp.where(sub == i, x * root, done)
            full = full - scaled * x
            if not more:
                continue
            steps.append(({k: entry * inverse for k, entry in entries.items()}, x * inverse))
            low = under[i] * inverse
            for k, entry in entries.items():
                under[k] = under[k] - low * entry
            for k in range(high):
                entry = along_rows(right[k], i)
                right[k] = right[k] - scaled * entry
                corner[k] = corner[k] - low * entry
            below_row = below_row - low * x
        found.append(jnp.where(lane < after, done, 0.0))
        if not more:
            break
        rows[b + 1] = below_row
        for g in range(b + 2, count):
            columns = along_lanes(rows[g], first)
            row = jnp.where(inside, 0.0, rows[g])
            for i, (entries, x) in enumerate(steps):
                for k, entry in entries.items():
                    columns[k] = columns[k] - columns[i] * entry
                row = row - columns[i] * x
            rows[g] = row
        here = corner
    return jnp.concatenate(found, axis=0)


def in_parts(block):
    high = block.astype(jnp.bfloat16)
    rest = block - high.astype(jnp.float32)
    middle = rest.astype(jnp.bfloat16)
    return high, middle, (rest - middle.astype(jnp.float32)).astype(jnp.bfloat16)


def short_dot(left, right):
    return jnp.dot(left, right, preferred_element_type=jnp.float32)


def quotient(value, divisor, below):
    shift = 20
    factor = -(-(2**shift) // divisor)
    assert all(v * factor >> shift == v // divisor for v in range(below))
    assert below * factor < 2**31
    return value * factor >> shift


def spmm_body(
    slots_ref,
    tiles_ref,
    sketch_ref,
    keep_ref,
    send_ref,
    dense,
    held,
    slots,
    tile_sem,
    sketch_sems,
    slots_sem,
    *,
    leaves,
):
    tile_count, tile_size, _ = tiles_ref.shape
    depth = sketch_ref.shape[0]
    rows = dense.shape[0]
    half = rows // 2
    col_tiles = depth // tile_size
    chunks = sketch_sems.shape[0]
    chunk = depth // chunks
    leaf_tiles = rows // leaves // tile_size
    me = lax.axis_index("col")
    slots_load = pltpu.make_async_copy(slots_ref, slots, slots_sem)
    loads = [
        pltpu.make_async_copy(
            sketch_ref.at[pl.ds(k * chunk, chunk)], held.at[pl.ds(k * chunk, chunk)], sketch_sems.at[k]
        )
        for k in range(chunks)
    ]
    for load in [slots_load] + loads:
        load.start()

    @pl.loop(0, rows // 64)
    def _(i):
        dense[pl.ds(pl.multiple_of(i * 64, 64), 64), :] = jnp.zeros((64, depth), dense.dtype)

    slots_load.wait()
    together = math.gcd(tile_count, 8)

    @pl.loop(0, tile_count // together)
    def _(group):
        for member in range(together):
            t = group * together + member
            slot = slots[t]
            row_tile = quotient(slot, col_tiles, rows // tile_size * col_tiles)
            column = slot - row_tile * col_tiles
            leaf = quotient(row_tile, leaf_tiles, rows // tile_size)
            away = leaf ^ me
            block = (away & 1) * (leaves // 2) + (away >> 1)
            row = pl.multiple_of((block * leaf_tiles + row_tile - leaf * leaf_tiles) * tile_size, tile_size)
            col = pl.multiple_of(column * tile_size, tile_size)
            pltpu.make_async_copy(
                tiles_ref.at[t], dense.at[pl.ds(row, tile_size), pl.ds(col, tile_size)], tile_sem
            ).start()

    pltpu.make_async_copy(tiles_ref, tiles_ref, tile_sem).wait()
    for k in range(chunks):
        loads[k].wait()
        for start, ref in ((half, send_ref), (0, keep_ref)):
            part = jnp.dot(
                dense[start : start + half, k * chunk : (k + 1) * chunk],
                held[k * chunk : (k + 1) * chunk, :],
                preferred_element_type=jnp.float32,
            )
            if k == 0:
                ref[...] = part
            else:
                ref[...] += part


def sample_rows(tiles, tile_slots, sketch, leaf):
    tile_size = tiles.shape[1]
    depth, width = sketch.shape
    leaves = lax.axis_size("col")
    rows = leaf * leaves
    half = rows // 2
    chunks = math.gcd(depth // tile_size, 4)
    return pl.pallas_call(
        functools.partial(spmm_body, leaves=leaves),
        out_shape=[jax.ShapeDtypeStruct((half, width), jnp.float32)] * 2,
        in_specs=[HBM] * 3,
        out_specs=[VMEM] * 2,
        scratch_shapes=[
            pltpu.VMEM((rows, depth), jnp.bfloat16),
            pltpu.VMEM((depth, width), jnp.bfloat16),
            pltpu.SMEM(tile_slots.shape, jnp.int32),
            pltpu.SemaphoreType.DMA,
            pltpu.SemaphoreType.DMA((chunks,)),
            pltpu.SemaphoreType.DMA,
        ],
        compiler_params=pltpu.CompilerParams(vmem_limit_bytes=48 * 2**20),
        cost_estimate=pl.CostEstimate(
            flops=2 * rows * depth * width,
            bytes_accessed=2 * (tiles.size + sketch.size) + 4 * rows * width,
            transcendentals=0,
        ),
        name="spmm",
    )(tile_slots, tiles, sketch)


def reduce_body(*refs):
    sub_ref, ref = refs[:2]
    outs = refs[len(refs) // 2 + 1 :]
    rank = sub_ref.shape[1]
    high, middle, low = in_parts(sub_ref[...])
    two = jnp.concatenate([high, middle], axis=1)
    first, second, third = in_parts(ref[...])
    wide = short_dot(second, two) + short_dot(first, two)
    rest = short_dot(third, high) + short_dot(first, low)
    outs[0][...] = wide[:, :rank] + (wide[:, rank:] + rest)
    if len(outs) > 1:
        exact = refs[2][...]
        wide = short_dot(exact, two)
        outs[1][...] = wide[:, :rank] + (wide[:, rank:] + short_dot(exact, low))


def reduce_step(subsketch, *blocks):
    rank = subsketch.shape[1]
    return pl.pallas_call(
        reduce_body,
        out_shape=[jax.ShapeDtypeStruct((block.shape[0], rank), jnp.float32) for block in blocks],
        in_specs=[VMEM] * (1 + len(blocks)),
        out_specs=[VMEM] * len(blocks),
        compiler_params=small_params(),
        cost_estimate=small_cost(1),
        name="reduced_" + str(len(blocks)),
    )(subsketch, *blocks)


def leaf_body(keep_ref, first_ref, second_ref, sketch_red_ref, _, basis_t_ref, pair_ref):
    rank = keep_ref.shape[-1]
    reduced = keep_ref[...] + first_ref[...] + second_ref[...]
    reduced_t = reduced.T
    both = dot(reduced_t, jnp.concatenate([reduced, sketch_red_ref[...]], axis=1))
    inverse = inverse_factor(both[:, :rank], square_sum(reduced))
    moved = dot(inverse, jnp.concatenate([both, reduced_t], axis=1))
    pair_ref[:rank, :] = moved[:, :rank]
    pair_ref[rank:, :] = moved[:, rank : 2 * rank]
    basis_t_ref[...] = moved[:, 2 * rank :]


def small_params():
    return pltpu.CompilerParams(vmem_limit_bytes=32 * 2**20)


def small_cost(micros):
    return pl.CostEstimate(flops=micros * 10**7, bytes_accessed=micros * 3 * 10**4, transcendentals=0)


def leaf_step(keep, first, second, sketch_red, after):
    leaf, rank = sketch_red.shape
    f32 = jnp.float32
    part = pl.BlockSpec((leaf, rank), lambda step: (0, 0))
    return pl.pallas_call(
        leaf_body,
        grid=(1,),
        out_shape=[
            jax.ShapeDtypeStruct((rank, leaf), f32),
            jax.ShapeDtypeStruct((2 * rank, rank), f32),
        ],
        in_specs=[part, part, VMEM, VMEM, ANY],
        out_specs=[VMEM] * 2,
        compiler_params=small_params(),
        cost_estimate=small_cost(8),
        name="leaf_orth",
    )(keep, first, second, sketch_red, after)


def basis_body(basis_t_ref, basis_ref, mark_ref):
    basis_ref[...] = basis_t_ref[...].T
    mark_ref[...] = jnp.zeros_like(mark_ref)


def basis_step(basis_t):
    return pl.pallas_call(
        basis_body,
        out_shape=[
            jax.ShapeDtypeStruct(basis_t.shape[::-1], jnp.float32),
            jax.ShapeDtypeStruct((8, 128), jnp.float32),
        ],
        in_specs=[VMEM],
        out_specs=[VMEM] * 2,
        compiler_params=small_params(),
        cost_estimate=small_cost(1),
        name="leaf_basis",
    )(basis_t)


def position():
    return lax.axis_index("row") * lax.axis_size("col") + lax.axis_index("col")


def turned(coupling_ref, tree_level):
    upper = position() // 2**tree_level % 2 == 1
    coupling = coupling_ref[0, 0].astype(jnp.float32)
    coupling_t = coupling.T
    return jnp.where(upper, coupling_t, coupling), jnp.where(upper, coupling, coupling_t)


def merge_body(tree_level, *refs):
    last = tree_level == LEVELS - 1
    coupling_ref, own_ref, other_ref = refs[:3]
    if tree_level == LEVELS - 2:
        block_ref, maps_ref, pair_ref, half_ref = refs[-4:]
    else:
        block_ref, maps_ref, pair_ref = refs[-3:]
    odd = position() % 2 == 1
    rank = own_ref.shape[-1]
    ahead, back = turned(coupling_ref, tree_level)
    own_sample, own_sketch = own_ref[:rank], own_ref[rank:]
    if last:
        other_sample = jnp.where(odd, refs[3][...], other_ref[...])
        other_sketch = jnp.where(odd, other_ref[...], refs[3][...])
    else:
        other_sample, other_sketch = other_ref[:rank], other_ref[rank:]
    own = own_sample - dot(ahead, other_sketch)
    other = other_sample - dot(back, own_sketch)
    own_t, other_t = own.T, other.T
    stacked_t = jnp.concatenate([own_t, other_t], axis=1)
    stacked = jnp.concatenate([own, other], axis=0)
    right = jnp.concatenate(
        [stacked, jnp.concatenate([own_sketch, other_sketch], axis=0)], axis=1
    )
    both = dot(stacked_t, stacked if last else right)
    if not last:
        sides = [own_t, dot(other_t, back)]
        if maps_ref.shape[0] == 4:
            sides += [other_t, dot(own_t, ahead)]
    inverse = inverse_factor(both[:, :rank], square_sum(own) + square_sum(other))
    block_ref[...] = dot_nt(own, inverse)
    if last:
        pair_ref[...] = dot(inverse, stacked_t)
        return
    moved = dot(inverse, jnp.concatenate([both] + sides, axis=1))
    pair_ref[:rank, :] = moved[:, :rank]
    pair_ref[rank:, :] = moved[:, rank : 2 * rank]
    if tree_level == LEVELS - 2:
        half_ref[...] = jnp.where(odd, moved[:, rank : 2 * rank], moved[:, :rank])
    for side in range(len(sides)):
        maps_ref[side] = moved[:, (2 + side) * rank : (3 + side) * rank]


def coupling_spec(couplings, tree_level):
    return pl.BlockSpec((1, 1) + couplings.shape[2:], lambda step: (0, tree_level, 0, 0))


def merge_step(tree_level, own, others, couplings, sides, after):
    rank = own.shape[1]
    f32 = jnp.float32
    last = tree_level == LEVELS - 1
    split = tree_level == LEVELS - 2
    return pl.pallas_call(
        functools.partial(merge_body, tree_level),
        grid=(1,),
        out_shape=[
            jax.ShapeDtypeStruct((rank, rank), f32),
            jax.ShapeDtypeStruct((8, rank) if last else (2 * sides, rank, rank), f32),
            jax.ShapeDtypeStruct((rank, 2 * rank) if last else (2 * rank, rank), f32),
        ]
        + [jax.ShapeDtypeStruct((rank, rank), f32)] * split,
        in_specs=[coupling_spec(couplings, tree_level)] + [VMEM] * (1 + len(others)) + [ANY] * len(after),
        out_specs=[VMEM, ANY if last else VMEM, VMEM] + [VMEM] * split,
        compiler_params=small_params(),
        cost_estimate=small_cost(8),
        name=f"merge_orth_{tree_level}",
    )(couplings, own, *others, *after)


def lower_body(*refs):
    keep_ref, first_ref, second_ref, leaf_sketch_ref, basis_t_ref = refs[:5]
    ways = (refs[-1].shape[1]) // refs[-2].shape[1]
    maps_refs = refs[5 : -1 - ways]
    out_refs = refs[-1 - ways : -1]
    wide = refs[-1]
    rank = basis_t_ref.shape[0]
    sample = keep_ref[...] + first_ref[...] + second_ref[...]
    sketch = leaf_sketch_ref[...].astype(jnp.float32)
    on_sample = basis_t_ref[...]
    on_sketch = jnp.zeros_like(on_sample)
    for maps_ref in maps_refs:
        lifted, crossed = maps_ref[0], maps_ref[1]
        on_sketch = dot(lifted, on_sketch) - dot(crossed, on_sample)
        on_sample = dot(lifted, on_sample)
    wide[:rank, :] = dot(on_sample, sample) + dot(on_sketch, sketch)
    wide[rank:, :] = dot(on_sample, sketch)
    me = lax.axis_index("col")
    part = wide.shape[1] // ways
    for away in range(ways):
        out_refs[away][...] = wide[:, pl.ds(pl.multiple_of((me ^ away) * part, part), part)]


def lower_step(keep, first, second, row_sketch, basis_t, maps):
    ways = lax.axis_size("col")
    leaf, width = row_sketch.shape
    rank = basis_t.shape[0]
    part = pl.BlockSpec((leaf, width), lambda step: (0, 0))
    return pl.pallas_call(
        lower_body,
        grid=(1,),
        out_shape=[jax.ShapeDtypeStruct((2 * rank, width // ways), jnp.float32)] * ways,
        in_specs=[part, part] + [VMEM] * (3 + len(maps)),
        out_specs=[VMEM] * ways,
        scratch_shapes=[pltpu.VMEM((2 * rank, width), jnp.float32)],
        compiler_params=small_params(),
        cost_estimate=small_cost(2),
        name="lower_maps",
    )(keep, first, second, row_sketch, basis_t, *maps)


def upper_body(count, *refs):
    maps_ref, out_ref = refs[-2:]

    def total(parts):
        added = parts[0][...]
        for ref in parts[1:]:
            added = added + ref[...]
        return added

    rank = maps_ref.shape[1]
    own, other = total(refs[:count]), total(refs[count:-2])
    nodes = jnp.concatenate([own, other], axis=0)
    sketches = jnp.concatenate([own[rank:], other[rank:]], axis=0)
    lifts = jnp.concatenate([maps_ref[0], maps_ref[2]], axis=1)
    signed = jnp.concatenate([maps_ref[0], -maps_ref[1], maps_ref[2], -maps_ref[3]], axis=1)
    out_ref[:rank, :] = dot(signed, nodes)
    out_ref[rank:, :] = dot(lifts, sketches)


def upper_step(tree_level, own, other, maps):
    return pl.pallas_call(
        functools.partial(upper_body, len(own)),
        out_shape=jax.ShapeDtypeStruct(own[0].shape, jnp.float32),
        in_specs=[VMEM] * (len(own) + len(other) + 1),
        out_specs=VMEM,
        compiler_params=small_params(),
        cost_estimate=small_cost(1),
        name=f"upper_maps_{tree_level}",
    )(*own, *other, maps)


def top_body(own_ref, other_ref, coupling_ref, basis_t_ref, out_ref):
    rank = own_ref.shape[0] // 2
    ahead, back = turned(coupling_ref, LEVELS - 1)
    own = own_ref[:rank] - dot(ahead, other_ref[rank:])
    other = other_ref[:rank] - dot(back, own_ref[rank:])
    out_ref[...] = dot(basis_t_ref[...], jnp.concatenate([own, other], axis=0))


def top_step(own, other, couplings, basis_t):
    return pl.pallas_call(
        top_body,
        grid=(1,),
        out_shape=jax.ShapeDtypeStruct((own.shape[0] // 2, own.shape[1]), jnp.float32),
        in_specs=[VMEM, VMEM, coupling_spec(couplings, LEVELS - 1), VMEM],
        out_specs=VMEM,
        compiler_params=small_params(),
        cost_estimate=small_cost(1),
        name="top_sample",
    )(own, other, couplings, basis_t)


def columns_body(*refs):
    sems = refs[-1]
    out_ref = refs[-2]
    pieces = refs[:-2]
    ways = len(pieces)
    me = lax.axis_index("col")
    part = out_ref.shape[2] // ways
    copies = [
        pltpu.make_async_copy(
            pieces[away],
            out_ref.at[0, :, pl.ds(pl.multiple_of((me ^ away) * part, part), part)],
            sems.at[away],
        )
        for away in range(ways)
    ]
    for copy in copies:
        copy.start()
    for copy in copies:
        copy.wait()


def columns_step(pieces):
    rank, part = pieces[0].shape
    ways = len(pieces)
    return pl.pallas_call(
        columns_body,
        out_shape=jax.ShapeDtypeStruct((1, rank, part * ways), jnp.float32),
        in_specs=[VMEM] * ways,
        out_specs=ANY,
        scratch_shapes=[pltpu.SemaphoreType.DMA((ways,))],
        compiler_params=small_params(),
        name="top_columns",
    )(*pieces)


def per_device(tiles, tile_slots, sketch, row_sketch, subsketch, couplings):
    ways = lax.axis_size("col")
    col_bits = ways.bit_length() - 1
    leaf = row_sketch.shape[0]
    keep, send = sample_rows(tiles, tile_slots, sketch, leaf)
    (send_red,) = reduce_step(subsketch, send)
    first_red = from_partner(send_red, "col", 1)
    keep_red, sketch_red = reduce_step(subsketch, keep, row_sketch)
    passed_red, send = lax.optimization_barrier((keep_red[leaf:] + first_red[leaf:], send))
    second_red = from_partner(passed_red, "col", 2)
    first = from_partner(send, "col", 1)
    passed, second_red = lax.optimization_barrier((keep[leaf:] + first[leaf:], second_red))
    second = from_partner(passed, "col", 2)
    basis_t, pair = leaf_step(keep_red, first_red, second_red, sketch_red, passed)
    blocks, low_maps, after = [], [], []
    for tree_level in range(LEVELS):
        if tree_level < LEVELS - 1:
            others = [from_partner(pair, ROW_COL, 2**tree_level)]
        else:
            others = [waiting, from_partner(waiting, ROW_COL, 1)]
        if tree_level == 1:
            leaf_basis, mark = basis_step(basis_t)
            after = after + [mark]
        sides = 1 if tree_level < col_bits - 1 else 2
        block, maps, pair, *half = merge_step(tree_level, pair, others, couplings, sides, after)
        blocks.append(block)
        if tree_level == LEVELS - 1:
            break
        if tree_level == LEVELS - 2:
            waiting = from_partner(half[0], ROW_COL, 2 ** (LEVELS - 1))
        if tree_level < col_bits - 1:
            low_maps.append(maps)
        else:
            total = upper_step(tree_level, own, other, maps)
            own = [total]
            other = [from_partner(total, ROW_COL, 2 ** (tree_level + 1))]
            after = [total]
        if tree_level == col_bits - 2:
            cut = lower_step(keep, first, second, row_sketch, basis_t, low_maps)
            cut = [cut[0]] + [from_partner(cut[away], "col", away) for away in range(1, ways)]
            own, other = cut[: ways // 2], cut[ways // 2 :]
            after = [cut[0]]
    top = top_step(own[0], other[0], couplings, pair)
    pieces = [top] + [from_partner(top, "col", away) for away in range(1, ways)]
    transfer = jnp.stack(blocks, axis=0)[None]
    return (leaf_basis, transfer, columns_step(pieces))


def solution(mesh):
    return jax.shard_map(
        per_device,
        mesh=mesh,
        in_specs=(
            P(("row", "col"), None, None),
            P(("row", "col")),
            P("col", None),
            P(("row", "col"), None),
            P(),
            P(("row", "col"), None, None, None),
        ),
        out_specs=(
            P(("row", "col"), None),
            P(("row", "col"), None, None, None),
            P(("row", "col"), None, None),
        ),
        check_vma=False,
    )
```

```python
import functools
import math

import jax
import jax.numpy as jnp
from jax import lax
from jax.experimental import pallas as pl
from jax.experimental.pallas import tpu as pltpu
from jax.sharding import PartitionSpec as P

LEVELS = 5
ROW_COL = ("row", "col")
VMEM = pl.BlockSpec(memory_space=pltpu.VMEM)
ANY = pl.BlockSpec(memory_space=pl.ANY)
HBM = pl.BlockSpec(memory_space=pltpu.HBM)


def from_partner(block, axis, distance):
    count = lax.axis_size(axis)
    route = []
    for low in range(count):
        high = low ^ distance
        if high < count:
            route.append((low, high))
    return lax.ppermute(block, axis, route)


def dot(left, right):
    return jnp.dot(left, right, precision=lax.Precision.HIGHEST, preferred_element_type=jnp.float32)


def dot_nt(left, right):
    return lax.dot_general(
        left,
        right,
        (((1,), (1,)), ((), ())),
        precision=lax.Precision.HIGHEST,
        preferred_element_type=jnp.float32,
    )


def square_sum(block):
    squares = block * block
    return jnp.sum(jnp.sum(squares, axis=0, keepdims=True), axis=1, keepdims=True)


def inverse_factor(gram, trace):
    size = gram.shape[0]
    high = 8
    count = size // high
    square = (size, size)
    diag = lax.broadcasted_iota(jnp.int32, square, 1) == lax.broadcasted_iota(jnp.int32, square, 0)
    gram = jnp.where(diag, gram + (0.0001 * trace / size + 1e-06), gram)
    rows = [gram[high * g : high * g + high, :] for g in range(count)]
    shape = (high, size)
    lane = lax.broadcasted_iota(jnp.int32, shape, 1)
    sub = lax.broadcasted_iota(jnp.int32, shape, 0)

    def along_lanes(block, first):
        return [jnp.broadcast_to(block[:, first + k : first + k + 1], shape) for k in range(high)]

    def along_rows(block, at):
        return jnp.broadcast_to(block[at : at + 1, :], shape)

    found = []
    here = along_lanes(rows[0], 0)
    for b in range(count):
        first, after = b * high, (b + 1) * high
        more = b + 1 < count
        inside = (lane >= first) & (lane < after)
        full = jnp.where(inside, jnp.where(lane - first == sub, 1.0, 0.0), rows[b])
        done = jnp.zeros(shape, jnp.float32)
        steps = []
        if more:
            under = along_lanes(rows[b + 1], first)
            right = along_lanes(rows[b], after)
            corner = along_lanes(rows[b + 1], after)
            below_row = jnp.where(inside, 0.0, rows[b + 1])
        for i in range(high):
            root = lax.rsqrt(along_rows(here[i], i))
            inverse = root * root
            below = jnp.where(sub > i, here[i], 0.0)
            scaled = below * inverse
            entries = {k: along_rows(here[k], i) for k in range(i + 1, high)}
            for k, x in entries.items():
                here[k] = here[k] - ((below * x) * inverse if k < i + 3 else scaled * x)
            x = along_rows(full, i)
            done = jnp.where(sub == i, x * root, done)
            full = full - scaled * x
            if not more:
                continue
            steps.append(({k: entry * inverse for k, entry in entries.items()}, x * inverse))
            low = under[i] * inverse
            for k, entry in entries.items():
                under[k] = under[k] - low * entry
            for k in range(high):
                entry = along_rows(right[k], i)
                right[k] = right[k] - scaled * entry
                corner[k] = corner[k] - low * entry
            below_row = below_row - low * x
        found.append(jnp.where(lane < after, done, 0.0))
        if not more:
            break
        rows[b + 1] = below_row
        for g in range(b + 2, count):
            columns = along_lanes(rows[g], first)
            row = jnp.where(inside, 0.0, rows[g])
            for i, (entries, x) in enumerate(steps):
                for k, entry in entries.items():
                    columns[k] = columns[k] - columns[i] * entry
                row = row - columns[i] * x
            rows[g] = row
        here = corner
    return jnp.concatenate(found, axis=0)


def in_parts(block):
    high = block.astype(jnp.bfloat16)
    rest = block - high.astype(jnp.float32)
    middle = rest.astype(jnp.bfloat16)
    return high, middle, (rest - middle.astype(jnp.float32)).astype(jnp.bfloat16)


def short_dot(left, right):
    return jnp.dot(left, right, preferred_element_type=jnp.float32)


def quotient(value, divisor, below):
    shift = 20
    factor = -(-(2**shift) // divisor)
    assert all(v * factor >> shift == v // divisor for v in range(below))
    assert below * factor < 2**31
    return value * factor >> shift


def spmm_body(
    slots_ref,
    tiles_ref,
    sketch_ref,
    keep_ref,
    send_ref,
    dense,
    held,
    slots,
    tile_sem,
    sketch_sems,
    slots_sem,
    *,
    leaves,
):
    tile_count, tile_size, _ = tiles_ref.shape
    depth = sketch_ref.shape[0]
    rows = dense.shape[0]
    half = rows // 2
    col_tiles = depth // tile_size
    chunks = sketch_sems.shape[0]
    chunk = depth // chunks
    leaf_tiles = rows // leaves // tile_size
    me = lax.axis_index("col")
    slots_load = pltpu.make_async_copy(slots_ref, slots, slots_sem)
    loads = [
        pltpu.make_async_copy(
            sketch_ref.at[pl.ds(k * chunk, chunk)], held.at[pl.ds(k * chunk, chunk)], sketch_sems.at[k]
        )
        for k in range(chunks)
    ]
    for load in [slots_load] + loads:
        load.start()

    @pl.loop(0, rows // 64)
    def _(i):
        dense[pl.ds(pl.multiple_of(i * 64, 64), 64), :] = jnp.zeros((64, depth), dense.dtype)

    slots_load.wait()
    together = math.gcd(tile_count, 8)

    @pl.loop(0, tile_count // together)
    def _(group):
        for member in range(together):
            t = group * together + member
            slot = slots[t]
            row_tile = quotient(slot, col_tiles, rows // tile_size * col_tiles)
            column = slot - row_tile * col_tiles
            leaf = quotient(row_tile, leaf_tiles, rows // tile_size)
            away = leaf ^ me
            block = (away & 1) * (leaves // 2) + (away >> 1)
            row = pl.multiple_of((block * leaf_tiles + row_tile - leaf * leaf_tiles) * tile_size, tile_size)
            col = pl.multiple_of(column * tile_size, tile_size)
            pltpu.make_async_copy(
                tiles_ref.at[t], dense.at[pl.ds(row, tile_size), pl.ds(col, tile_size)], tile_sem
            ).start()

    pltpu.make_async_copy(tiles_ref, tiles_ref, tile_sem).wait()
    for k in range(chunks):
        loads[k].wait()
        for start, ref in ((half, send_ref), (0, keep_ref)):
            part = jnp.dot(
                dense[start : start + half, k * chunk : (k + 1) * chunk],
                held[k * chunk : (k + 1) * chunk, :],
                preferred_element_type=jnp.float32,
            )
            if k == 0:
                ref[...] = part
            else:
                ref[...] += part


def sample_rows(tiles, tile_slots, sketch, leaf):
    tile_size = tiles.shape[1]
    depth, width = sketch.shape
    leaves = lax.axis_size("col")
    rows = leaf * leaves
    half = rows // 2
    chunks = math.gcd(depth // tile_size, 4)
    return pl.pallas_call(
        functools.partial(spmm_body, leaves=leaves),
        out_shape=[jax.ShapeDtypeStruct((half, width), jnp.float32)] * 2,
        in_specs=[HBM] * 3,
        out_specs=[VMEM] * 2,
        scratch_shapes=[
            pltpu.VMEM((rows, depth), jnp.bfloat16),
            pltpu.VMEM((depth, width), jnp.bfloat16),
            pltpu.SMEM(tile_slots.shape, jnp.int32),
            pltpu.SemaphoreType.DMA,
            pltpu.SemaphoreType.DMA((chunks,)),
            pltpu.SemaphoreType.DMA,
        ],
        compiler_params=pltpu.CompilerParams(vmem_limit_bytes=48 * 2**20),
        cost_estimate=pl.CostEstimate(
            flops=2 * rows * depth * width,
            bytes_accessed=2 * (tiles.size + sketch.size) + 4 * rows * width,
            transcendentals=0,
        ),
        name="spmm",
    )(tile_slots, tiles, sketch)


def reduce_body(*refs):
    sub_ref, ref = refs[:2]
    outs = refs[len(refs) // 2 + 1 :]
    rank = sub_ref.shape[1]
    high, middle, low = in_parts(sub_ref[...])
    two = jnp.concatenate([high, middle], axis=1)
    first, second, third = in_parts(ref[...])
    wide = short_dot(second, two) + short_dot(first, two)
    rest = short_dot(third, high) + short_dot(first, low)
    outs[0][...] = wide[:, :rank] + (wide[:, rank:] + rest)
    if len(outs) > 1:
        exact = refs[2][...]
        wide = short_dot(exact, two)
        outs[1][...] = wide[:, :rank] + (wide[:, rank:] + short_dot(exact, low))


def reduce_step(subsketch, *blocks):
    rank = subsketch.shape[1]
    return pl.pallas_call(
        reduce_body,
        out_shape=[jax.ShapeDtypeStruct((block.shape[0], rank), jnp.float32) for block in blocks],
        in_specs=[VMEM] * (1 + len(blocks)),
        out_specs=[VMEM] * len(blocks),
        compiler_params=small_params(),
        cost_estimate=small_cost(1),
        name="reduced_" + str(len(blocks)),
    )(subsketch, *blocks)


def leaf_body(keep_ref, first_ref, second_ref, sketch_red_ref, _, basis_t_ref, pair_ref):
    rank = keep_ref.shape[-1]
    reduced = keep_ref[...] + first_ref[...] + second_ref[...]
    reduced_t = reduced.T
    both = dot(reduced_t, jnp.concatenate([reduced, sketch_red_ref[...]], axis=1))
    inverse = inverse_factor(both[:, :rank], square_sum(reduced))
    moved = dot(inverse, jnp.concatenate([both, reduced_t], axis=1))
    pair_ref[:rank, :] = moved[:, :rank]
    pair_ref[rank:, :] = moved[:, rank : 2 * rank]
    basis_t_ref[...] = moved[:, 2 * rank :]


def small_params():
    return pltpu.CompilerParams(vmem_limit_bytes=32 * 2**20)


def small_cost(micros):
    return pl.CostEstimate(flops=micros * 10**7, bytes_accessed=micros * 3 * 10**4, transcendentals=0)


def leaf_step(keep, first, second, sketch_red, after):
    leaf, rank = sketch_red.shape
    f32 = jnp.float32
    part = pl.BlockSpec((leaf, rank), lambda step: (0, 0))
    return pl.pallas_call(
        leaf_body,
        grid=(1,),
        out_shape=[
            jax.ShapeDtypeStruct((rank, leaf), f32),
            jax.ShapeDtypeStruct((2 * rank, rank), f32),
        ],
        in_specs=[part, part, VMEM, VMEM, ANY],
        out_specs=[VMEM] * 2,
        compiler_params=small_params(),
        cost_estimate=small_cost(8),
        name="leaf_orth",
    )(keep, first, second, sketch_red, after)


def basis_body(basis_t_ref, _, basis_ref, mark_ref):
    basis_ref[...] = basis_t_ref[...].T
    mark_ref[...] = jnp.zeros_like(mark_ref)


def basis_step(basis_t, after):
    return pl.pallas_call(
        basis_body,
        out_shape=[
            jax.ShapeDtypeStruct(basis_t.shape[::-1], jnp.float32),
            jax.ShapeDtypeStruct((8, 128), jnp.float32),
        ],
        in_specs=[VMEM, ANY],
        out_specs=[VMEM] * 2,
        compiler_params=small_params(),
        cost_estimate=small_cost(1),
        name="leaf_basis",
    )(basis_t, after)


def position():
    return lax.axis_index("row") * lax.axis_size("col") + lax.axis_index("col")


def turned(coupling_ref, tree_level):
    upper = position() // 2**tree_level % 2 == 1
    coupling = coupling_ref[0, 0].astype(jnp.float32)
    coupling_t = coupling.T
    return jnp.where(upper, coupling_t, coupling), jnp.where(upper, coupling, coupling_t)


def merge_body(tree_level, *refs):
    last = tree_level == LEVELS - 1
    coupling_ref, own_ref, other_ref = refs[:3]
    if tree_level == LEVELS - 2:
        block_ref, maps_ref, pair_ref, half_ref = refs[-4:]
    else:
        block_ref, maps_ref, pair_ref = refs[-3:]
    odd = position() % 2 == 1
    rank = own_ref.shape[-1]
    ahead, back = turned(coupling_ref, tree_level)
    own_sample, own_sketch = own_ref[:rank], own_ref[rank:]
    if last:
        other_sample = jnp.where(odd, refs[3][...], other_ref[...])
        other_sketch = jnp.where(odd, other_ref[...], refs[3][...])
    else:
        other_sample, other_sketch = other_ref[:rank], other_ref[rank:]
    own = own_sample - dot(ahead, other_sketch)
    other = other_sample - dot(back, own_sketch)
    own_t, other_t = own.T, other.T
    stacked_t = jnp.concatenate([own_t, other_t], axis=1)
    stacked = jnp.concatenate([own, other], axis=0)
    right = jnp.concatenate(
        [stacked, jnp.concatenate([own_sketch, other_sketch], axis=0)], axis=1
    )
    both = dot(stacked_t, stacked if last else right)
    if not last:
        sides = [own_t, dot(other_t, back)]
        if maps_ref.shape[0] == 4:
            sides += [other_t, dot(own_t, ahead)]
    inverse = inverse_factor(both[:, :rank], square_sum(own) + square_sum(other))
    block_ref[...] = dot_nt(own, inverse)
    if last:
        pair_ref[...] = dot(inverse, stacked_t)
        return
    moved = dot(inverse, jnp.concatenate([both] + sides, axis=1))
    pair_ref[:rank, :] = moved[:, :rank]
    pair_ref[rank:, :] = moved[:, rank : 2 * rank]
    if tree_level == LEVELS - 2:
        half_ref[...] = jnp.where(odd, moved[:, rank : 2 * rank], moved[:, :rank])
    for side in range(len(sides)):
        maps_ref[side] = moved[:, (2 + side) * rank : (3 + side) * rank]


def coupling_spec(couplings, tree_level):
    return pl.BlockSpec((1, 1) + couplings.shape[2:], lambda step: (0, tree_level, 0, 0))


def merge_step(tree_level, own, others, couplings, sides, after):
    rank = own.shape[1]
    f32 = jnp.float32
    last = tree_level == LEVELS - 1
    split = tree_level == LEVELS - 2
    return pl.pallas_call(
        functools.partial(merge_body, tree_level),
        grid=(1,),
        out_shape=[
            jax.ShapeDtypeStruct((rank, rank), f32),
            jax.ShapeDtypeStruct((8, rank) if last else (2 * sides, rank, rank), f32),
            jax.ShapeDtypeStruct((rank, 2 * rank) if last else (2 * rank, rank), f32),
        ]
        + [jax.ShapeDtypeStruct((rank, rank), f32)] * split,
        in_specs=[coupling_spec(couplings, tree_level)] + [VMEM] * (1 + len(others)) + [ANY] * len(after),
        out_specs=[VMEM, ANY if last else VMEM, VMEM] + [VMEM] * split,
        compiler_params=small_params(),
        cost_estimate=small_cost(8),
        name=f"merge_orth_{tree_level}",
    )(couplings, own, *others, *after)


def lower_body(*refs):
    keep_ref, first_ref, second_ref, leaf_sketch_ref, basis_t_ref = refs[:5]
    ways = (refs[-1].shape[1]) // refs[-2].shape[1]
    maps_refs = refs[5 : -1 - ways]
    out_refs = refs[-1 - ways : -1]
    wide = refs[-1]
    rank = basis_t_ref.shape[0]
    sample = keep_ref[...] + first_ref[...] + second_ref[...]
    sketch = leaf_sketch_ref[...].astype(jnp.float32)
    on_sample = basis_t_ref[...]
    on_sketch = jnp.zeros_like(on_sample)
    for maps_ref in maps_refs:
        lifted, crossed = maps_ref[0], maps_ref[1]
        on_sketch = dot(lifted, on_sketch) - dot(crossed, on_sample)
        on_sample = dot(lifted, on_sample)
    wide[:rank, :] = dot(on_sample, sample) + dot(on_sketch, sketch)
    wide[rank:, :] = dot(on_sample, sketch)
    me = lax.axis_index("col")
    part = wide.shape[1] // ways
    for away in range(ways):
        out_refs[away][...] = wide[:, pl.ds(pl.multiple_of((me ^ away) * part, part), part)]


def lower_step(keep, first, second, row_sketch, basis_t, maps):
    ways = lax.axis_size("col")
    leaf, width = row_sketch.shape
    rank = basis_t.shape[0]
    part = pl.BlockSpec((leaf, width), lambda step: (0, 0))
    return pl.pallas_call(
        lower_body,
        grid=(1,),
        out_shape=[jax.ShapeDtypeStruct((2 * rank, width // ways), jnp.float32)] * ways,
        in_specs=[part, part] + [VMEM] * (3 + len(maps)),
        out_specs=[VMEM] * ways,
        scratch_shapes=[pltpu.VMEM((2 * rank, width), jnp.float32)],
        compiler_params=small_params(),
        cost_estimate=small_cost(2),
        name="lower_maps",
    )(keep, first, second, row_sketch, basis_t, *maps)


def upper_body(count, *refs):
    maps_ref, out_ref = refs[-2:]

    def total(parts):
        added = parts[0][...]
        for ref in parts[1:]:
            added = added + ref[...]
        return added

    rank = maps_ref.shape[1]
    own, other = total(refs[:count]), total(refs[count:-2])
    nodes = jnp.concatenate([own, other], axis=0)
    sketches = jnp.concatenate([own[rank:], other[rank:]], axis=0)
    lifts = jnp.concatenate([maps_ref[0], maps_ref[2]], axis=1)
    signed = jnp.concatenate([maps_ref[0], -maps_ref[1], maps_ref[2], -maps_ref[3]], axis=1)
    out_ref[:rank, :] = dot(signed, nodes)
    out_ref[rank:, :] = dot(lifts, sketches)


def upper_step(tree_level, own, other, maps):
    return pl.pallas_call(
        functools.partial(upper_body, len(own)),
        out_shape=jax.ShapeDtypeStruct(own[0].shape, jnp.float32),
        in_specs=[VMEM] * (len(own) + len(other) + 1),
        out_specs=VMEM,
        compiler_params=small_params(),
        cost_estimate=small_cost(1),
        name=f"upper_maps_{tree_level}",
    )(*own, *other, maps)


def top_body(own_ref, other_ref, coupling_ref, basis_t_ref, out_ref):
    rank = own_ref.shape[0] // 2
    ahead, back = turned(coupling_ref, LEVELS - 1)
    own = own_ref[:rank] - dot(ahead, other_ref[rank:])
    other = other_ref[:rank] - dot(back, own_ref[rank:])
    out_ref[...] = dot(basis_t_ref[...], jnp.concatenate([own, other], axis=0))


def top_step(own, other, couplings, basis_t):
    return pl.pallas_call(
        top_body,
        grid=(1,),
        out_shape=jax.ShapeDtypeStruct((own.shape[0] // 2, own.shape[1]), jnp.float32),
        in_specs=[VMEM, VMEM, coupling_spec(couplings, LEVELS - 1), VMEM],
        out_specs=VMEM,
        compiler_params=small_params(),
        cost_estimate=small_cost(1),
        name="top_sample",
    )(own, other, couplings, basis_t)


def columns_body(*refs):
    sems = refs[-1]
    out_ref = refs[-2]
    pieces = refs[:-2]
    ways = len(pieces)
    me = lax.axis_index("col")
    part = out_ref.shape[2] // ways
    copies = [
        pltpu.make_async_copy(
            pieces[away],
            out_ref.at[0, :, pl.ds(pl.multiple_of((me ^ away) * part, part), part)],
            sems.at[away],
        )
        for away in range(ways)
    ]
    for copy in copies:
        copy.start()
    for copy in copies:
        copy.wait()


def columns_step(pieces):
    rank, part = pieces[0].shape
    ways = len(pieces)
    return pl.pallas_call(
        columns_body,
        out_shape=jax.ShapeDtypeStruct((1, rank, part * ways), jnp.float32),
        in_specs=[VMEM] * ways,
        out_specs=ANY,
        scratch_shapes=[pltpu.SemaphoreType.DMA((ways,))],
        compiler_params=small_params(),
        name="top_columns",
    )(*pieces)


def per_device(tiles, tile_slots, sketch, row_sketch, subsketch, couplings):
    ways = lax.axis_size("col")
    col_bits = ways.bit_length() - 1
    leaf = row_sketch.shape[0]
    keep, send = sample_rows(tiles, tile_slots, sketch, leaf)
    (send_red,) = reduce_step(subsketch, send)
    first_red = from_partner(send_red, "col", 1)
    keep_red, sketch_red = reduce_step(subsketch, keep, row_sketch)
    passed_red, send = lax.optimization_barrier((keep_red[leaf:] + first_red[leaf:], send))
    second_red = from_partner(passed_red, "col", 2)
    first = from_partner(send, "col", 1)
    passed, second_red = lax.optimization_barrier((keep[leaf:] + first[leaf:], second_red))
    second = from_partner(passed, "col", 2)
    basis_t, pair = leaf_step(keep_red, first_red, second_red, sketch_red, passed)
    blocks, low_maps, after = [], [], []
    for tree_level in range(LEVELS):
        if tree_level < LEVELS - 1:
            others = [from_partner(pair, ROW_COL, 2**tree_level)]
        else:
            others = [waiting, from_partner(waiting, ROW_COL, 1)]
        if tree_level == LEVELS - 2:
            leaf_basis, mark = basis_step(basis_t, after[0])
            after = after + [mark]
        sides = 1 if tree_level < col_bits - 1 else 2
        block, maps, pair, *half = merge_step(tree_level, pair, others, couplings, sides, after)
        blocks.append(block)
        if tree_level == LEVELS - 1:
            break
        if tree_level == LEVELS - 2:
            waiting = from_partner(half[0], ROW_COL, 2 ** (LEVELS - 1))
        if tree_level < col_bits - 1:
            low_maps.append(maps)
        else:
            total = upper_step(tree_level, own, other, maps)
            own = [total]
            if tree_level == LEVELS - 2:
                total, waiting = lax.optimization_barrier((total, waiting))
            other = [from_partner(total, ROW_COL, 2 ** (tree_level + 1))]
            after = [total]
        if tree_level == col_bits - 2:
            cut = lower_step(keep, first, second, row_sketch, basis_t, low_maps)
            cut = [cut[0]] + [from_partner(cut[away], "col", away) for away in range(1, ways)]
            own, other = cut[: ways // 2], cut[ways // 2 :]
            after = [cut[0]]
    top = top_step(own[0], other[0], couplings, pair)
    pieces = [top] + [from_partner(top, "col", away) for away in range(1, ways)]
    transfer = jnp.stack(blocks, axis=0)[None]
    return (leaf_basis, transfer, columns_step(pieces))


def solution(mesh):
    return jax.shard_map(
        per_device,
        mesh=mesh,
        in_specs=(
            P(("row", "col"), None, None),
            P(("row", "col")),
            P("col", None),
            P(("row", "col"), None),
            P(),
            P(("row", "col"), None, None, None),
        ),
        out_specs=(
            P(("row", "col"), None),
            P(("row", "col"), None, None, None),
            P(("row", "col"), None, None),
        ),
        check_vma=False,
    )
```

```python
import functools
import math

import jax
import jax.numpy as jnp
from jax import lax
from jax.experimental import pallas as pl
from jax.experimental.pallas import tpu as pltpu
from jax.sharding import PartitionSpec as P

LEVELS = 5
ROW_COL = ("row", "col")
VMEM = pl.BlockSpec(memory_space=pltpu.VMEM)
ANY = pl.BlockSpec(memory_space=pl.ANY)
HBM = pl.BlockSpec(memory_space=pltpu.HBM)


def from_partner(block, axis, distance):
    count = lax.axis_size(axis)
    route = []
    for low in range(count):
        high = low ^ distance
        if high < count:
            route.append((low, high))
    return lax.ppermute(block, axis, route)


def dot(left, right):
    return jnp.dot(left, right, precision=lax.Precision.HIGHEST, preferred_element_type=jnp.float32)


def dot_nt(left, right):
    return lax.dot_general(
        left,
        right,
        (((1,), (1,)), ((), ())),
        precision=lax.Precision.HIGHEST,
        preferred_element_type=jnp.float32,
    )


def square_sum(block):
    squares = block * block
    return jnp.sum(jnp.sum(squares, axis=0, keepdims=True), axis=1, keepdims=True)


def inverse_factor(gram, trace):
    size = gram.shape[0]
    high = 8
    count = size // high
    square = (size, size)
    diag = lax.broadcasted_iota(jnp.int32, square, 1) == lax.broadcasted_iota(jnp.int32, square, 0)
    gram = jnp.where(diag, gram + (0.0001 * trace / size + 1e-06), gram)
    rows = [gram[high * g : high * g + high, :] for g in range(count)]
    shape = (high, size)
    lane = lax.broadcasted_iota(jnp.int32, shape, 1)
    sub = lax.broadcasted_iota(jnp.int32, shape, 0)

    def along_lanes(block, first):
        return [jnp.broadcast_to(block[:, first + k : first + k + 1], shape) for k in range(high)]

    def along_rows(block, at):
        return jnp.broadcast_to(block[at : at + 1, :], shape)

    found = []
    here = along_lanes(rows[0], 0)
    for b in range(count):
        first, after = b * high, (b + 1) * high
        more = b + 1 < count
        inside = (lane >= first) & (lane < after)
        full = jnp.where(inside, jnp.where(lane - first == sub, 1.0, 0.0), rows[b])
        done = jnp.zeros(shape, jnp.float32)
        steps = []
        if more:
            under = along_lanes(rows[b + 1], first)
            right = along_lanes(rows[b], after)
            corner = along_lanes(rows[b + 1], after)
            below_row = jnp.where(inside, 0.0, rows[b + 1])
        for i in range(high):
            root = lax.rsqrt(along_rows(here[i], i))
            inverse = root * root
            below = jnp.where(sub > i, here[i], 0.0)
            scaled = below * inverse
            entries = {k: along_rows(here[k], i) for k in range(i + 1, high)}
            for k, x in entries.items():
                here[k] = here[k] - ((below * x) * inverse if k < i + 3 else scaled * x)
            x = along_rows(full, i)
            done = jnp.where(sub == i, x * root, done)
            full = full - scaled * x
            if not more:
                continue
            steps.append(({k: entry * inverse for k, entry in entries.items()}, x * inverse))
            low = under[i] * inverse
            for k, entry in entries.items():
                under[k] = under[k] - low * entry
            for k in range(high):
                entry = along_rows(right[k], i)
                right[k] = right[k] - scaled * entry
                corner[k] = corner[k] - low * entry
            below_row = below_row - low * x
        found.append(jnp.where(lane < after, done, 0.0))
        if not more:
            break
        rows[b + 1] = below_row
        for g in range(b + 2, count):
            columns = along_lanes(rows[g], first)
            row = jnp.where(inside, 0.0, rows[g])
            for i, (entries, x) in enumerate(steps):
                for k, entry in entries.items():
                    columns[k] = columns[k] - columns[i] * entry
                row = row - columns[i] * x
            rows[g] = row
        here = corner
    return jnp.concatenate(found, axis=0)


def in_parts(block):
    high = block.astype(jnp.bfloat16)
    rest = block - high.astype(jnp.float32)
    middle = rest.astype(jnp.bfloat16)
    return high, middle, (rest - middle.astype(jnp.float32)).astype(jnp.bfloat16)


def short_dot(left, right):
    return jnp.dot(left, right, preferred_element_type=jnp.float32)


def quotient(value, divisor, below):
    shift = 20
    factor = -(-(2**shift) // divisor)
    assert all(v * factor >> shift == v // divisor for v in range(below))
    assert below * factor < 2**31
    return value * factor >> shift


def spmm_body(
    slots_ref,
    tiles_ref,
    sketch_ref,
    keep_ref,
    send_ref,
    dense,
    held,
    slots,
    tile_sem,
    sketch_sems,
    slots_sem,
    *,
    leaves,
):
    tile_count, tile_size, _ = tiles_ref.shape
    depth = sketch_ref.shape[0]
    rows = dense.shape[0]
    half = rows // 2
    col_tiles = depth // tile_size
    chunks = sketch_sems.shape[0]
    chunk = depth // chunks
    leaf_tiles = rows // leaves // tile_size
    me = lax.axis_index("col")
    slots_load = pltpu.make_async_copy(slots_ref, slots, slots_sem)
    loads = [
        pltpu.make_async_copy(
            sketch_ref.at[pl.ds(k * chunk, chunk)], held.at[pl.ds(k * chunk, chunk)], sketch_sems.at[k]
        )
        for k in range(chunks)
    ]
    for load in [slots_load] + loads:
        load.start()

    @pl.loop(0, rows // 64)
    def _(i):
        dense[pl.ds(pl.multiple_of(i * 64, 64), 64), :] = jnp.zeros((64, depth), dense.dtype)

    slots_load.wait()
    together = math.gcd(tile_count, 8)

    @pl.loop(0, tile_count // together)
    def _(group):
        for member in range(together):
            t = group * together + member
            slot = slots[t]
            row_tile = quotient(slot, col_tiles, rows // tile_size * col_tiles)
            column = slot - row_tile * col_tiles
            leaf = quotient(row_tile, leaf_tiles, rows // tile_size)
            away = leaf ^ me
            block = (away & 1) * (leaves // 2) + (away >> 1)
            row = pl.multiple_of((block * leaf_tiles + row_tile - leaf * leaf_tiles) * tile_size, tile_size)
            col = pl.multiple_of(column * tile_size, tile_size)
            pltpu.make_async_copy(
                tiles_ref.at[t], dense.at[pl.ds(row, tile_size), pl.ds(col, tile_size)], tile_sem
            ).start()

    pltpu.make_async_copy(tiles_ref, tiles_ref, tile_sem).wait()
    for k in range(chunks):
        loads[k].wait()
        for start, ref in ((half, send_ref), (0, keep_ref)):
            part = jnp.dot(
                dense[start : start + half, k * chunk : (k + 1) * chunk],
                held[k * chunk : (k + 1) * chunk, :],
                preferred_element_type=jnp.float32,
            )
            if k == 0:
                ref[...] = part
            else:
                ref[...] += part


def sample_rows(tiles, tile_slots, sketch, leaf):
    tile_size = tiles.shape[1]
    depth, width = sketch.shape
    leaves = lax.axis_size("col")
    rows = leaf * leaves
    half = rows // 2
    chunks = math.gcd(depth // tile_size, 4)
    return pl.pallas_call(
        functools.partial(spmm_body, leaves=leaves),
        out_shape=[jax.ShapeDtypeStruct((half, width), jnp.float32)] * 2,
        in_specs=[HBM] * 3,
        out_specs=[VMEM] * 2,
        scratch_shapes=[
            pltpu.VMEM((rows, depth), jnp.bfloat16),
            pltpu.VMEM((depth, width), jnp.bfloat16),
            pltpu.SMEM(tile_slots.shape, jnp.int32),
            pltpu.SemaphoreType.DMA,
            pltpu.SemaphoreType.DMA((chunks,)),
            pltpu.SemaphoreType.DMA,
        ],
        compiler_params=pltpu.CompilerParams(vmem_limit_bytes=48 * 2**20),
        cost_estimate=pl.CostEstimate(
            flops=2 * rows * depth * width,
            bytes_accessed=2 * (tiles.size + sketch.size) + 4 * rows * width,
            transcendentals=0,
        ),
        name="spmm",
    )(tile_slots, tiles, sketch)


def reduce_body(*refs):
    sub_ref, ref = refs[:2]
    outs = refs[len(refs) // 2 + 1 :]
    rank = sub_ref.shape[1]
    high, middle, low = in_parts(sub_ref[...])
    two = jnp.concatenate([high, middle], axis=1)
    first, second, third = in_parts(ref[...])
    wide = short_dot(second, two) + short_dot(first, two)
    rest = short_dot(third, high) + short_dot(first, low)
    outs[0][...] = wide[:, :rank] + (wide[:, rank:] + rest)
    if len(outs) > 1:
        exact = refs[2][...]
        wide = short_dot(exact, two)
        outs[1][...] = wide[:, :rank] + (wide[:, rank:] + short_dot(exact, low))


def reduce_step(subsketch, *blocks):
    rank = subsketch.shape[1]
    return pl.pallas_call(
        reduce_body,
        out_shape=[jax.ShapeDtypeStruct((block.shape[0], rank), jnp.float32) for block in blocks],
        in_specs=[VMEM] * (1 + len(blocks)),
        out_specs=[VMEM] * len(blocks),
        compiler_params=small_params(),
        cost_estimate=small_cost(1),
        name="reduced_" + str(len(blocks)),
    )(subsketch, *blocks)


def leaf_body(keep_ref, first_ref, second_ref, sketch_red_ref, _, basis_t_ref, pair_ref):
    rank = keep_ref.shape[-1]
    reduced = keep_ref[...] + first_ref[...] + second_ref[...]
    reduced_t = reduced.T
    both = dot(reduced_t, jnp.concatenate([reduced, sketch_red_ref[...]], axis=1))
    inverse = inverse_factor(both[:, :rank], square_sum(reduced))
    moved = dot(inverse, jnp.concatenate([both, reduced_t], axis=1))
    pair_ref[:rank, :] = moved[:, :rank]
    pair_ref[rank:, :] = moved[:, rank : 2 * rank]
    basis_t_ref[...] = moved[:, 2 * rank :]


def small_params():
    return pltpu.CompilerParams(vmem_limit_bytes=32 * 2**20)


def small_cost(micros):
    return pl.CostEstimate(flops=micros * 10**7, bytes_accessed=micros * 3 * 10**4, transcendentals=0)


def leaf_step(keep, first, second, sketch_red, after):
    leaf, rank = sketch_red.shape
    f32 = jnp.float32
    part = pl.BlockSpec((leaf, rank), lambda step: (0, 0))
    return pl.pallas_call(
        leaf_body,
        grid=(1,),
        out_shape=[
            jax.ShapeDtypeStruct((rank, leaf), f32),
            jax.ShapeDtypeStruct((2 * rank, rank), f32),
        ],
        in_specs=[part, part, VMEM, VMEM, ANY],
        out_specs=[VMEM] * 2,
        compiler_params=small_params(),
        cost_estimate=small_cost(8),
        name="leaf_orth",
    )(keep, first, second, sketch_red, after)


def basis_body(basis_t_ref, basis_ref, mark_ref):
    basis_ref[...] = basis_t_ref[...].T
    mark_ref[...] = jnp.zeros_like(mark_ref)


def basis_step(basis_t):
    return pl.pallas_call(
        basis_body,
        out_shape=[
            jax.ShapeDtypeStruct(basis_t.shape[::-1], jnp.float32),
            jax.ShapeDtypeStruct((8, 128), jnp.float32),
        ],
        in_specs=[VMEM],
        out_specs=[VMEM] * 2,
        compiler_params=small_params(),
        cost_estimate=small_cost(1),
        name="leaf_basis",
    )(basis_t)


def position():
    return lax.axis_index("row") * lax.axis_size("col") + lax.axis_index("col")


def turned(coupling_ref, tree_level):
    upper = position() // 2**tree_level % 2 == 1
    coupling = coupling_ref[0, 0].astype(jnp.float32)
    coupling_t = coupling.T
    return jnp.where(upper, coupling_t, coupling), jnp.where(upper, coupling, coupling_t)


def merge_body(tree_level, *refs):
    last = tree_level == LEVELS - 1
    coupling_ref, own_ref, other_ref = refs[:3]
    block_ref, maps_ref, pair_ref = refs[-3:]
    rank = own_ref.shape[-1]
    ahead, back = turned(coupling_ref, tree_level)
    own_sample, own_sketch = own_ref[:rank], own_ref[rank:]
    other_sample, other_sketch = other_ref[:rank], other_ref[rank:]
    own = own_sample - dot(ahead, other_sketch)
    other = other_sample - dot(back, own_sketch)
    own_t, other_t = own.T, other.T
    stacked_t = jnp.concatenate([own_t, other_t], axis=1)
    stacked = jnp.concatenate([own, other], axis=0)
    right = jnp.concatenate(
        [stacked, jnp.concatenate([own_sketch, other_sketch], axis=0)], axis=1
    )
    both = dot(stacked_t, stacked if last else right)
    if not last:
        sides = [own_t, dot(other_t, back)]
        if maps_ref.shape[0] == 4:
            sides += [other_t, dot(own_t, ahead)]
    inverse = inverse_factor(both[:, :rank], square_sum(own) + square_sum(other))
    block_ref[...] = dot_nt(own, inverse)
    if last:
        pair_ref[...] = dot(inverse, stacked_t)
        return
    moved = dot(inverse, jnp.concatenate([both] + sides, axis=1))
    pair_ref[:rank, :] = moved[:, :rank]
    pair_ref[rank:, :] = moved[:, rank : 2 * rank]
    for side in range(len(sides)):
        maps_ref[side] = moved[:, (2 + side) * rank : (3 + side) * rank]


def coupling_spec(couplings, tree_level):
    return pl.BlockSpec((1, 1) + couplings.shape[2:], lambda step: (0, tree_level, 0, 0))


def merge_step(tree_level, own, others, couplings, sides, after):
    rank = own.shape[1]
    f32 = jnp.float32
    last = tree_level == LEVELS - 1
    split = 0
    return pl.pallas_call(
        functools.partial(merge_body, tree_level),
        grid=(1,),
        out_shape=[
            jax.ShapeDtypeStruct((rank, rank), f32),
            jax.ShapeDtypeStruct((8, rank) if last else (2 * sides, rank, rank), f32),
            jax.ShapeDtypeStruct((rank, 2 * rank) if last else (2 * rank, rank), f32),
        ]
        + [jax.ShapeDtypeStruct((rank, rank), f32)] * split,
        in_specs=[coupling_spec(couplings, tree_level)] + [VMEM] * (1 + len(others)) + [ANY] * len(after),
        out_specs=[VMEM, ANY if last else VMEM, VMEM] + [VMEM] * split,
        compiler_params=small_params(),
        cost_estimate=small_cost(8),
        name=f"merge_orth_{tree_level}",
    )(couplings, own, *others, *after)


def lower_body(*refs):
    keep_ref, first_ref, second_ref, leaf_sketch_ref, basis_t_ref = refs[:5]
    ways = (refs[-1].shape[1]) // refs[-2].shape[1]
    maps_refs = refs[5 : -1 - ways]
    out_refs = refs[-1 - ways : -1]
    wide = refs[-1]
    rank = basis_t_ref.shape[0]
    sample = keep_ref[...] + first_ref[...] + second_ref[...]
    sketch = leaf_sketch_ref[...].astype(jnp.float32)
    on_sample = basis_t_ref[...]
    on_sketch = jnp.zeros_like(on_sample)
    for maps_ref in maps_refs:
        lifted, crossed = maps_ref[0], maps_ref[1]
        on_sketch = dot(lifted, on_sketch) - dot(crossed, on_sample)
        on_sample = dot(lifted, on_sample)
    wide[:rank, :] = dot(on_sample, sample) + dot(on_sketch, sketch)
    wide[rank:, :] = dot(on_sample, sketch)
    me = lax.axis_index("col")
    part = wide.shape[1] // ways
    for away in range(ways):
        out_refs[away][...] = wide[:, pl.ds(pl.multiple_of((me ^ away) * part, part), part)]


def lower_step(keep, first, second, row_sketch, basis_t, maps):
    ways = lax.axis_size("col")
    leaf, width = row_sketch.shape
    rank = basis_t.shape[0]
    part = pl.BlockSpec((leaf, width), lambda step: (0, 0))
    return pl.pallas_call(
        lower_body,
        grid=(1,),
        out_shape=[jax.ShapeDtypeStruct((2 * rank, width // ways), jnp.float32)] * ways,
        in_specs=[part, part] + [VMEM] * (3 + len(maps)),
        out_specs=[VMEM] * ways,
        scratch_shapes=[pltpu.VMEM((2 * rank, width), jnp.float32)],
        compiler_params=small_params(),
        cost_estimate=small_cost(2),
        name="lower_maps",
    )(keep, first, second, row_sketch, basis_t, *maps)


def upper_body(count, *refs):
    maps_ref, out_ref = refs[-2:]

    def total(parts):
        added = parts[0][...]
        for ref in parts[1:]:
            added = added + ref[...]
        return added

    rank = maps_ref.shape[1]
    own, other = total(refs[:count]), total(refs[count:-2])
    nodes = jnp.concatenate([own, other], axis=0)
    sketches = jnp.concatenate([own[rank:], other[rank:]], axis=0)
    lifts = jnp.concatenate([maps_ref[0], maps_ref[2]], axis=1)
    signed = jnp.concatenate([maps_ref[0], -maps_ref[1], maps_ref[2], -maps_ref[3]], axis=1)
    out_ref[:rank, :] = dot(signed, nodes)
    out_ref[rank:, :] = dot(lifts, sketches)


def upper_step(tree_level, own, other, maps):
    return pl.pallas_call(
        functools.partial(upper_body, len(own)),
        out_shape=jax.ShapeDtypeStruct(own[0].shape, jnp.float32),
        in_specs=[VMEM] * (len(own) + len(other) + 1),
        out_specs=VMEM,
        compiler_params=small_params(),
        cost_estimate=small_cost(1),
        name=f"upper_maps_{tree_level}",
    )(*own, *other, maps)


def top_body(own_ref, other_ref, coupling_ref, basis_t_ref, out_ref):
    rank = own_ref.shape[0] // 2
    ahead, back = turned(coupling_ref, LEVELS - 1)
    own = own_ref[:rank] - dot(ahead, other_ref[rank:])
    other = other_ref[:rank] - dot(back, own_ref[rank:])
    out_ref[...] = dot(basis_t_ref[...], jnp.concatenate([own, other], axis=0))


def top_step(own, other, couplings, basis_t):
    return pl.pallas_call(
        top_body,
        grid=(1,),
        out_shape=jax.ShapeDtypeStruct((own.shape[0] // 2, own.shape[1]), jnp.float32),
        in_specs=[VMEM, VMEM, coupling_spec(couplings, LEVELS - 1), VMEM],
        out_specs=VMEM,
        compiler_params=small_params(),
        cost_estimate=small_cost(1),
        name="top_sample",
    )(own, other, couplings, basis_t)


def columns_body(*refs):
    sems = refs[-1]
    out_ref = refs[-2]
    pieces = refs[:-2]
    ways = len(pieces)
    me = lax.axis_index("col")
    part = out_ref.shape[2] // ways
    copies = [
        pltpu.make_async_copy(
            pieces[away],
            out_ref.at[0, :, pl.ds(pl.multiple_of((me ^ away) * part, part), part)],
            sems.at[away],
        )
        for away in range(ways)
    ]
    for copy in copies:
        copy.start()
    for copy in copies:
        copy.wait()


def columns_step(pieces):
    rank, part = pieces[0].shape
    ways = len(pieces)
    return pl.pallas_call(
        columns_body,
        out_shape=jax.ShapeDtypeStruct((1, rank, part * ways), jnp.float32),
        in_specs=[VMEM] * ways,
        out_specs=ANY,
        scratch_shapes=[pltpu.SemaphoreType.DMA((ways,))],
        compiler_params=small_params(),
        name="top_columns",
    )(*pieces)


def per_device(tiles, tile_slots, sketch, row_sketch, subsketch, couplings):
    ways = lax.axis_size("col")
    col_bits = ways.bit_length() - 1
    leaf = row_sketch.shape[0]
    keep, send = sample_rows(tiles, tile_slots, sketch, leaf)
    (send_red,) = reduce_step(subsketch, send)
    first_red = from_partner(send_red, "col", 1)
    keep_red, sketch_red = reduce_step(subsketch, keep, row_sketch)
    passed_red, send = lax.optimization_barrier((keep_red[leaf:] + first_red[leaf:], send))
    second_red = from_partner(passed_red, "col", 2)
    first = from_partner(send, "col", 1)
    passed, second_red = lax.optimization_barrier((keep[leaf:] + first[leaf:], second_red))
    second = from_partner(passed, "col", 2)
    basis_t, pair = leaf_step(keep_red, first_red, second_red, sketch_red, passed)
    blocks, low_maps, after = [], [], []
    for tree_level in range(LEVELS):
        others = [from_partner(pair, ROW_COL, 2**tree_level)]
        if tree_level == 1:
            leaf_basis, mark = basis_step(basis_t)
            after = after + [mark]
        sides = 1 if tree_level < col_bits - 1 else 2
        block, maps, pair = merge_step(tree_level, pair, others, couplings, sides, after)
        blocks.append(block)
        if tree_level == LEVELS - 1:
            break
        if tree_level < col_bits - 1:
            low_maps.append(maps)
        else:
            total = upper_step(tree_level, own, other, maps)
            own = [total]
            other = [from_partner(total, ROW_COL, 2 ** (tree_level + 1))]
            after = [total]
        if tree_level == col_bits - 2:
            cut = lower_step(keep, first, second, row_sketch, basis_t, low_maps)
            cut = [cut[0]] + [from_partner(cut[away], "col", away) for away in range(1, ways)]
            own, other = cut[: ways // 2], cut[ways // 2 :]
            after = [cut[0]]
    top = top_step(own[0], other[0], couplings, pair)
    pieces = [top] + [from_partner(top, "col", away) for away in range(1, ways)]
    transfer = jnp.stack(blocks, axis=0)[None]
    return (leaf_basis, transfer, columns_step(pieces))


def solution(mesh):
    return jax.shard_map(
        per_device,
        mesh=mesh,
        in_specs=(
            P(("row", "col"), None, None),
            P(("row", "col")),
            P("col", None),
            P(("row", "col"), None),
            P(),
            P(("row", "col"), None, None, None),
        ),
        out_specs=(
            P(("row", "col"), None),
            P(("row", "col"), None, None, None),
            P(("row", "col"), None, None),
        ),
        check_vma=False,
    )
```

```python
import functools
import math

import jax
import jax.numpy as jnp
from jax import lax
from jax.experimental import pallas as pl
from jax.experimental.pallas import tpu as pltpu
from jax.sharding import PartitionSpec as P

LEVELS = 5
ROW_COL = ("row", "col")
VMEM = pl.BlockSpec(memory_space=pltpu.VMEM)
ANY = pl.BlockSpec(memory_space=pl.ANY)
HBM = pl.BlockSpec(memory_space=pltpu.HBM)


def from_partner(block, axis, distance):
    count = lax.axis_size(axis)
    route = []
    for low in range(count):
        high = low ^ distance
        if high < count:
            route.append((low, high))
    return lax.ppermute(block, axis, route)


def dot(left, right):
    return jnp.dot(left, right, precision=lax.Precision.HIGHEST, preferred_element_type=jnp.float32)


def dot_nt(left, right):
    return lax.dot_general(
        left,
        right,
        (((1,), (1,)), ((), ())),
        precision=lax.Precision.HIGHEST,
        preferred_element_type=jnp.float32,
    )


def square_sum(block):
    squares = block * block
    return jnp.sum(jnp.sum(squares, axis=0, keepdims=True), axis=1, keepdims=True)


def inverse_factor(gram, trace):
    size = gram.shape[0]
    high = 8
    count = size // high
    square = (size, size)
    diag = lax.broadcasted_iota(jnp.int32, square, 1) == lax.broadcasted_iota(jnp.int32, square, 0)
    gram = jnp.where(diag, gram + (0.0001 * trace / size + 1e-06), gram)
    rows = [gram[high * g : high * g + high, :] for g in range(count)]
    shape = (high, size)
    lane = lax.broadcasted_iota(jnp.int32, shape, 1)
    sub = lax.broadcasted_iota(jnp.int32, shape, 0)

    def along_lanes(block, first):
        return [jnp.broadcast_to(block[:, first + k : first + k + 1], shape) for k in range(high)]

    def along_rows(block, at):
        return jnp.broadcast_to(block[at : at + 1, :], shape)

    found = []
    here = along_lanes(rows[0], 0)
    for b in range(count):
        first, after = b * high, (b + 1) * high
        more = b + 1 < count
        inside = (lane >= first) & (lane < after)
        full = jnp.where(inside, jnp.where(lane - first == sub, 1.0, 0.0), rows[b])
        done = jnp.zeros(shape, jnp.float32)
        steps = []
        if more:
            under = along_lanes(rows[b + 1], first)
            right = along_lanes(rows[b], after)
            corner = along_lanes(rows[b + 1], after)
            below_row = jnp.where(inside, 0.0, rows[b + 1])
        for i in range(high):
            root = lax.rsqrt(along_rows(here[i], i))
            inverse = root * root
            below = jnp.where(sub > i, here[i], 0.0)
            scaled = below * inverse
            entries = {k: along_rows(here[k], i) for k in range(i + 1, high)}
            for k, x in entries.items():
                here[k] = here[k] - ((below * x) * inverse if k < i + 3 else scaled * x)
            x = along_rows(full, i)
            done = jnp.where(sub == i, x * root, done)
            full = full - scaled * x
            if not more:
                continue
            steps.append(({k: entry * inverse for k, entry in entries.items()}, x * inverse))
            low = under[i] * inverse
            for k, entry in entries.items():
                under[k] = under[k] - low * entry
            for k in range(high):
                entry = along_rows(right[k], i)
                right[k] = right[k] - scaled * entry
                corner[k] = corner[k] - low * entry
            below_row = below_row - low * x
        found.append(jnp.where(lane < after, done, 0.0))
        if not more:
            break
        rows[b + 1] = below_row
        for g in range(b + 2, count):
            columns = along_lanes(rows[g], first)
            row = jnp.where(inside, 0.0, rows[g])
            for i, (entries, x) in enumerate(steps):
                for k, entry in entries.items():
                    columns[k] = columns[k] - columns[i] * entry
                row = row - columns[i] * x
            rows[g] = row
        here = corner
    return jnp.concatenate(found, axis=0)


def in_parts(block):
    high = block.astype(jnp.bfloat16)
    rest = block - high.astype(jnp.float32)
    middle = rest.astype(jnp.bfloat16)
    return high, middle, (rest - middle.astype(jnp.float32)).astype(jnp.bfloat16)


def short_dot(left, right):
    return jnp.dot(left, right, preferred_element_type=jnp.float32)


def quotient(value, divisor, below):
    shift = 20
    factor = -(-(2**shift) // divisor)
    assert all(v * factor >> shift == v // divisor for v in range(below))
    assert below * factor < 2**31
    return value * factor >> shift


def spmm_body(
    slots_ref,
    tiles_ref,
    sketch_ref,
    keep_ref,
    send_ref,
    dense,
    held,
    slots,
    tile_sem,
    sketch_sems,
    slots_sem,
    *,
    leaves,
):
    tile_count, tile_size, _ = tiles_ref.shape
    depth = sketch_ref.shape[0]
    rows = dense.shape[0]
    half = rows // 2
    col_tiles = depth // tile_size
    chunks = sketch_sems.shape[0]
    chunk = depth // chunks
    leaf_tiles = rows // leaves // tile_size
    me = lax.axis_index("col")
    slots_load = pltpu.make_async_copy(slots_ref, slots, slots_sem)
    loads = [
        pltpu.make_async_copy(
            sketch_ref.at[pl.ds(k * chunk, chunk)], held.at[pl.ds(k * chunk, chunk)], sketch_sems.at[k]
        )
        for k in range(chunks)
    ]
    for load in [slots_load] + loads:
        load.start()

    @pl.loop(0, rows // 64)
    def _(i):
        dense[pl.ds(pl.multiple_of(i * 64, 64), 64), :] = jnp.zeros((64, depth), dense.dtype)

    slots_load.wait()
    together = math.gcd(tile_count, 8)

    @pl.loop(0, tile_count // together)
    def _(group):
        for member in range(together):
            t = group * together + member
            slot = slots[t]
            row_tile = quotient(slot, col_tiles, rows // tile_size * col_tiles)
            column = slot - row_tile * col_tiles
            leaf = quotient(row_tile, leaf_tiles, rows // tile_size)
            away = leaf ^ me
            block = (away & 1) * (leaves // 2) + (away >> 1)
            row = pl.multiple_of((block * leaf_tiles + row_tile - leaf * leaf_tiles) * tile_size, tile_size)
            col = pl.multiple_of(column * tile_size, tile_size)
            pltpu.make_async_copy(
                tiles_ref.at[t], dense.at[pl.ds(row, tile_size), pl.ds(col, tile_size)], tile_sem
            ).start()

    pltpu.make_async_copy(tiles_ref, tiles_ref, tile_sem).wait()
    for k in range(chunks):
        loads[k].wait()
        for start, ref in ((half, send_ref), (0, keep_ref)):
            part = jnp.dot(
                dense[start : start + half, k * chunk : (k + 1) * chunk],
                held[k * chunk : (k + 1) * chunk, :],
                preferred_element_type=jnp.float32,
            )
            if k == 0:
                ref[...] = part
            else:
                ref[...] += part


def sample_rows(tiles, tile_slots, sketch, leaf):
    tile_size = tiles.shape[1]
    depth, width = sketch.shape
    leaves = lax.axis_size("col")
    rows = leaf * leaves
    half = rows // 2
    chunks = 1
    return pl.pallas_call(
        functools.partial(spmm_body, leaves=leaves),
        out_shape=[jax.ShapeDtypeStruct((half, width), jnp.float32)] * 2,
        in_specs=[HBM] * 3,
        out_specs=[VMEM] * 2,
        scratch_shapes=[
            pltpu.VMEM((rows, depth), jnp.bfloat16),
            pltpu.VMEM((depth, width), jnp.bfloat16),
            pltpu.SMEM(tile_slots.shape, jnp.int32),
            pltpu.SemaphoreType.DMA,
            pltpu.SemaphoreType.DMA((chunks,)),
            pltpu.SemaphoreType.DMA,
        ],
        compiler_params=pltpu.CompilerParams(vmem_limit_bytes=48 * 2**20),
        cost_estimate=pl.CostEstimate(
            flops=2 * rows * depth * width,
            bytes_accessed=2 * (tiles.size + sketch.size) + 4 * rows * width,
            transcendentals=0,
        ),
        name="spmm",
    )(tile_slots, tiles, sketch)


def reduce_body(*refs):
    sub_ref, ref = refs[:2]
    outs = refs[len(refs) // 2 + 1 :]
    rank = sub_ref.shape[1]
    high, middle, low = in_parts(sub_ref[...])
    two = jnp.concatenate([high, middle], axis=1)
    first, second, third = in_parts(ref[...])
    wide = short_dot(second, two) + short_dot(first, two)
    rest = short_dot(third, high) + short_dot(first, low)
    outs[0][...] = wide[:, :rank] + (wide[:, rank:] + rest)
    if len(outs) > 1:
        exact = refs[2][...]
        wide = short_dot(exact, two)
        outs[1][...] = wide[:, :rank] + (wide[:, rank:] + short_dot(exact, low))


def reduce_step(subsketch, *blocks):
    rank = subsketch.shape[1]
    return pl.pallas_call(
        reduce_body,
        out_shape=[jax.ShapeDtypeStruct((block.shape[0], rank), jnp.float32) for block in blocks],
        in_specs=[VMEM] * (1 + len(blocks)),
        out_specs=[VMEM] * len(blocks),
        compiler_params=small_params(),
        cost_estimate=small_cost(1),
        name="reduced_" + str(len(blocks)),
    )(subsketch, *blocks)


def leaf_body(keep_ref, first_ref, second_ref, sketch_red_ref, _, basis_t_ref, pair_ref):
    rank = keep_ref.shape[-1]
    reduced = keep_ref[...] + first_ref[...] + second_ref[...]
    reduced_t = reduced.T
    both = dot(reduced_t, jnp.concatenate([reduced, sketch_red_ref[...]], axis=1))
    inverse = inverse_factor(both[:, :rank], square_sum(reduced))
    moved = dot(inverse, jnp.concatenate([both, reduced_t], axis=1))
    pair_ref[:rank, :] = moved[:, :rank]
    pair_ref[rank:, :] = moved[:, rank : 2 * rank]
    basis_t_ref[...] = moved[:, 2 * rank :]


def small_params():
    return pltpu.CompilerParams(vmem_limit_bytes=32 * 2**20)


def small_cost(micros):
    return pl.CostEstimate(flops=micros * 10**7, bytes_accessed=micros * 3 * 10**4, transcendentals=0)


def leaf_step(keep, first, second, sketch_red, after):
    leaf, rank = sketch_red.shape
    f32 = jnp.float32
    part = pl.BlockSpec((leaf, rank), lambda step: (0, 0))
    return pl.pallas_call(
        leaf_body,
        grid=(1,),
        out_shape=[
            jax.ShapeDtypeStruct((rank, leaf), f32),
            jax.ShapeDtypeStruct((2 * rank, rank), f32),
        ],
        in_specs=[part, part, VMEM, VMEM, ANY],
        out_specs=[VMEM] * 2,
        compiler_params=small_params(),
        cost_estimate=small_cost(8),
        name="leaf_orth",
    )(keep, first, second, sketch_red, after)


def basis_body(basis_t_ref, basis_ref, mark_ref):
    basis_ref[...] = basis_t_ref[...].T
    mark_ref[...] = jnp.zeros_like(mark_ref)


def basis_step(basis_t):
    return pl.pallas_call(
        basis_body,
        out_shape=[
            jax.ShapeDtypeStruct(basis_t.shape[::-1], jnp.float32),
            jax.ShapeDtypeStruct((8, 128), jnp.float32),
        ],
        in_specs=[VMEM],
        out_specs=[VMEM] * 2,
        compiler_params=small_params(),
        cost_estimate=small_cost(1),
        name="leaf_basis",
    )(basis_t)


def position():
    return lax.axis_index("row") * lax.axis_size("col") + lax.axis_index("col")


def turned(coupling_ref, tree_level):
    upper = position() // 2**tree_level % 2 == 1
    coupling = coupling_ref[0, 0].astype(jnp.float32)
    coupling_t = coupling.T
    return jnp.where(upper, coupling_t, coupling), jnp.where(upper, coupling, coupling_t)


def merge_body(tree_level, *refs):
    last = tree_level == LEVELS - 1
    coupling_ref, own_ref, other_ref = refs[:3]
    if tree_level == LEVELS - 2:
        block_ref, maps_ref, pair_ref, half_ref = refs[-4:]
    else:
        block_ref, maps_ref, pair_ref = refs[-3:]
    odd = position() % 2 == 1
    rank = own_ref.shape[-1]
    ahead, back = turned(coupling_ref, tree_level)
    own_sample, own_sketch = own_ref[:rank], own_ref[rank:]
    if last:
        other_sample = jnp.where(odd, refs[3][...], other_ref[...])
        other_sketch = jnp.where(odd, other_ref[...], refs[3][...])
    else:
        other_sample, other_sketch = other_ref[:rank], other_ref[rank:]
    own = own_sample - dot(ahead, other_sketch)
    other = other_sample - dot(back, own_sketch)
    own_t, other_t = own.T, other.T
    stacked_t = jnp.concatenate([own_t, other_t], axis=1)
    stacked = jnp.concatenate([own, other], axis=0)
    right = jnp.concatenate(
        [stacked, jnp.concatenate([own_sketch, other_sketch], axis=0)], axis=1
    )
    both = dot(stacked_t, stacked if last else right)
    if not last:
        sides = [own_t, dot(other_t, back)]
        if maps_ref.shape[0] == 4:
            sides += [other_t, dot(own_t, ahead)]
    inverse = inverse_factor(both[:, :rank], square_sum(own) + square_sum(other))
    block_ref[...] = dot_nt(own, inverse)
    if last:
        pair_ref[...] = dot(inverse, stacked_t)
        return
    moved = dot(inverse, jnp.concatenate([both] + sides, axis=1))
    pair_ref[:rank, :] = moved[:, :rank]
    pair_ref[rank:, :] = moved[:, rank : 2 * rank]
    if tree_level == LEVELS - 2:
        half_ref[...] = jnp.where(odd, moved[:, rank : 2 * rank], moved[:, :rank])
    for side in range(len(sides)):
        maps_ref[side] = moved[:, (2 + side) * rank : (3 + side) * rank]


def coupling_spec(couplings, tree_level):
    return pl.BlockSpec((1, 1) + couplings.shape[2:], lambda step: (0, tree_level, 0, 0))


def merge_step(tree_level, own, others, couplings, sides, after):
    rank = own.shape[1]
    f32 = jnp.float32
    last = tree_level == LEVELS - 1
    split = tree_level == LEVELS - 2
    return pl.pallas_call(
        functools.partial(merge_body, tree_level),
        grid=(1,),
        out_shape=[
            jax.ShapeDtypeStruct((rank, rank), f32),
            jax.ShapeDtypeStruct((8, rank) if last else (2 * sides, rank, rank), f32),
            jax.ShapeDtypeStruct((rank, 2 * rank) if last else (2 * rank, rank), f32),
        ]
        + [jax.ShapeDtypeStruct((rank, rank), f32)] * split,
        in_specs=[coupling_spec(couplings, tree_level)] + [VMEM] * (1 + len(others)) + [ANY] * len(after),
        out_specs=[VMEM, ANY if last else VMEM, VMEM] + [VMEM] * split,
        compiler_params=small_params(),
        cost_estimate=small_cost(8),
        name=f"merge_orth_{tree_level}",
    )(couplings, own, *others, *after)


def lower_body(*refs):
    keep_ref, first_ref, second_ref, leaf_sketch_ref, basis_t_ref = refs[:5]
    ways = (refs[-1].shape[1]) // refs[-2].shape[1]
    maps_refs = refs[5 : -1 - ways]
    out_refs = refs[-1 - ways : -1]
    wide = refs[-1]
    rank = basis_t_ref.shape[0]
    sample = keep_ref[...] + first_ref[...] + second_ref[...]
    sketch = leaf_sketch_ref[...].astype(jnp.float32)
    on_sample = basis_t_ref[...]
    on_sketch = jnp.zeros_like(on_sample)
    for maps_ref in maps_refs:
        lifted, crossed = maps_ref[0], maps_ref[1]
        on_sketch = dot(lifted, on_sketch) - dot(crossed, on_sample)
        on_sample = dot(lifted, on_sample)
    wide[:rank, :] = dot(on_sample, sample) + dot(on_sketch, sketch)
    wide[rank:, :] = dot(on_sample, sketch)
    me = lax.axis_index("col")
    part = wide.shape[1] // ways
    for away in range(ways):
        out_refs[away][...] = wide[:, pl.ds(pl.multiple_of((me ^ away) * part, part), part)]


def lower_step(keep, first, second, row_sketch, basis_t, maps):
    ways = lax.axis_size("col")
    leaf, width = row_sketch.shape
    rank = basis_t.shape[0]
    part = pl.BlockSpec((leaf, width), lambda step: (0, 0))
    return pl.pallas_call(
        lower_body,
        grid=(1,),
        out_shape=[jax.ShapeDtypeStruct((2 * rank, width // ways), jnp.float32)] * ways,
        in_specs=[part, part] + [VMEM] * (3 + len(maps)),
        out_specs=[VMEM] * ways,
        scratch_shapes=[pltpu.VMEM((2 * rank, width), jnp.float32)],
        compiler_params=small_params(),
        cost_estimate=small_cost(2),
        name="lower_maps",
    )(keep, first, second, row_sketch, basis_t, *maps)


def upper_body(count, *refs):
    maps_ref, out_ref = refs[-2:]

    def total(parts):
        added = parts[0][...]
        for ref in parts[1:]:
            added = added + ref[...]
        return added

    rank = maps_ref.shape[1]
    own, other = total(refs[:count]), total(refs[count:-2])
    nodes = jnp.concatenate([own, other], axis=0)
    sketches = jnp.concatenate([own[rank:], other[rank:]], axis=0)
    lifts = jnp.concatenate([maps_ref[0], maps_ref[2]], axis=1)
    signed = jnp.concatenate([maps_ref[0], -maps_ref[1], maps_ref[2], -maps_ref[3]], axis=1)
    out_ref[:rank, :] = dot(signed, nodes)
    out_ref[rank:, :] = dot(lifts, sketches)


def upper_step(tree_level, own, other, maps):
    return pl.pallas_call(
        functools.partial(upper_body, len(own)),
        out_shape=jax.ShapeDtypeStruct(own[0].shape, jnp.float32),
        in_specs=[VMEM] * (len(own) + len(other) + 1),
        out_specs=VMEM,
        compiler_params=small_params(),
        cost_estimate=small_cost(1),
        name=f"upper_maps_{tree_level}",
    )(*own, *other, maps)


def top_body(own_ref, other_ref, coupling_ref, basis_t_ref, out_ref):
    rank = own_ref.shape[0] // 2
    ahead, back = turned(coupling_ref, LEVELS - 1)
    own = own_ref[:rank] - dot(ahead, other_ref[rank:])
    other = other_ref[:rank] - dot(back, own_ref[rank:])
    out_ref[...] = dot(basis_t_ref[...], jnp.concatenate([own, other], axis=0))


def top_step(own, other, couplings, basis_t):
    return pl.pallas_call(
        top_body,
        grid=(1,),
        out_shape=jax.ShapeDtypeStruct((own.shape[0] // 2, own.shape[1]), jnp.float32),
        in_specs=[VMEM, VMEM, coupling_spec(couplings, LEVELS - 1), VMEM],
        out_specs=VMEM,
        compiler_params=small_params(),
        cost_estimate=small_cost(1),
        name="top_sample",
    )(own, other, couplings, basis_t)


def columns_body(*refs):
    sems = refs[-1]
    out_ref = refs[-2]
    pieces = refs[:-2]
    ways = len(pieces)
    me = lax.axis_index("col")
    part = out_ref.shape[2] // ways
    copies = [
        pltpu.make_async_copy(
            pieces[away],
            out_ref.at[0, :, pl.ds(pl.multiple_of((me ^ away) * part, part), part)],
            sems.at[away],
        )
        for away in range(ways)
    ]
    for copy in copies:
        copy.start()
    for copy in copies:
        copy.wait()


def columns_step(pieces):
    rank, part = pieces[0].shape
    ways = len(pieces)
    return pl.pallas_call(
        columns_body,
        out_shape=jax.ShapeDtypeStruct((1, rank, part * ways), jnp.float32),
        in_specs=[VMEM] * ways,
        out_specs=ANY,
        scratch_shapes=[pltpu.SemaphoreType.DMA((ways,))],
        compiler_params=small_params(),
        name="top_columns",
    )(*pieces)


def per_device(tiles, tile_slots, sketch, row_sketch, subsketch, couplings):
    ways = lax.axis_size("col")
    col_bits = ways.bit_length() - 1
    leaf = row_sketch.shape[0]
    keep, send = sample_rows(tiles, tile_slots, sketch, leaf)
    (send_red,) = reduce_step(subsketch, send)
    first_red = from_partner(send_red, "col", 1)
    keep_red, sketch_red = reduce_step(subsketch, keep, row_sketch)
    passed_red, send = lax.optimization_barrier((keep_red[leaf:] + first_red[leaf:], send))
    second_red = from_partner(passed_red, "col", 2)
    first = from_partner(send, "col", 1)
    passed, second_red = lax.optimization_barrier((keep[leaf:] + first[leaf:], second_red))
    second = from_partner(passed, "col", 2)
    basis_t, pair = leaf_step(keep_red, first_red, second_red, sketch_red, passed)
    blocks, low_maps, after = [], [], []
    for tree_level in range(LEVELS):
        if tree_level < LEVELS - 1:
            others = [from_partner(pair, ROW_COL, 2**tree_level)]
        else:
            others = [waiting, from_partner(waiting, ROW_COL, 1)]
        if tree_level == 1:
            leaf_basis, mark = basis_step(basis_t)
            after = after + [mark]
        sides = 1 if tree_level < col_bits - 1 else 2
        block, maps, pair, *half = merge_step(tree_level, pair, others, couplings, sides, after)
        blocks.append(block)
        if tree_level == LEVELS - 1:
            break
        if tree_level == LEVELS - 2:
            waiting = from_partner(half[0], ROW_COL, 2 ** (LEVELS - 1))
        if tree_level < col_bits - 1:
            low_maps.append(maps)
        else:
            total = upper_step(tree_level, own, other, maps)
            own = [total]
            other = [from_partner(total, ROW_COL, 2 ** (tree_level + 1))]
            after = [total]
        if tree_level == col_bits - 2:
            cut = lower_step(keep, first, second, row_sketch, basis_t, low_maps)
            cut = [cut[0]] + [from_partner(cut[away], "col", away) for away in range(1, ways)]
            own, other = cut[: ways // 2], cut[ways // 2 :]
            after = [cut[0]]
    top = top_step(own[0], other[0], couplings, pair)
    pieces = [top] + [from_partner(top, "col", away) for away in range(1, ways)]
    transfer = jnp.stack(blocks, axis=0)[None]
    return (leaf_basis, transfer, columns_step(pieces))


def solution(mesh):
    return jax.shard_map(
        per_device,
        mesh=mesh,
        in_specs=(
            P(("row", "col"), None, None),
            P(("row", "col")),
            P("col", None),
            P(("row", "col"), None),
            P(),
            P(("row", "col"), None, None, None),
        ),
        out_specs=(
            P(("row", "col"), None),
            P(("row", "col"), None, None, None),
            P(("row", "col"), None, None),
        ),
        check_vma=False,
    )
```
